128 devices in a mesh: row: 16 (over x_hi, z, core), col: 8 (over x_lo, y).
Axes of the slice: x: 4 (x_hi: 2, x_lo: 2; x = x_hi * 2 + x_lo), y: 4, z: 4, core: 2. Of those that a mesh axis runs over, the one named last changes fastest.
Arguments:
- features: bfloat16 [512, 512, 180], P('row', 'col'), may hold values from -6 to 6
- cotangent: bfloat16 [512, 512, 180], P('row', 'col'), may hold values from -6 to 6
- w_qkv: bfloat16 [180, 540], replicated, may hold values from -8 to 8
- w_proj: bfloat16 [180, 180], replicated, may hold values from -0.4375 to 0.4375
- w_fc1: bfloat16 [180, 360], replicated, may hold values from -0.4375 to 0.4375
- w_fc2: bfloat16 [360, 180], replicated, may hold values from -0.3125 to 0.3125
- w_conv: bfloat16 [9, 180, 180], replicated, may hold values from -0.15625 to 0.15625
- gain_attn: float32 [180], replicated, may hold values from 0.25 to 1.75
- gain_mlp: float32 [180], replicated, may hold values from 0.25 to 1.75
- pos_table: float32 [225, 6], replicated, may hold values from -4 to 4
Outputs:
- d_features: bfloat16 [512, 512, 180], P('row', 'col')
- grad_qkv: float32 [180, 540], replicated
- grad_proj: float32 [180, 180], replicated
- grad_fc1: float32 [180, 360], replicated
- grad_fc2: float32 [360, 180], replicated
- grad_conv: float32 [9, 180, 180], replicated
The draws below stay inside these ranges and needn't reach their ends.
All inputs are finite; a program needn't handle non-finite values.
Results may differ from the reference program's by a relative error of at most 0.025.
The reference program's roundings to bfloat16 on the way (of `shifted`, `packed`, `attended`, `hidden`, `z_plain`, `d_plain` and `d_packed`) count: a program that leaves them out, or rounds other values in their place, can miss the bound.
Values may be sent and summed in bfloat16 or wider, within the bound.
A program may use at most 128 MiB of HBM per device.

```python
import math
import jax
import jax.numpy as jnp
import numpy as np
from jax import lax

C = 180
HEADS = 6
FF = 360
WIN = 8
SHIFT = 4
H_DEV = 32
W_DEV = 64
HEIGHT = 512
WIDTH = 512
TABLE = 225
N_ROW = 16
N_COL = 8


def draw_w_qkv(key, part):
    key = jax.random.fold_in(key, 11)
    base = jax.random.truncated_normal(key, -4.0, 4.0, (C, 3 * C), jnp.float32) / jnp.sqrt(jnp.float32(C))
    return base.astype(jnp.bfloat16)


def block_levels(key, dims, pieces, smallest, top_value):
    def one(axis_at, parts):
        heights = jax.random.uniform(jax.random.fold_in(jax.random.fold_in(key, 6), axis_at), (parts,), jnp.float32, smallest / len(pieces), top_value / len(pieces))
        return jnp.repeat(jnp.exp(heights), dims[axis_at] // parts).reshape((-1,) + (1,) * (len(dims) - axis_at - 1))

    loudness = one(*pieces[0])
    for cut in pieces[1:]:
        loudness = loudness * one(*cut)
    return loudness


def noise(key, shape, scale, bound, pieces=(), kind=jnp.bfloat16):
    result = jax.random.normal(key, shape, jnp.float32) * scale
    if len(pieces) > 0:
        result = block_levels(key, shape, pieces, -0.22, 0.18) * result
    return jnp.clip(result, min=-bound, max=bound).astype(kind)


def setup_inputs(seed: int = 0) -> dict:
    key_of = jax.random.split(jax.random.key(seed), 11)
    return {
        "features": noise(key_of[0], (HEIGHT, WIDTH, C), 1.0, 6.0, ((0, 16), (1, 8))),
        "cotangent": noise(key_of[1], (HEIGHT, WIDTH, C), 1.0, 6.0, ((0, 16), (1, 8))),
        "w_qkv": draw_w_qkv(jax.random.fold_in(key_of[10], 71), 0),
        "w_proj": noise(key_of[3], (C, C), C ** -0.5, 0.4375),
        "w_fc1": noise(key_of[4], (C, FF), C ** -0.5, 0.4375),
        "w_fc2": noise(key_of[5], (FF, C), FF ** -0.5, 0.3125),
        "w_conv": noise(key_of[6], (9, C, C), (9 * C) ** -0.5, 0.15625),
        "gain_attn": jnp.clip(1.0 + 0.15 * jax.random.normal(key_of[7], (C,), jnp.float32), 0.25, 1.75),
        "gain_mlp": jnp.clip(1.0 + 0.15 * jax.random.normal(key_of[8], (C,), jnp.float32), 0.25, 1.75),
        "pos_table": noise(key_of[9], (TABLE, HEADS), 1.0, 4.0, (), jnp.float32),
    }


def batched(form, left, right):
    return jnp.einsum(form, left.astype(jnp.float32), right.astype(jnp.float32))

def flat_dot(left, right):
    merged = left.reshape(-1, left.shape[-1])
    product = jnp.dot(merged, right, preferred_element_type=jnp.float32)
    return product.reshape(left.shape[:-1] + (right.shape[1],))

def cross_dot(left, right):
    return lax.dot_general(left.reshape(-1, left.shape[-1]), right.reshape(-1, right.shape[-1]), (((0,), (0,)), ((), ())), preferred_element_type=jnp.float32)

def windows(field):
    tile_rows, tile_cols, channels = field.shape
    blocks = field.reshape(tile_rows // WIN, WIN, tile_cols // WIN, WIN, channels)
    return blocks.transpose(0, 2, 1, 3, 4).reshape(-1, WIN * WIN, channels)

def unwindows(tokens, tile_rows, tile_cols):
    channels = tokens.shape[-1]
    blocks = tokens.reshape(tile_rows // WIN, tile_cols // WIN, WIN, WIN, channels)
    return blocks.transpose(0, 2, 1, 3, 4).reshape(tile_rows, tile_cols, channels)

def region(places, extent):
    return (places >= extent - WIN).astype(jnp.int32) + (places >= extent - SHIFT).astype(jnp.int32)

def window_mask(region_rows, region_cols):
    labels = region_rows[:, None] * 3 + region_cols[None, :]
    grouped = windows(labels[:, :, None])[:, :, 0]
    return jnp.where(grouped[:, :, None] == grouped[:, None, :], 0.0, -100.0).astype(jnp.float32)

def position_bias(pos_table):
    coords = np.arange(WIN)
    rows_a = np.repeat(coords, WIN)
    cols_a = np.tile(coords, WIN)
    lookup = (rows_a[:, None] - rows_a[None, :] + WIN - 1) * (2 * WIN - 1) + (cols_a[:, None] - cols_a[None, :] + WIN - 1)
    return pos_table[lookup].transpose(2, 0, 1)

def normalize(values):
    centred = values - lax.optimization_barrier(jnp.mean(values, axis=-1, keepdims=True))
    inverse = lax.rsqrt(lax.optimization_barrier(jnp.mean(centred * centred, axis=-1, keepdims=True)) + 1e-05)
    return (centred * inverse, inverse)

def norm_back(upstream, normed, inverse, gain):
    scaled = upstream * gain
    return inverse * (scaled - lax.optimization_barrier(jnp.mean(scaled, axis=-1, keepdims=True)) - normed * lax.optimization_barrier(jnp.mean(scaled * normed, axis=-1, keepdims=True)))

def gelu_exact(values):
    return jax.nn.gelu(values, approximate=False)

def forward(tokens, masking, params):
    w_qkv, w_proj, w_fc1, w_fc2, gain_attn, gain_mlp, pos_table = params
    n_windows, length, channels = tokens.shape
    head_dim = channels // HEADS
    factor = head_dim ** (-0.5)
    inputs = tokens.astype(jnp.float32)
    normed_one, inverse_one = normalize(inputs)
    n_one = (normed_one * gain_attn).astype(jnp.bfloat16)
    packed = flat_dot(n_one, w_qkv).astype(jnp.bfloat16)
    q_heads = packed[..., :channels].reshape(n_windows, length, HEADS, head_dim)
    k_heads = packed[..., channels:2 * channels].reshape(n_windows, length, HEADS, head_dim)
    v_heads = packed[..., 2 * channels:].reshape(n_windows, length, HEADS, head_dim)
    scores = batched('wqhd,wkhd->whqk', q_heads, k_heads) * factor + position_bias(pos_table)[None] + masking[:, None]
    row_max = lax.optimization_barrier(jnp.max(scores, axis=-1, keepdims=True))
    exp_scores = jnp.exp(scores - row_max)
    attn_prob = exp_scores / lax.optimization_barrier(jnp.sum(exp_scores, axis=-1, keepdims=True))
    attn_low = attn_prob.astype(jnp.bfloat16)
    attended = batched('whqk,wkhd->wqhd', attn_low, v_heads).reshape(n_windows, length, channels).astype(jnp.bfloat16)
    middle = inputs + flat_dot(attended, w_proj)
    normed_two, inverse_two = normalize(middle)
    n_two = (normed_two * gain_mlp).astype(jnp.bfloat16)
    hidden_pre = flat_dot(n_two, w_fc1)
    hidden = gelu_exact(hidden_pre).astype(jnp.bfloat16)
    output = (middle + flat_dot(hidden, w_fc2)).astype(jnp.bfloat16)
    stored = (n_one, normed_one, inverse_one, q_heads, k_heads, v_heads, attn_prob, attn_low, attended, normed_two, inverse_two, n_two, hidden_pre, hidden)
    return (output, stored)

def backward(upstream, stored, params):
    w_qkv, w_proj, w_fc1, w_fc2, gain_attn, gain_mlp, pos_table = params
    n_one, normed_one, inverse_one, q_heads, k_heads, v_heads, attn_prob, attn_low, attended, normed_two, inverse_two, n_two, hidden_pre, hidden = stored
    n_windows, length, channels = upstream.shape
    head_dim = channels // HEADS
    factor = head_dim ** (-0.5)
    grad_fc2 = cross_dot(hidden, upstream)
    d_hidden = flat_dot(upstream, w_fc2.T)
    pullback = jax.vjp(gelu_exact, hidden_pre)[1]
    d_pre = pullback(d_hidden)[0].astype(jnp.bfloat16)
    grad_fc1 = cross_dot(n_two, d_pre)
    d_middle = upstream.astype(jnp.float32) + norm_back(flat_dot(d_pre, w_fc1.T), normed_two, inverse_two, gain_mlp)
    d_attn = d_middle.astype(jnp.bfloat16)
    grad_proj = cross_dot(attended, d_attn)
    d_heads = flat_dot(d_attn, w_proj.T).astype(jnp.bfloat16).reshape(n_windows, length, HEADS, head_dim)
    d_prob = batched('wqhd,wkhd->whqk', d_heads, v_heads)
    d_values = batched('whqk,wqhd->wkhd', attn_low, d_heads)
    d_scores = (attn_prob * (d_prob - lax.optimization_barrier(jnp.sum(attn_prob * d_prob, axis=-1, keepdims=True))) * factor).astype(jnp.bfloat16)
    d_queries = batched('whqk,wkhd->wqhd', d_scores, k_heads)
    d_keys = batched('whqk,wqhd->wkhd', d_scores, q_heads)
    d_packed = jnp.concatenate([d_queries.reshape(n_windows, length, channels), d_keys.reshape(n_windows, length, channels), d_values.reshape(n_windows, length, channels)], axis=-1).astype(jnp.bfloat16)
    grad_qkv = cross_dot(n_one, d_packed)
    d_inputs = d_middle + norm_back(flat_dot(d_packed, w_qkv.T), normed_one, inverse_one, gain_attn)
    return (d_inputs.astype(jnp.bfloat16), (grad_qkv, grad_proj, grad_fc1, grad_fc2))

def conv_back(padded_z, padded_g, w_conv):
    tile_rows = padded_z.shape[0] - 2
    tile_cols = padded_z.shape[1] - 2
    plain_g = padded_g[1:-1, 1:-1]
    d_plain = jnp.zeros((tile_rows, tile_cols, w_conv.shape[1]), jnp.float32)
    taps = []
    for offset in range(9):
        row_tap = offset // 3
        col_tap = offset % 3
        source = padded_g[2 - row_tap:2 - row_tap + tile_rows, 2 - col_tap:2 - col_tap + tile_cols]
        d_plain = d_plain + flat_dot(source, w_conv[offset].T)
        taps.append(cross_dot(padded_z[row_tap:row_tap + tile_rows, col_tap:col_tap + tile_cols], plain_g))
    return (d_plain.astype(jnp.bfloat16), jnp.stack(taps))

def reference(features, cotangent, w_qkv, w_proj, w_fc1, w_fc2, w_conv, gain_attn, gain_mlp, pos_table):
    height = H_DEV * N_ROW
    width = W_DEV * N_COL
    params = (w_qkv, w_proj, w_fc1, w_fc2, gain_attn, gain_mlp, pos_table)
    shifted = jnp.roll(features, (-SHIFT, -SHIFT), (0, 1))
    bands = shifted.reshape(height // WIN, WIN, width, C)
    region_cols = region(jnp.arange(width, dtype=jnp.int32), width)
    numbers = jnp.arange(height // WIN, dtype=jnp.int32)

    def band_mask(number):
        return window_mask(region(number * WIN + jnp.arange(WIN, dtype=jnp.int32), height), region_cols)

    def band_forward(item):
        band, number = item
        return unwindows(forward(windows(band), band_mask(number), params)[0], WIN, width)
    z_shift = lax.map(band_forward, (bands, numbers)).reshape(height, width, C)
    z_plain = jnp.roll(z_shift, (SHIFT, SHIFT), (0, 1))
    padded_z = jnp.pad(z_plain, ((1, 1), (1, 1), (0, 0)))
    padded_g = jnp.pad(cotangent, ((1, 1), (1, 1), (0, 0)))
    d_plain, grad_conv = conv_back(padded_z, padded_g, w_conv)
    d_shift = jnp.roll(d_plain, (-SHIFT, -SHIFT), (0, 1)).reshape(height // WIN, WIN, width, C)
    initial = (jnp.zeros(w_qkv.shape, jnp.float32), jnp.zeros(w_proj.shape, jnp.float32), jnp.zeros(w_fc1.shape, jnp.float32), jnp.zeros(w_fc2.shape, jnp.float32))

    def band_backward(carry, item):
        band, upstream, number = item
        stored = forward(windows(band), band_mask(number), params)[1]
        d_tokens, grads = backward(windows(upstream), stored, params)
        totals = (carry[0] + grads[0], carry[1] + grads[1], carry[2] + grads[2], carry[3] + grads[3])
        return (totals, unwindows(d_tokens, WIN, width))
    totals, d_bands = lax.scan(band_backward, initial, (bands, d_shift, numbers))
    d_features = jnp.roll(d_bands.reshape(height, width, C), (SHIFT, SHIFT), (0, 1))
    scale = 1.0 / math.sqrt(height * width)
    return (d_features, totals[0] * scale, totals[1] * scale, totals[2] * scale, totals[3] * scale, grad_conv * scale)
```

```python
import math

import jax
import jax.numpy as jnp
from jax import lax
from jax.experimental import pallas as pl
from jax.experimental.pallas import tpu as pltpu
from jax.sharding import PartitionSpec as P

C = 180
CP = 192
HEADS = 6
HD = 30
HP = 32
FF = 360
WIN = 8
SHIFT = 4
ROWS = 32
COLS = 64
BLK = 16
NBLK = COLS // BLK
TOK = ROWS * BLK
PAIR = WIN * BLK
FULL = 19
HALF = 7
GROWS = (FULL + HALF) * CP
BF = jnp.bfloat16
F32 = jnp.float32
MESH = pl.DeviceIdType.MESH
VMEM = pltpu.VMEM


def iota(shape, dim):
    return lax.broadcasted_iota(jnp.int32, shape, dim)


def nn(a, b):
    return lax.dot_general(a, b, (((1,), (0,)), ((), ())), preferred_element_type=F32)


def nt(a, b):
    return lax.dot_general(a, b, (((1,), (1,)), ((), ())), preferred_element_type=F32)


def low(a):
    return a.astype(BF)


def eye(rows, cols):
    return low(jnp.where(iota((rows, cols), 0) == iota((rows, cols), 1), 1.0, 0.0))


def spread(padded, plain, pad_dim):
    shape = (padded, plain) if pad_dim == 0 else (plain, padded)
    p = iota(shape, pad_dim)
    c = iota(shape, 1 - pad_dim)
    hit = ((p & (HP - 1)) < HD) & (c == (p >> 5) * HD + (p & (HP - 1)))
    return low(jnp.where(hit, 1.0, 0.0))


def exchange_in(f_ref, g_ref, fr_ref, gr_ref, strip_ref, corner_ref, mine, send, recv):
    row, col = lax.axis_index("row"), lax.axis_index("col")
    n_row, n_col = lax.axis_size("row"), lax.axis_size("col")
    up, down = lax.rem(row + n_row - 1, n_row), lax.rem(row + 1, n_row)
    left, right = lax.rem(col + n_col - 1, n_col), lax.rem(col + 1, n_col)
    barrier = pltpu.get_barrier_semaphore()
    for peer in ((down, col), (row, right), (down, right)):
        pl.semaphore_signal(barrier, inc=1, device_id=peer, device_id_type=MESH)
    fs = f_ref[:, 0:16, :].astype(F32)[:, 0:8, :]
    gs = g_ref[:, 0:16, :].astype(F32)[:, 0:8, :]
    both = jnp.where(iota((ROWS, 8, C), 1) < 4, fs, pltpu.roll(gs, 4, 1))
    mine[32:288, :] = low(both.reshape(ROWS * 8, C))
    mine[0:32, :] = low(gs[:, 4, :])
    pl.semaphore_wait(barrier, 3)
    pairs = (
        (f_ref.at[0:4], fr_ref, (up, col)),
        (g_ref.at[0:5], gr_ref, (up, col)),
        (mine, strip_ref, (row, left)),
        (mine.at[0:80], corner_ref, (up, left)),
    )
    copies = []
    for i, (src, dst, peer) in enumerate(pairs):
        copies.append(
            pltpu.make_async_remote_copy(
                src_ref=src,
                dst_ref=dst,
                send_sem=send.at[i],
                recv_sem=recv.at[i],
                device_id=peer,
                device_id_type=MESH,
            )
        )
        copies[-1].start()
    for copy in copies:
        copy.wait()


def call_exchange_in(features, cotangent):
    return pl.pallas_call(
        exchange_in,
        out_shape=(
            jax.ShapeDtypeStruct((4, COLS, C), BF),
            jax.ShapeDtypeStruct((5, COLS, C), BF),
            jax.ShapeDtypeStruct((288, C), BF),
            jax.ShapeDtypeStruct((80, C), BF),
        ),
        in_specs=[pl.BlockSpec(memory_space=VMEM)] * 2,
        out_specs=[pl.BlockSpec(memory_space=VMEM)] * 4,
        scratch_shapes=[
            VMEM((288, C), BF),
            pltpu.SemaphoreType.DMA((4,)),
            pltpu.SemaphoreType.DMA((4,)),
        ],
        compiler_params=pltpu.CompilerParams(
            collective_id=0, has_side_effects=True, vmem_limit_bytes=32 * 2**20
        ),
        name="exchange_in",
    )(features, cotangent)


def column(gain_ref):
    wide = jnp.where(iota((CP, C), 0) == iota((CP, C), 1), gain_ref[...], 0.0)
    return jnp.sum(wide, axis=1, keepdims=True)


def moments(values):
    mean = jnp.sum(values[:C], axis=0, keepdims=True) * (1.0 / C)
    centred = values - mean
    inner = centred[:C]
    var = jnp.sum(inner * inner, axis=0, keepdims=True) * (1.0 / C)
    return centred, lax.rsqrt(var + 1e-05)


def norm_back(upstream, normed, inverse, gain):
    scaled = upstream * gain
    first = jnp.sum(scaled, axis=0, keepdims=True) * (1.0 / C)
    second = jnp.sum(scaled * normed, axis=0, keepdims=True) * (1.0 / C)
    return inverse * (scaled - first - normed * second)


def gelu_parts(x):
    u = jnp.abs(x) * math.sqrt(0.5)
    t = 1.0 / (1.0 + 0.3275911 * u)
    e = jnp.exp(-u * u)
    poly = t * (
        0.254829592
        + t * (-0.284496736 + t * (1.421413741 + t * (-1.453152027 + t * 1.061405429)))
    )
    tail = 0.5 * poly * e
    cdf = jnp.where(x >= 0.0, 1.0 - tail, tail)
    return cdf, e * (1.0 / math.sqrt(2.0 * math.pi))


def fold(scores, second):
    parts = scores.reshape(WIN, 2, WIN, PAIR)
    return jnp.where(second, parts[:, 1], parts[:, 0]).reshape(WIN * WIN, PAIR)


def unfold(probs, second):
    parts = probs.reshape(WIN, WIN, PAIR)
    zero = jnp.zeros_like(parts)
    both = jnp.stack([jnp.where(second, zero, parts), jnp.where(second, parts, zero)], axis=1)
    return low(both.reshape(PAIR, PAIR))


def two_heads(block):
    zero = jnp.zeros((HP, PAIR), BF)
    top = jnp.concatenate([block[:HP], zero], axis=1)
    return jnp.concatenate([top, jnp.concatenate([zero, block[HP:]], axis=1)], axis=0)


def own_heads(product):
    return jnp.concatenate([product[:HP, :PAIR], product[HP:, PAIR:]], axis=0)


def compute(
    f_ref, g_ref, fr_ref, gr_ref, strip_ref, corner_ref,
    wqkv_ref, wproj_ref, w1_ref, w2_ref, wconv_ref, g1_ref, g2_ref, d_ref,
    out_ref, grads_ref,
    xs, gs, wqkvt, wqkvp, wprojt, wprojp, w1t, w1p, w2t, w2p, wcp, bias,
    packed, attended, probs, knat, vnat, dheads, dpacked,
    a_conv, a_proj, a_fc1, a_fc2, a_qkv,
):
    row, col = lax.axis_index("row"), lax.axis_index("col")
    last_row = row == lax.axis_size("row") - 1
    last_col = col == lax.axis_size("col") - 1
    factor = HD**-0.5

    pad = eye(CP, C)
    sel, sel_one = spread(3 * CP, 3 * C, 0), spread(CP, C, 0)
    wq = low(nn(pad, wqkv_ref[...]))
    wqkvt[...] = low(nt(sel, wq))
    wqkvp[...] = low(nt(wq, sel))
    turned = low(nt(pad, wproj_ref[...]))
    wprojt[...] = low(nt(turned, sel_one))
    wprojp[...] = low(nt(sel_one, turned))
    w1p[...] = low(nn(pad, w1_ref[...]))
    w1t[...] = low(nt(eye(FF, FF), w1p[...]))
    w2t[...] = low(nt(pad, w2_ref[...]))
    w2p[...] = low(nn(w2_ref[...], eye(C, CP)))
    for t in range(9):
        wcp[t] = low(nn(pad, wconv_ref[t]))
    gain1, gain2 = column(g1_ref), column(g2_ref)
    for h in range(HEADS):
        table = d_ref[h]
        for kr in range(WIN):
            start = (WIN - 1 - kr) * BLK
            bias[h, kr * WIN : (kr + 1) * WIN, :] = table[:, start : start + PAIR]
    for acc in (a_conv, a_proj, a_fc1, a_fc2, a_qkv):
        acc[...] = jnp.zeros_like(acc)

    sub = iota((8, C), 0)

    def tail(body, last):
        return jnp.concatenate([body[:56], last], axis=0)

    def put_x(i, v, extra):
        rolled = pltpu.roll(v, 60, 0)
        full = low(tail(rolled, jnp.where(sub < 4, rolled[56:], pltpu.roll(extra, 4, 0))))
        for b in range(NBLK):
            xs[b, pl.ds(pl.multiple_of(i * BLK, BLK), BLK), :] = full[b * BLK : (b + 1) * BLK]

    keep0 = jnp.where((sub == 3) & last_col, 0.0, 1.0)
    keep2 = jnp.where((sub == 4) & last_col, 0.0, 1.0)

    def put_g(i, v, extra, fifth):
        r5, r4, r3 = pltpu.roll(v, 59, 0), pltpu.roll(v, 60, 0), pltpu.roll(v, 61, 0)
        e5 = jnp.where(sub == 7, fifth, pltpu.roll(extra, 7, 0))
        l5 = jnp.where(sub < 3, r5[56:], e5) * keep0
        l4 = jnp.where(sub < 4, r4[56:], extra)
        l3 = jnp.where(sub < 5, r3[56:], pltpu.roll(extra, 1, 0)) * keep2
        for k, (r, last) in enumerate(((r5, l5), (r4, l4), (r3, l3))):
            full = low(tail(r, last))
            for b in range(NBLK):
                gs[k, b, pl.ds(pl.multiple_of(i * BLK, BLK), BLK), :] = full[
                    b * BLK : (b + 1) * BLK
                ]

    extras = strip_ref[32:288, :].astype(F32).reshape(ROWS, 8, C)
    fifths = strip_ref[0:32, :].astype(F32)
    c_extras = corner_ref[32:80, :].astype(F32).reshape(6, 8, C)
    c_fifths = corner_ref[0:16, :].astype(F32)
    for i in range(ROWS):
        if i < ROWS - 4:
            put_x(i, f_ref[i + 4].astype(F32), extras[i + 4])
        else:
            put_x(i, fr_ref[i - 28].astype(F32), c_extras[i - 28])
    for i in range(ROWS + 2):
        if i < ROWS - 3:
            put_g(i, g_ref[i + 3].astype(F32), extras[i + 3], fifths[i + 3 : i + 4])
        else:
            k = i - 29
            put_g(i, gr_ref[k].astype(F32), c_extras[k], c_fifths[k : k + 1])

    lane = iota((1, PAIR), 1)
    second = ((lane >> 3) & 1) == 1
    ones_pair = eye(PAIR, PAIR)
    k_sub, q_lane = iota((WIN * WIN, PAIR), 0), iota((WIN * WIN, PAIR), 1)
    rows_differ = ((k_sub >> 5) & 1) != ((q_lane >> 6) & 1)
    cols_differ = (((k_sub >> 2) & 1) != ((q_lane >> 2) & 1)) & (((q_lane >> 3) & 1) == 1)
    tok = iota((1, TOK), 1) >> 4
    drop0 = (tok == 27) & last_row
    drop2 = (tok == 28) & last_row

    def block(b, carry):
        x = nt(eye(CP, C), xs[b])
        centred, inv1 = moments(x)
        normed1 = centred * inv1
        n1 = low(normed1 * gain1)
        packed[...] = low(nn(wqkvt[...], n1))
        col_flag = last_col & (b == NBLK - 1)

        def attend(a, carry):
            lanes = pl.ds(pl.multiple_of(a * PAIR, PAIR), PAIR)
            row_flag = last_row & (a == ROWS // WIN - 1)
            mask = jnp.where((rows_differ & row_flag) | (cols_differ & col_flag), -100.0, 0.0)
            for j in range(HEADS // 2):
                q = packed[64 * j : 64 * j + 64, lanes]
                k = packed[CP + 64 * j : CP + 64 * j + 64, lanes]
                v = packed[2 * CP + 64 * j : 2 * CP + 64 * j + 64, lanes]
                kn = low(nt(ones_pair, k))
                knat[a, j] = kn
                vnat[a, j] = low(nt(ones_pair, v))
                scores = nn(kn, two_heads(q))
                wide = []
                for s in range(2):
                    sc = fold(scores[:, s * PAIR : (s + 1) * PAIR], second)
                    sc = sc * factor + bias[2 * j + s] + mask
                    e = jnp.exp(sc - jnp.max(sc, axis=0, keepdims=True))
                    p = e * (1.0 / jnp.sum(e, axis=0, keepdims=True))
                    probs[a, 2 * j + s] = p
                    wide.append(unfold(p, second))
                o = nn(v, jnp.concatenate(wide, axis=1))
                attended[64 * j : 64 * j + 64, lanes] = low(own_heads(o))
            return carry

        lax.fori_loop(0, ROWS // WIN, attend, 0)

        middle = x + nn(wprojt[...], attended[...])
        centred2, inv2 = moments(middle)
        normed2 = centred2 * inv2
        n2 = low(normed2 * gain2)
        pre = nn(w1t[...], n2)
        cdf, pdf = gelu_parts(pre)
        hidden = low(pre * cdf)
        slope = cdf + pre * pdf
        z = low(middle + nn(w2t[...], hidden))

        z0 = jnp.where(drop0, 0.0, z.astype(F32)).astype(BF)
        z2 = jnp.where(drop2, 0.0, z.astype(F32)).astype(BF)
        total = jnp.zeros((CP, TOK), F32)
        for dy in range(3):
            part = jnp.zeros((CP, TOK), F32)
            zd = (z0, z, z2)[dy]
            for dx in range(3):
                source = gs[dx, b, (2 - dy) * BLK : (2 - dy) * BLK + TOK, :]
                part = part + nt(wcp[3 * dy + dx], source)
                a_conv[3 * dy + dx] += nn(zd, source)
            if dy == 0:
                part = jnp.where(drop0, 0.0, part)
            if dy == 2:
                part = jnp.where(drop2, 0.0, part)
            total = total + part
        d_shift = low(total)

        a_fc2[:FF, :] += nt(hidden, d_shift)
        d_pre = low(nn(w2p[...], d_shift) * slope)
        a_fc1[:, :FF] += nt(n2, d_pre)
        d_middle = d_shift.astype(F32) + norm_back(nn(w1p[...], d_pre), normed2, inv2, gain2)
        d_attn = low(d_middle)
        a_proj[...] += nt(attended[...], d_attn)
        dheads[...] = low(nn(wprojp[...], d_attn))

        def attend_back(a, carry):
            lanes = pl.ds(pl.multiple_of(a * PAIR, PAIR), PAIR)
            for j in range(HEADS // 2):
                q = packed[64 * j : 64 * j + 64, lanes]
                k = packed[CP + 64 * j : CP + 64 * j + 64, lanes]
                do = dheads[64 * j : 64 * j + 64, lanes]
                d_prob = nn(vnat[a, j], two_heads(do))
                p_wide, s_wide = [], []
                for s in range(2):
                    p = probs[a, 2 * j + s]
                    dp = fold(d_prob[:, s * PAIR : (s + 1) * PAIR], second)
                    ds = p * (dp - jnp.sum(p * dp, axis=0, keepdims=True)) * factor
                    p_wide.append(unfold(p, second))
                    s_wide.append(unfold(ds, second))
                dv = nt(do, jnp.concatenate(p_wide, axis=0))
                dq = nn(k, jnp.concatenate(s_wide, axis=1))
                dk = nt(q, jnp.concatenate(s_wide, axis=0))
                dpacked[64 * j : 64 * j + 64, lanes] = low(own_heads(dq))
                dpacked[CP + 64 * j : CP + 64 * j + 64, lanes] = low(own_heads(dk))
                dpacked[2 * CP + 64 * j : 2 * CP + 64 * j + 64, lanes] = low(own_heads(dv))
            return carry

        lax.fori_loop(0, ROWS // WIN, attend_back, 0)

        a_qkv[...] += nt(n1, dpacked[...])
        d_in = d_middle + norm_back(nn(wqkvp[...], dpacked[...]), normed1, inv1, gain1)
        d_low = low(d_in)
        for a in range(ROWS // WIN):
            natural = nt(ones_pair, d_low[:, a * PAIR : (a + 1) * PAIR])
            out_ref[b, a * PAIR : (a + 1) * PAIR, :] = low(natural[:, :C])
        return carry

    lax.fori_loop(0, NBLK, block, 0)

    rests = []
    place = 0

    def put(tile):
        nonlocal place
        grads_ref[place * CP : (place + 1) * CP, :] = low(tile)
        place += 1

    half_zero = jnp.zeros((CP, 64), F32)
    for t in range(9):
        put(a_conv[t, :, 0:128])
        rests.append(jnp.concatenate([a_conv[t, :, 128:C], half_zero[:, : 64 - (C - 128)]], axis=1))
    put(a_proj[:, 0:128])
    rests.append(a_proj[:, 128:192])
    for i in range(2):
        put(a_fc2[i * CP : (i + 1) * CP, 0:128])
        rests.append(a_fc2[i * CP : (i + 1) * CP, 128:192])
    for i in range(3):
        put(a_fc1[:, i * 128 : (i + 1) * 128])
    for i in range(4):
        put(a_qkv[:, i * 128 : (i + 1) * 128])
    rests.append(a_qkv[:, 512:576])
    rests.append(half_zero)
    for i in range(HALF):
        put(jnp.concatenate([rests[2 * i], rests[2 * i + 1]], axis=1))


def call_compute(features, cotangent, halo, w_qkv, w_proj, w_fc1, w_fc2, w_conv, g1, g2, table):
    scratch = [
        VMEM((NBLK, TOK, C), BF),
        VMEM((3, NBLK, (ROWS + 2) * BLK, C), BF),
        VMEM((3 * CP, CP), BF),
        VMEM((CP, 3 * CP), BF),
        VMEM((CP, CP), BF),
        VMEM((CP, CP), BF),
        VMEM((FF, CP), BF),
        VMEM((CP, FF), BF),
        VMEM((CP, FF), BF),
        VMEM((FF, CP), BF),
        VMEM((9, CP, C), BF),
        VMEM((HEADS, WIN * WIN, PAIR), F32),
        VMEM((3 * CP, TOK), BF),
        VMEM((CP, TOK), BF),
        VMEM((ROWS // WIN, HEADS, WIN * WIN, PAIR), F32),
        VMEM((ROWS // WIN, HEADS // 2, PAIR, 64), BF),
        VMEM((ROWS // WIN, HEADS // 2, PAIR, 64), BF),
        VMEM((CP, TOK), BF),
        VMEM((3 * CP, TOK), BF),
        VMEM((9, CP, C), F32),
        VMEM((CP, CP), F32),
        VMEM((CP, 384), F32),
        VMEM((384, CP), F32),
        VMEM((CP, 3 * CP), F32),
    ]
    return pl.pallas_call(
        compute,
        out_shape=(
            jax.ShapeDtypeStruct((NBLK, TOK, C), BF),
            jax.ShapeDtypeStruct((GROWS, 128), BF),
        ),
        in_specs=[pl.BlockSpec(memory_space=VMEM)] * 14,
        out_specs=[pl.BlockSpec(memory_space=VMEM)] * 2,
        scratch_shapes=scratch,
        compiler_params=pltpu.CompilerParams(vmem_limit_bytes=56 * 2**20),
        name="compute",
    )(features, cotangent, *halo, w_qkv, w_proj, w_fc1, w_fc2, w_conv, g1, g2, table)


SIDE = 4
HALF_ROWS = GROWS // 2
PART = HALF_ROWS // 3
SHARE = PART // SIDE


def exchange_out(
    d_ref, grads_ref, sum_ref, hr_ref, hs_ref, hc_ref,
    mine, core_in, held, first_in, second_in, third_in,
    halo_send, halo_recv, core_send, core_recv, send, recv,
):
    row, col = lax.axis_index("row"), lax.axis_index("col")
    n_row, n_col = lax.axis_size("row"), lax.axis_size("col")
    up, down = lax.rem(row + n_row - 1, n_row), lax.rem(row + 1, n_row)
    left, right = lax.rem(col + n_col - 1, n_col), lax.rem(col + 1, n_col)
    core, z, y = lax.rem(row, 2), lax.rem(row // 2, SIDE), lax.rem(col, SIDE)
    x = (row // 8) * 2 + col // SIDE
    here = (x, y, z)

    def device(xyz, c):
        return ((xyz[0] // 2) * 8 + xyz[2] * 2 + c, lax.rem(xyz[0], 2) * SIDE + xyz[1])

    def along(axis, k):
        there = list(here)
        there[axis] = lax.rem(there[axis] + k, SIDE)
        return device(there, core)

    sibling = device(here, 1 - core)
    barrier = pltpu.get_barrier_semaphore()
    greeted = [sibling, (up, col), (row, left), (up, left)]
    greeted += [along(axis, k) for axis in range(3) for k in range(1, SIDE)]
    for peer in greeted:
        pl.semaphore_signal(barrier, inc=1, device_id=peer, device_id_type=MESH)
    pl.semaphore_wait(barrier, len(greeted))

    started = []

    def copy(src, dst, s, r, peer):
        c = pltpu.make_async_remote_copy(
            src_ref=src, dst_ref=dst, send_sem=s, recv_sem=r, device_id=peer, device_id_type=MESH
        )
        c.start()
        started.append(c)
        return c

    def rows(start, size):
        return pl.ds(pl.multiple_of(start, 16), size)

    mine_at, other_at = core * HALF_ROWS, (1 - core) * HALF_ROWS
    cores = [
        copy(
            grads_ref.at[rows(other_at + p * PART, PART)],
            core_in.at[p],
            core_send.at[p],
            core_recv.at[p],
            sibling,
        )
        for p in range(3)
    ]
    halos = [copy(d_ref.at[:, 448:512, :], hr_ref, halo_send.at[0], halo_recv.at[0], (down, col))]
    wide = d_ref[NBLK - 1].astype(F32).reshape(ROWS, 2, 8, C)[:, 1]
    mine[...] = low(wide.reshape(ROWS * 8, C))
    halos.append(copy(mine, hs_ref, halo_send.at[1], halo_recv.at[1], (row, right)))
    halos.append(
        copy(mine.at[224:256], hc_ref, halo_send.at[2], halo_recv.at[2], (down, right))
    )

    def spread_out(p, step, source, target, axis):
        target[p, here[axis]] = source
        return [
            copy(
                target.at[p, here[axis]],
                target.at[p, here[axis]],
                send.at[step, p, k - 1],
                recv.at[step, p, k - 1],
                along(axis, k),
            )
            for k in range(1, SIDE)
        ]

    def gathered(copies, target, p):
        for c in copies:
            c.wait_recv()
        total = target[p, 0].astype(F32)
        for k in range(1, SIDE):
            total = total + target[p, k].astype(F32)
        return low(total)

    waits = []
    for p in range(3):
        cores[p].wait_recv()
        own = grads_ref[rows(mine_at + p * PART, PART), :].astype(F32)
        held[p] = low(own + core_in[p].astype(F32))
        group = []
        for k in range(1, SIDE):
            share = lax.rem(here[p] + k, SIDE)
            group.append(
                copy(
                    held.at[p, rows(share * SHARE, SHARE)],
                    first_in.at[p, k - 1],
                    send.at[0, p, k - 1],
                    recv.at[0, p, k - 1],
                    along(p, k),
                )
            )
        waits.append(group)
    nexts = []
    for p in range(3):
        total = held[p, rows(here[p] * SHARE, SHARE), :].astype(F32)
        for k in range(1, SIDE):
            waits[p][k - 1].wait_recv()
            total = total + first_in[p, k - 1].astype(F32)
        nexts.append(spread_out(p, 1, low(total), second_in, (p + 1) % 3))
    lasts = []
    for p in range(3):
        lasts.append(
            spread_out(p, 2, gathered(nexts[p], second_in, p), third_in, (p + 2) % 3)
        )
    backs = []
    for p in range(3):
        at = rows(mine_at + p * PART + here[p] * SHARE, SHARE)
        sum_ref[at, :] = gathered(lasts[p], third_in, p)
        backs.append(
            [
                copy(
                    sum_ref.at[at],
                    sum_ref.at[at],
                    send.at[3, p, k - 1],
                    recv.at[3, p, k - 1],
                    along(p, k),
                )
                for k in range(1, SIDE)
            ]
        )
    ends = []
    for p in range(3):
        for c in backs[p]:
            c.wait_recv()
        at = rows(mine_at + p * PART, PART)
        ends.append(
            copy(sum_ref.at[at], sum_ref.at[at], core_send.at[3 + p], core_recv.at[3 + p], sibling)
        )
    for c in ends + halos:
        c.wait_recv()
    for c in started:
        c.wait_send()


def call_exchange_out(d_shifted, grads):
    slots = VMEM((3, SIDE, SHARE, 128), BF)
    return pl.pallas_call(
        exchange_out,
        out_shape=(
            jax.ShapeDtypeStruct((GROWS, 128), BF),
            jax.ShapeDtypeStruct((NBLK, 64, C), BF),
            jax.ShapeDtypeStruct((256, C), BF),
            jax.ShapeDtypeStruct((32, C), BF),
        ),
        in_specs=[pl.BlockSpec(memory_space=VMEM)] * 2,
        out_specs=[pl.BlockSpec(memory_space=VMEM)] * 4,
        scratch_shapes=[
            VMEM((256, C), BF),
            VMEM((3, PART, 128), BF),
            VMEM((3, PART, 128), BF),
            VMEM((3, SIDE - 1, SHARE, 128), BF),
            slots,
            slots,
            pltpu.SemaphoreType.DMA((3,)),
            pltpu.SemaphoreType.DMA((3,)),
            pltpu.SemaphoreType.DMA((6,)),
            pltpu.SemaphoreType.DMA((6,)),
            pltpu.SemaphoreType.DMA((4, 3, SIDE - 1)),
            pltpu.SemaphoreType.DMA((4, 3, SIDE - 1)),
        ],
        compiler_params=pltpu.CompilerParams(
            collective_id=1, has_side_effects=True, vmem_limit_bytes=32 * 2**20
        ),
        name="exchange_out",
    )(d_shifted, grads)


def results(
    d_ref, hr_ref, hs_ref, hc_ref, sum_ref, out_ref, qkv_ref, proj_ref, fc1_ref, fc2_ref, conv_ref
):
    sub = iota((8, C), 0)
    extras = hs_ref[...].astype(F32).reshape(ROWS, 8, C)
    corners = hc_ref[...].astype(F32).reshape(4, 8, C)
    for i in range(ROWS):
        if i < 4:
            pieces = [hr_ref[b, i * BLK : (i + 1) * BLK, :] for b in range(NBLK)]
            extra = corners[i]
        else:
            pieces = [d_ref[b, (i - 4) * BLK : (i - 3) * BLK, :] for b in range(NBLK)]
            extra = extras[i - 4]
        v = pltpu.roll(jnp.concatenate(pieces, axis=0).astype(F32), 4, 0)
        head = jnp.where(sub < 4, pltpu.roll(extra, 4, 0), v[:8])
        out_ref[i] = low(jnp.concatenate([head, v[8:]], axis=0))

    scale = 1.0 / math.sqrt(ROWS * COLS * lax.axis_size("row") * lax.axis_size("col"))

    def full(i):
        return sum_ref[i * CP : (i + 1) * CP, :]

    def rest(i):
        return full(FULL + i // 2)[:, 64 * (i % 2) : 64 * (i % 2) + 64]

    def square(i, r):
        return jnp.concatenate([full(i), rest(r)], axis=1)

    for t in range(9):
        conv_ref[t] = square(t, t).astype(F32)[:C, :C] * scale
    proj_ref[...] = nn(spread(CP, C, 1), square(9, 9))[:, :C] * scale
    fc2_ref[:CP, :] = square(10, 10).astype(F32)[:, :C] * scale
    fc2_ref[CP:, :] = square(11, 11).astype(F32)[: FF - CP, :C] * scale
    fc1 = jnp.concatenate([full(12), full(13), full(14)], axis=1).astype(F32)
    fc1_ref[...] = fc1[:C, :FF] * scale
    qkv = jnp.concatenate([full(15), full(16), full(17), full(18), rest(12)], axis=1)
    qkv_ref[...] = nn(qkv, spread(3 * CP, 3 * C, 0))[:C] * scale


def call_results(d_shifted, halo, sums):
    return pl.pallas_call(
        results,
        out_shape=(
            jax.ShapeDtypeStruct((ROWS, COLS, C), BF),
            jax.ShapeDtypeStruct((C, 3 * C), F32),
            jax.ShapeDtypeStruct((C, C), F32),
            jax.ShapeDtypeStruct((C, FF), F32),
            jax.ShapeDtypeStruct((FF, C), F32),
            jax.ShapeDtypeStruct((9, C, C), F32),
        ),
        in_specs=[pl.BlockSpec(memory_space=VMEM)] * 5,
        out_specs=[pl.BlockSpec(memory_space=VMEM)] * 6,
        compiler_params=pltpu.CompilerParams(vmem_limit_bytes=32 * 2**20),
        name="results",
    )(d_shifted, *halo, sums)


def bias_rows(pos_table):
    square = pos_table.reshape(15, 15, HEADS)
    rows = jnp.stack([square[:, 7 - kc : 15 - kc] for kc in range(WIN)])
    rows = rows.transpose(3, 0, 1, 2)[:, :, :, None, :]
    return jnp.broadcast_to(rows, (HEADS, WIN, 15, 2, WIN)).reshape(HEADS, WIN, 15 * BLK)


def local(features, cotangent, w_qkv, w_proj, w_fc1, w_fc2, w_conv, gain_attn, gain_mlp, pos_table):
    halo = call_exchange_in(features, cotangent)
    d_shifted, grads = call_compute(
        features,
        cotangent,
        halo,
        w_qkv,
        w_proj,
        w_fc1,
        w_fc2,
        w_conv,
        gain_attn.reshape(1, C),
        gain_mlp.reshape(1, C),
        bias_rows(pos_table),
    )
    sums, *halo_out = call_exchange_out(d_shifted, grads)
    return call_results(d_shifted, halo_out, sums)


def solution(mesh):
    return jax.shard_map(
        local,
        mesh=mesh,
        in_specs=(P("row", "col", None), P("row", "col", None)) + (P(),) * 8,
        out_specs=(P("row", "col", None),) + (P(),) * 5,
        check_vma=False,
    )
```

```python
import math

import jax
import jax.numpy as jnp
from jax import lax
from jax.experimental import pallas as pl
from jax.experimental.pallas import tpu as pltpu
from jax.sharding import PartitionSpec as P

C = 180
CP = 192
HEADS = 6
HD = 30
HP = 32
FF = 360
WIN = 8
SHIFT = 4
ROWS = 32
COLS = 64
BLK = 16
NBLK = COLS // BLK
TOK = ROWS * BLK
PAIR = WIN * BLK
SIDE = 4
TILES = (22, 6)
BASE = (0, TILES[0] * CP)
GROWS = sum(TILES) * CP
HALVES = tuple(t * CP // 2 for t in TILES)
PARTS = tuple(h // 3 for h in HALVES)
SHARES = tuple(p // SIDE for p in PARTS)
BF = jnp.bfloat16
F32 = jnp.float32
MESH = pl.DeviceIdType.MESH
VMEM = pltpu.VMEM


def iota(shape, dim):
    return lax.broadcasted_iota(jnp.int32, shape, dim)


def nn(a, b):
    return lax.dot_general(a, b, (((1,), (0,)), ((), ())), preferred_element_type=F32)


def nt(a, b):
    return lax.dot_general(a, b, (((1,), (1,)), ((), ())), preferred_element_type=F32)


def low(a):
    return a.astype(BF)


def eye(rows, cols):
    return low(jnp.where(iota((rows, cols), 0) == iota((rows, cols), 1), 1.0, 0.0))


def spread(padded, plain, pad_dim):
    shape = (padded, plain) if pad_dim == 0 else (plain, padded)
    p = iota(shape, pad_dim)
    c = iota(shape, 1 - pad_dim)
    hit = ((p & (HP - 1)) < HD) & (c == (p >> 5) * HD + (p & (HP - 1)))
    return low(jnp.where(hit, 1.0, 0.0))


def column(gain_ref):
    wide = jnp.where(iota((CP, C), 0) == iota((CP, C), 1), gain_ref[...], 0.0)
    return jnp.sum(wide, axis=1, keepdims=True)


def moments(values):
    mean = jnp.sum(values[:C], axis=0, keepdims=True) * (1.0 / C)
    centred = values - mean
    inner = centred[:C]
    var = jnp.sum(inner * inner, axis=0, keepdims=True) * (1.0 / C)
    return centred, lax.rsqrt(var + 1e-05)


def norm_back(upstream, normed, inverse, gain):
    scaled = upstream * gain
    first = jnp.sum(scaled, axis=0, keepdims=True) * (1.0 / C)
    second = jnp.sum(scaled * normed, axis=0, keepdims=True) * (1.0 / C)
    return inverse * (scaled - first - normed * second)


def gelu_parts(x):
    u = jnp.abs(x) * math.sqrt(0.5)
    t = 1.0 / (1.0 + 0.3275911 * u)
    e = jnp.exp(-u * u)
    poly = t * (
        0.254829592
        + t * (-0.284496736 + t * (1.421413741 + t * (-1.453152027 + t * 1.061405429)))
    )
    tail = 0.5 * poly * e
    cdf = jnp.where(x >= 0.0, 1.0 - tail, tail)
    return cdf, e * (1.0 / math.sqrt(2.0 * math.pi))


def fold(scores, second):
    parts = scores.reshape(WIN, 2, WIN, PAIR)
    return jnp.where(second, parts[:, 1], parts[:, 0]).reshape(WIN * WIN, PAIR)


def unfold(probs, second):
    parts = probs.reshape(WIN, WIN, PAIR)
    zero = jnp.zeros_like(parts)
    both = jnp.stack([jnp.where(second, zero, parts), jnp.where(second, parts, zero)], axis=1)
    return low(both.reshape(PAIR, PAIR))


def two_heads(block):
    zero = jnp.zeros((HP, PAIR), BF)
    top = jnp.concatenate([block[:HP], zero], axis=1)
    return jnp.concatenate([top, jnp.concatenate([zero, block[HP:]], axis=1)], axis=0)


def own_heads(product):
    return jnp.concatenate([product[:HP, :PAIR], product[HP:, PAIR:]], axis=0)


def tn(a, b):
    return lax.dot_general(a, b, (((0,), (0,)), ((), ())), preferred_element_type=F32)


def layer(
    f_ref, g_ref, wqkv_ref, wproj_ref, w1_ref, w2_ref, wconv_ref, g1_ref, g2_ref, pos_ref,
    d_ref, sum_ref, hr_ref, hs_ref, hc_ref,
    fr_ref, gr_ref, strip_ref, corner_ref, strip_in, strip_out,
    grads_ref, core_in0, core_in1, held0, held1, first0, first1, second0, second1, third0, third1,
    xs, gs, wqkvt, wqkvp, wprojt, wprojp, w1t, w1p, w2t, w2p, wcp, bias,
    s_x, s_inv1, s_n1, packed, attended, probs, s_norm2, s_inv2, s_n2, s_slope, s_hidden, s_z,
    dheads, dpacked, s_dmid,
    a_conv, a_proj, a_fc1, a_fc2, a_qkv,
    in_send, in_recv, out_send, out_recv, core_send, core_recv, send, recv,
):
    row, col = lax.axis_index("row"), lax.axis_index("col")
    n_row, n_col = lax.axis_size("row"), lax.axis_size("col")
    up, down = lax.rem(row + n_row - 1, n_row), lax.rem(row + 1, n_row)
    left, right = lax.rem(col + n_col - 1, n_col), lax.rem(col + 1, n_col)
    last_row, last_col = row == n_row - 1, col == n_col - 1
    factor = HD**-0.5
    core, z, y = lax.rem(row, 2), lax.rem(row // 2, SIDE), lax.rem(col, SIDE)
    x = (row // 8) * 2 + col // SIDE
    here = (x, y, z)

    def device(xyz, c):
        return ((xyz[0] // 2) * 8 + xyz[2] * 2 + c, lax.rem(xyz[0], 2) * SIDE + xyz[1])

    def along(axis, k):
        there = list(here)
        there[axis] = lax.rem(there[axis] + k, SIDE)
        return device(there, core)

    sibling = device(here, 1 - core)
    barrier = pltpu.get_barrier_semaphore()
    greeted = [sibling, (up, col), (row, left), (up, left), (down, col), (row, right)]
    greeted += [(down, right)] + [along(axis, k) for axis in range(3) for k in range(1, SIDE)]
    for peer in greeted:
        pl.semaphore_signal(barrier, inc=1, device_id=peer, device_id_type=MESH)

    started = []

    def copy(src, dst, s, r, peer):
        c = pltpu.make_async_remote_copy(
            src_ref=src, dst_ref=dst, send_sem=s, recv_sem=r, device_id=peer, device_id_type=MESH
        )
        c.start()
        started.append(c)
        return c

    fs = f_ref[:, 0:16, :].astype(F32)[:, 0:8, :]
    cs = g_ref[:, 0:16, :].astype(F32)[:, 0:8, :]
    both = jnp.where(iota((ROWS, 8, C), 1) < 4, fs, pltpu.roll(cs, 4, 1))
    strip_in[32:288, :] = low(both.reshape(ROWS * 8, C))
    strip_in[0:32, :] = low(cs[:, 4, :])
    pl.semaphore_wait(barrier, len(greeted))
    arriving = [
        copy(strip_in.at[0:80], corner_ref, in_send.at[3], in_recv.at[3], (up, left)),
        copy(strip_in, strip_ref, in_send.at[2], in_recv.at[2], (row, left)),
        copy(f_ref.at[0:4], fr_ref, in_send.at[0], in_recv.at[0], (up, col)),
        copy(g_ref.at[0:5], gr_ref, in_send.at[1], in_recv.at[1], (up, col)),
    ]

    pad = eye(CP, C)
    sel, sel_one = spread(3 * CP, 3 * C, 0), spread(CP, C, 0)
    wq = low(nn(pad, wqkv_ref[...]))
    wqkvt[...] = low(nt(sel, wq))
    wqkvp[...] = low(nt(wq, sel))
    turned = low(nt(pad, wproj_ref[...]))
    wprojt[...] = low(nt(turned, sel_one))
    wprojp[...] = low(nt(sel_one, turned))
    w1p[...] = low(nn(pad, w1_ref[...]))
    w1t[...] = low(nt(eye(FF, FF), w1p[...]))
    w2t[...] = low(nn(pad, w2_ref[...]))
    w2p[...] = low(nt(eye(FF, FF), w2t[...]))
    for t in range(9):
        wcp[t] = low(nn(pad, wconv_ref[t]))
    gain1, gain2 = column(g1_ref), column(g2_ref)

    table = pos_ref[...]
    high = low(table)
    mid = low(table - high.astype(F32))
    rest_piece = low(table - high.astype(F32) - mid.astype(F32))
    entry, place = iota((225, 15 * BLK), 0), iota((225, 15 * BLK), 1)
    for kc in range(WIN):
        hit = entry == (place >> 4) * 15 + (place & 7) - kc + 7
        pick = low(jnp.where(hit, 1.0, 0.0))
        line = nn(high, pick) + nn(mid, pick) + nn(rest_piece, pick)
        for h in range(HEADS):
            for kr in range(WIN):
                start = (WIN - 1 - kr) * BLK
                at = kr * WIN + kc
                bias[h, at : at + 1, :] = line[h : h + 1, start : start + PAIR]
    for acc in (a_conv, a_proj, a_fc1, a_fc2, a_qkv):
        acc[...] = jnp.zeros_like(acc)

    for c in arriving:
        c.wait_recv()

    sub = iota((8, C), 0)

    def tail(body, last):
        return jnp.concatenate([body[:56], last], axis=0)

    def put_x(i, v, extra):
        rolled = pltpu.roll(v, 60, 0)
        whole = low(tail(rolled, jnp.where(sub < 4, rolled[56:], pltpu.roll(extra, 4, 0))))
        for b in range(NBLK):
            xs[b, i * BLK : (i + 1) * BLK, :] = whole[b * BLK : (b + 1) * BLK]

    keep0 = jnp.where((sub == 3) & last_col, 0.0, 1.0)
    keep2 = jnp.where((sub == 4) & last_col, 0.0, 1.0)

    def put_g(i, v, extra, fifth):
        r5, r4, r3 = pltpu.roll(v, 59, 0), pltpu.roll(v, 60, 0), pltpu.roll(v, 61, 0)
        e5 = jnp.where(sub == 7, fifth, pltpu.roll(extra, 7, 0))
        l5 = jnp.where(sub < 3, r5[56:], e5) * keep0
        l4 = jnp.where(sub < 4, r4[56:], extra)
        l3 = jnp.where(sub < 5, r3[56:], pltpu.roll(extra, 1, 0)) * keep2
        for k, (r, last) in enumerate(((r5, l5), (r4, l4), (r3, l3))):
            whole = low(tail(r, last))
            for b in range(NBLK):
                gs[k, b, i * BLK : (i + 1) * BLK, :] = whole[b * BLK : (b + 1) * BLK]

    extras = strip_ref[32:288, :].astype(F32).reshape(ROWS, 8, C)
    fifths = strip_ref[0:32, :].astype(F32)
    c_extras = corner_ref[32:80, :].astype(F32).reshape(6, 8, C)
    c_fifths = corner_ref[0:16, :].astype(F32)
    for i in range(ROWS):
        if i < ROWS - 4:
            put_x(i, f_ref[i + 4].astype(F32), extras[i + 4])
        else:
            put_x(i, fr_ref[i - 28].astype(F32), c_extras[i - 28])
    for i in range(ROWS + 2):
        if i < ROWS - 3:
            put_g(i, g_ref[i + 3].astype(F32), extras[i + 3], fifths[i + 3 : i + 4])
        else:
            k = i - 29
            put_g(i, gr_ref[k].astype(F32), c_extras[k], c_fifths[k : k + 1])

    lane = iota((1, PAIR), 1)
    second = ((lane >> 3) & 1) == 1
    k_sub, q_lane = iota((WIN * WIN, PAIR), 0), iota((WIN * WIN, PAIR), 1)
    rows_differ = ((k_sub >> 5) & 1) != ((q_lane >> 6) & 1)
    cols_differ = (((k_sub >> 2) & 1) != ((q_lane >> 2) & 1)) & (((q_lane >> 3) & 1) == 1)
    tok = iota((1, TOK), 1) >> 4
    drop0 = (tok == 27) & last_row
    drop2 = (tok == 28) & last_row

    def forward(b, carry):
        x = nt(pad, xs[b])
        centred, inv1 = moments(x)
        normed1 = centred * inv1
        s_x[b] = normed1
        s_inv1[b] = inv1
        n1 = low(normed1 * gain1)
        s_n1[b] = n1
        packed[b] = low(nn(wqkvt[...], n1))
        col_flag = last_col & (b == NBLK - 1)

        def attend(a, carry):
            lanes = pl.ds(pl.multiple_of(a * PAIR, PAIR), PAIR)
            row_flag = last_row & (a == ROWS // WIN - 1)
            mask = jnp.where((rows_differ & row_flag) | (cols_differ & col_flag), -100.0, 0.0)
            for j in range(HEADS // 2):
                q = packed[b, 64 * j : 64 * j + 64, lanes]
                k = packed[b, CP + 64 * j : CP + 64 * j + 64, lanes]
                v = packed[b, 2 * CP + 64 * j : 2 * CP + 64 * j + 64, lanes]
                scores = tn(k, two_heads(q))
                wide = []
                for s in range(2):
                    sc = fold(scores[:, s * PAIR : (s + 1) * PAIR], second)
                    sc = sc * factor + bias[2 * j + s] + mask
                    e = jnp.exp(sc - jnp.max(sc, axis=0, keepdims=True))
                    p = e * (1.0 / jnp.sum(e, axis=0, keepdims=True))
                    probs[b, a, 2 * j + s] = p
                    wide.append(unfold(p, second))
                o = nn(v, jnp.concatenate(wide, axis=1))
                attended[b, 64 * j : 64 * j + 64, lanes] = low(own_heads(o))
            return carry

        lax.fori_loop(0, ROWS // WIN, attend, 0, unroll=True)

        middle = x + nn(wprojt[...], attended[b])
        centred2, inv2 = moments(middle)
        normed2 = centred2 * inv2
        s_norm2[b] = normed2
        s_inv2[b] = inv2
        n2 = low(normed2 * gain2)
        s_n2[b] = n2
        pre = nn(w1t[...], n2)
        cdf, pdf = gelu_parts(pre)
        hidden = low(pre * cdf)
        s_hidden[b] = hidden
        s_slope[b] = cdf + pre * pdf
        s_z[b] = low(middle + nn(w2t[...], hidden))
        return carry

    lax.fori_loop(0, NBLK, forward, 0)

    def back_to_heads(b, carry):
        z = s_z[b]
        z0 = jnp.where(drop0, 0.0, z.astype(F32)).astype(BF)
        z2 = jnp.where(drop2, 0.0, z.astype(F32)).astype(BF)
        total = jnp.zeros((CP, TOK), F32)
        for dy in range(3):
            part = jnp.zeros((CP, TOK), F32)
            zd = (z0, z, z2)[dy]
            for dx in range(3):
                source = gs[dx, b, (2 - dy) * BLK : (2 - dy) * BLK + TOK, :]
                part = part + nt(wcp[3 * dy + dx], source)
                a_conv[3 * dy + dx] += nn(zd, source)
            if dy == 0:
                part = jnp.where(drop0, 0.0, part)
            if dy == 2:
                part = jnp.where(drop2, 0.0, part)
            total = total + part
        d_shift = low(total)
        a_fc2[:, :FF] += nt(d_shift, s_hidden[b])
        d_pre = low(nn(w2p[...], d_shift) * s_slope[b])
        a_fc1[:, :FF] += nt(s_n2[b], d_pre)
        d_middle = d_shift.astype(F32) + norm_back(
            nn(w1p[...], d_pre), s_norm2[b], s_inv2[b], gain2
        )
        s_dmid[b] = d_middle
        d_attn = low(d_middle)
        a_proj[...] += nt(attended[b], d_attn)
        dheads[b] = low(nn(wprojp[...], d_attn))
        return carry

    lax.fori_loop(0, NBLK, back_to_heads, 0)

    steps = (
        (core_in0, held0, first0, second0, third0),
        (core_in1, held1, first1, second1, third1),
    )
    flying = [{}, {}]

    def rows(start, size):
        return pl.ds(pl.multiple_of(start, 16), size)

    def at_part(g, c, p):
        return BASE[g] + c * HALVES[g] + p * PARTS[g]

    def go_core(g):
        flying[g]["core"] = [
            copy(
                grads_ref.at[rows(at_part(g, 1 - core, p), PARTS[g])],
                steps[g][0].at[p],
                core_send.at[g, p],
                core_recv.at[g, p],
                sibling,
            )
            for p in range(3)
        ]

    def go_first(g):
        core_in, held, first = steps[g][:3]
        flying[g]["first"] = []
        for p in range(3):
            flying[g]["core"][p].wait_recv()
            own = grads_ref[rows(at_part(g, core, p), PARTS[g]), :].astype(F32)
            held[p] = low(own + core_in[p].astype(F32))
            group = []
            for k in range(1, SIDE):
                share = lax.rem(here[p] + k, SIDE)
                group.append(
                    copy(
                        held.at[p, rows(share * SHARES[g], SHARES[g])],
                        first.at[p, k - 1],
                        send.at[g, 0, p, k - 1],
                        recv.at[g, 0, p, k - 1],
                        along(p, k),
                    )
                )
            flying[g]["first"].append(group)

    def spread_out(g, p, step, source, target, axis):
        target[p, here[axis]] = source
        return [
            copy(
                target.at[p, here[axis]],
                target.at[p, here[axis]],
                send.at[g, step, p, k - 1],
                recv.at[g, step, p, k - 1],
                along(axis, k),
            )
            for k in range(1, SIDE)
        ]

    def gathered(copies, target, p):
        for c in copies:
            c.wait_recv()
        total = target[p, 0].astype(F32)
        for k in range(1, SIDE):
            total = total + target[p, k].astype(F32)
        return low(total)

    def go_second(g):
        held, first, second_in = steps[g][1:4]
        flying[g]["second"] = []
        for p in range(3):
            total = held[p, rows(here[p] * SHARES[g], SHARES[g]), :].astype(F32)
            for k in range(1, SIDE):
                flying[g]["first"][p][k - 1].wait_recv()
                total = total + first[p, k - 1].astype(F32)
            flying[g]["second"].append(
                spread_out(g, p, 1, low(total), second_in, (p + 1) % 3)
            )

    def go_third(g):
        second_in, third_in = steps[g][3:5]
        flying[g]["third"] = []
        for p in range(3):
            total = gathered(flying[g]["second"][p], second_in, p)
            flying[g]["third"].append(spread_out(g, p, 2, total, third_in, (p + 2) % 3))

    def go_back(g):
        flying[g]["back"] = []
        for p in range(3):
            at = rows(at_part(g, core, p) + here[p] * SHARES[g], SHARES[g])
            sum_ref[at, :] = gathered(flying[g]["third"][p], steps[g][4], p)
            flying[g]["back"].append(
                [
                    copy(
                        sum_ref.at[at],
                        sum_ref.at[at],
                        send.at[g, 3, p, k - 1],
                        recv.at[g, 3, p, k - 1],
                        along(p, k),
                    )
                    for k in range(1, SIDE)
                ]
            )

    def go_end(g):
        flying[g]["end"] = []
        for p in range(3):
            for c in flying[g]["back"][p]:
                c.wait_recv()
            at = rows(at_part(g, core, p), PARTS[g])
            flying[g]["end"].append(
                copy(
                    sum_ref.at[at],
                    sum_ref.at[at],
                    core_send.at[g, 3 + p],
                    core_recv.at[g, 3 + p],
                    sibling,
                )
            )

    def put(place, tile):
        grads_ref[place * CP : (place + 1) * CP, :] = low(tile)

    half_zero = jnp.zeros((CP, 64), F32)
    rests = []
    for t in range(9):
        put(t, a_conv[t, :, 0:128])
        rests.append(jnp.concatenate([a_conv[t, :, 128:C], half_zero[:, : 64 - (C - 128)]], axis=1))
    put(9, a_proj[:, 0:128])
    rests.append(a_proj[:, 128:192])
    for i in range(3):
        put(10 + i, a_fc2[:, i * 128 : (i + 1) * 128])
        put(13 + i, a_fc1[:, i * 128 : (i + 1) * 128])
    for i in range(5):
        put(16 + i, jnp.concatenate([rests[2 * i], rests[2 * i + 1]], axis=1))
    put(21, jnp.zeros((CP, 128), F32))
    go_core(0)

    def heads_back(b):
        def attend_back(a, carry):
            lanes = pl.ds(pl.multiple_of(a * PAIR, PAIR), PAIR)
            for j in range(HEADS // 2):
                q = packed[b, 64 * j : 64 * j + 64, lanes]
                k = packed[b, CP + 64 * j : CP + 64 * j + 64, lanes]
                v = packed[b, 2 * CP + 64 * j : 2 * CP + 64 * j + 64, lanes]
                do = dheads[b, 64 * j : 64 * j + 64, lanes]
                d_prob = tn(v, two_heads(do))
                p_wide, s_wide = [], []
                for s in range(2):
                    p = probs[b, a, 2 * j + s]
                    dp = fold(d_prob[:, s * PAIR : (s + 1) * PAIR], second)
                    ds = p * (dp - jnp.sum(p * dp, axis=0, keepdims=True)) * factor
                    p_wide.append(unfold(p, second))
                    s_wide.append(unfold(ds, second))
                dv = nt(do, jnp.concatenate(p_wide, axis=0))
                dq = nn(k, jnp.concatenate(s_wide, axis=1))
                dk = nt(q, jnp.concatenate(s_wide, axis=0))
                dpacked[b, 64 * j : 64 * j + 64, lanes] = low(own_heads(dq))
                dpacked[b, CP + 64 * j : CP + 64 * j + 64, lanes] = low(own_heads(dk))
                dpacked[b, 2 * CP + 64 * j : 2 * CP + 64 * j + 64, lanes] = low(own_heads(dv))
            return carry

        lax.fori_loop(0, ROWS // WIN, attend_back, 0, unroll=True)
        a_qkv[...] += nt(s_n1[b], dpacked[b])

    heads_back(0)
    go_first(0)
    heads_back(1)
    go_second(0)
    heads_back(2)
    go_third(0)
    heads_back(3)
    for i in range(4):
        put(22 + i, a_qkv[:, i * 128 : (i + 1) * 128])
    put(26, jnp.concatenate([a_qkv[:, 512:576], half_zero], axis=1))
    put(27, jnp.zeros((CP, 128), F32))
    go_core(1)
    go_back(0)

    ones_pair = eye(PAIR, PAIR)

    def inputs_back(b):
        d_in = s_dmid[b] + norm_back(nn(wqkvp[...], dpacked[b]), s_x[b], s_inv1[b], gain1)
        d_low = low(d_in)
        for a in range(ROWS // WIN):
            natural = nt(ones_pair, d_low[:, a * PAIR : (a + 1) * PAIR])
            d_ref[b, a * PAIR : (a + 1) * PAIR, :] = low(natural[:, :C])

    inputs_back(NBLK - 1)
    go_first(1)
    edge = d_ref[NBLK - 1].astype(F32).reshape(ROWS, 2, 8, C)[:, 1]
    strip_out[...] = low(edge.reshape(ROWS * 8, C))
    leaving = [
        copy(strip_out.at[224:256], hc_ref, out_send.at[2], out_recv.at[2], (down, right)),
        copy(strip_out, hs_ref, out_send.at[1], out_recv.at[1], (row, right)),
    ]
    inputs_back(0)
    inputs_back(1)
    go_second(1)
    inputs_back(2)
    leaving.append(
        copy(d_ref.at[:, 448:512, :], hr_ref, out_send.at[0], out_recv.at[0], (down, col))
    )
    go_end(0)
    go_third(1)
    go_back(1)
    go_end(1)
    for c in flying[0]["end"] + flying[1]["end"] + leaving:
        c.wait_recv()
    for c in started:
        c.wait_send()


def call_layer(features, cotangent, w_qkv, w_proj, w_fc1, w_fc2_t, w_conv, g1, g2, table):
    blocks = ROWS // WIN
    reductions = []
    for sizes in (
        (3, PARTS),
        (3, PARTS),
        ((3, SIDE - 1), SHARES),
        ((3, SIDE), SHARES),
        ((3, SIDE), SHARES),
    ):
        lead, lengths = sizes
        lead = lead if isinstance(lead, tuple) else (lead,)
        reductions += [VMEM((*lead, n, 128), BF) for n in lengths]
    scratch = [
        VMEM((4, COLS, C), BF),
        VMEM((5, COLS, C), BF),
        VMEM((288, C), BF),
        VMEM((80, C), BF),
        VMEM((288, C), BF),
        VMEM((256, C), BF),
        VMEM((GROWS, 128), BF),
        *reductions,
        VMEM((NBLK, TOK, C), BF),
        VMEM((3, NBLK, (ROWS + 2) * BLK, C), BF),
        VMEM((3 * CP, CP), BF),
        VMEM((CP, 3 * CP), BF),
        VMEM((CP, CP), BF),
        VMEM((CP, CP), BF),
        VMEM((FF, CP), BF),
        VMEM((CP, FF), BF),
        VMEM((CP, FF), BF),
        VMEM((FF, CP), BF),
        VMEM((9, CP, C), BF),
        VMEM((HEADS, WIN * WIN, PAIR), F32),
        VMEM((NBLK, CP, TOK), F32),
        VMEM((NBLK, 1, TOK), F32),
        VMEM((NBLK, CP, TOK), BF),
        VMEM((NBLK, 3 * CP, TOK), BF),
        VMEM((NBLK, CP, TOK), BF),
        VMEM((NBLK, blocks, HEADS, WIN * WIN, PAIR), F32),
        VMEM((NBLK, CP, TOK), F32),
        VMEM((NBLK, 1, TOK), F32),
        VMEM((NBLK, CP, TOK), BF),
        VMEM((NBLK, FF, TOK), F32),
        VMEM((NBLK, FF, TOK), BF),
        VMEM((NBLK, CP, TOK), BF),
        VMEM((NBLK, CP, TOK), BF),
        VMEM((NBLK, 3 * CP, TOK), BF),
        VMEM((NBLK, CP, TOK), F32),
        VMEM((9, CP, C), F32),
        VMEM((CP, CP), F32),
        VMEM((CP, 384), F32),
        VMEM((CP, 384), F32),
        VMEM((CP, 3 * CP), F32),
        pltpu.SemaphoreType.DMA((4,)),
        pltpu.SemaphoreType.DMA((4,)),
        pltpu.SemaphoreType.DMA((3,)),
        pltpu.SemaphoreType.DMA((3,)),
        pltpu.SemaphoreType.DMA((2, 6)),
        pltpu.SemaphoreType.DMA((2, 6)),
        pltpu.SemaphoreType.DMA((2, 4, 3, SIDE - 1)),
        pltpu.SemaphoreType.DMA((2, 4, 3, SIDE - 1)),
    ]
    return pl.pallas_call(
        layer,
        out_shape=(
            jax.ShapeDtypeStruct((NBLK, TOK, C), BF),
            jax.ShapeDtypeStruct((GROWS, 128), BF),
            jax.ShapeDtypeStruct((NBLK, 64, C), BF),
            jax.ShapeDtypeStruct((256, C), BF),
            jax.ShapeDtypeStruct((32, C), BF),
        ),
        in_specs=[pl.BlockSpec(memory_space=VMEM)] * 10,
        out_specs=[pl.BlockSpec(memory_space=VMEM)] * 5,
        scratch_shapes=scratch,
        compiler_params=pltpu.CompilerParams(
            collective_id=0, has_side_effects=True, vmem_limit_bytes=60 * 2**20
        ),
        name="layer",
    )(features, cotangent, w_qkv, w_proj, w_fc1, w_fc2_t, w_conv, g1, g2, table)


def results(
    d_ref, hr_ref, hs_ref, hc_ref, sum_ref, out_ref, qkv_ref, proj_ref, fc1_ref, fc2_ref, conv_ref
):
    sub = iota((8, C), 0)
    extras = hs_ref[...].astype(F32).reshape(ROWS, 8, C)
    corners = hc_ref[...].astype(F32).reshape(4, 8, C)
    for i in range(ROWS):
        if i < 4:
            pieces = [hr_ref[b, i * BLK : (i + 1) * BLK, :] for b in range(NBLK)]
            extra = corners[i]
        else:
            pieces = [d_ref[b, (i - 4) * BLK : (i - 3) * BLK, :] for b in range(NBLK)]
            extra = extras[i - 4]
        v = pltpu.roll(jnp.concatenate(pieces, axis=0).astype(F32), 4, 0)
        head = jnp.where(sub < 4, pltpu.roll(extra, 4, 0), v[:8])
        out_ref[i] = low(jnp.concatenate([head, v[8:]], axis=0))

    scale = 1.0 / math.sqrt(ROWS * COLS * lax.axis_size("row") * lax.axis_size("col"))

    def full(i):
        return sum_ref[i * CP : (i + 1) * CP, :]

    def rest(i):
        return full(16 + i // 2)[:, 64 * (i % 2) : 64 * (i % 2) + 64]

    def square(i, r):
        return jnp.concatenate([full(i), rest(r)], axis=1)

    for t in range(9):
        conv_ref[t] = square(t, t).astype(F32)[:C, :C] * scale
    proj_ref[...] = nn(spread(CP, C, 1), square(9, 9))[:, :C] * scale
    fc2 = jnp.concatenate([full(10), full(11), full(12)], axis=1).astype(F32)
    fc2_ref[...] = fc2[:C, :FF] * scale
    fc1 = jnp.concatenate([full(13), full(14), full(15)], axis=1).astype(F32)
    fc1_ref[...] = fc1[:C, :FF] * scale
    qkv = jnp.concatenate([full(22), full(23), full(24), full(25), full(26)[:, :64]], axis=1)
    qkv_ref[...] = nn(qkv, spread(3 * CP, 3 * C, 0))[:C] * scale


def call_results(d_shifted, halo, sums):
    return pl.pallas_call(
        results,
        out_shape=(
            jax.ShapeDtypeStruct((ROWS, COLS, C), BF),
            jax.ShapeDtypeStruct((C, 3 * C), F32),
            jax.ShapeDtypeStruct((C, C), F32),
            jax.ShapeDtypeStruct((C, FF), F32),
            jax.ShapeDtypeStruct((C, FF), F32),
            jax.ShapeDtypeStruct((9, C, C), F32),
        ),
        in_specs=[pl.BlockSpec(memory_space=VMEM)] * 5,
        out_specs=[pl.BlockSpec(memory_space=VMEM)] * 6,
        compiler_params=pltpu.CompilerParams(vmem_limit_bytes=32 * 2**20),
        name="results",
    )(d_shifted, *halo, sums)


def local(features, cotangent, w_qkv, w_proj, w_fc1, w_fc2, w_conv, gain_attn, gain_mlp, pos_table):
    d_shifted, sums, *halo = call_layer(
        features,
        cotangent,
        w_qkv,
        w_proj,
        w_fc1,
        w_fc2.T,
        w_conv,
        gain_attn.reshape(1, C),
        gain_mlp.reshape(1, C),
        pos_table.T,
    )
    d_features, qkv, proj, fc1, fc2, conv = call_results(d_shifted, halo, sums)
    return d_features, qkv, proj, fc1, fc2.T, conv


def solution(mesh):
    return jax.shard_map(
        local,
        mesh=mesh,
        in_specs=(P("row", "col", None), P("row", "col", None)) + (P(),) * 8,
        out_specs=(P("row", "col", None),) + (P(),) * 5,
        check_vma=False,
    )
```

```python
import math

import jax
import jax.numpy as jnp
from jax import lax
from jax.experimental import pallas as pl
from jax.experimental.pallas import tpu as pltpu
from jax.sharding import PartitionSpec as P

C = 180
CP = 192
HEADS = 6
HD = 30
HP = 32
FF = 360
WIN = 8
SHIFT = 4
ROWS = 32
COLS = 64
BLK = 16
NBLK = COLS // BLK
TOK = ROWS * BLK
PAIR = WIN * BLK
SIDE = 4
TILES = (14, 12)
BASE = (0, TILES[0] * CP)
GROWS = sum(TILES) * CP
HALVES = tuple(t * CP // 2 for t in TILES)
PARTS = tuple(h // 3 for h in HALVES)
SHARES = tuple(p // SIDE for p in PARTS)
BF = jnp.bfloat16
F32 = jnp.float32
MESH = pl.DeviceIdType.MESH
VMEM = pltpu.VMEM


def iota(shape, dim):
    return lax.broadcasted_iota(jnp.int32, shape, dim)


def nn(a, b):
    return lax.dot_general(a, b, (((1,), (0,)), ((), ())), preferred_element_type=F32)


def nt(a, b):
    return lax.dot_general(a, b, (((1,), (1,)), ((), ())), preferred_element_type=F32)


def low(a):
    return a.astype(BF)


def eye(rows, cols):
    return low(jnp.where(iota((rows, cols), 0) == iota((rows, cols), 1), 1.0, 0.0))


def spread(padded, plain, pad_dim):
    shape = (padded, plain) if pad_dim == 0 else (plain, padded)
    p = iota(shape, pad_dim)
    c = iota(shape, 1 - pad_dim)
    hit = ((p & (HP - 1)) < HD) & (c == (p >> 5) * HD + (p & (HP - 1)))
    return low(jnp.where(hit, 1.0, 0.0))


def column(gain_ref):
    wide = jnp.where(iota((CP, C), 0) == iota((CP, C), 1), gain_ref[...], 0.0)
    return jnp.sum(wide, axis=1, keepdims=True)


def moments(values):
    mean = jnp.sum(values[:C], axis=0, keepdims=True) * (1.0 / C)
    centred = values - mean
    inner = centred[:C]
    var = jnp.sum(inner * inner, axis=0, keepdims=True) * (1.0 / C)
    return centred, lax.rsqrt(var + 1e-05)


def norm_back(upstream, normed, inverse, gain):
    scaled = upstream * gain
    first = jnp.sum(scaled, axis=0, keepdims=True) * (1.0 / C)
    second = jnp.sum(scaled * normed, axis=0, keepdims=True) * (1.0 / C)
    return inverse * (scaled - first - normed * second)


def gelu_parts(x):
    u = jnp.abs(x) * math.sqrt(0.5)
    t = 1.0 / (1.0 + 0.3275911 * u)
    e = jnp.exp(-u * u)
    poly = t * (
        0.254829592
        + t * (-0.284496736 + t * (1.421413741 + t * (-1.453152027 + t * 1.061405429)))
    )
    tail = 0.5 * poly * e
    cdf = jnp.where(x >= 0.0, 1.0 - tail, tail)
    return cdf, e * (1.0 / math.sqrt(2.0 * math.pi))


def fold(scores, second):
    parts = scores.reshape(WIN, 2, WIN, PAIR)
    return jnp.where(second, parts[:, 1], parts[:, 0]).reshape(WIN * WIN, PAIR)


def unfold(probs, second):
    parts = probs.reshape(WIN, WIN, PAIR)
    zero = jnp.zeros_like(parts)
    both = jnp.stack([jnp.where(second, zero, parts), jnp.where(second, parts, zero)], axis=1)
    return low(both.reshape(PAIR, PAIR))


def two_heads(block):
    zero = jnp.zeros((HP, PAIR), BF)
    top = jnp.concatenate([block[:HP], zero], axis=1)
    return jnp.concatenate([top, jnp.concatenate([zero, block[HP:]], axis=1)], axis=0)


def own_heads(product):
    return jnp.concatenate([product[:HP, :PAIR], product[HP:, PAIR:]], axis=0)


def tn(a, b):
    return lax.dot_general(a, b, (((0,), (0,)), ((), ())), preferred_element_type=F32)


def layer(
    f_hbm, g_hbm, wqkv_hbm, wproj_hbm, w1_hbm, w2_hbm, wconv_hbm, g1_hbm, g2_hbm, pos_hbm,
    d_hbm, sum_hbm, hr_ref, hs_ref, hc_ref,
    f_ref, g_ref, wqkv_ref, wproj_ref, w1_ref, w2_ref, wconv_ref, g1_ref, g2_ref, pos_ref,
    d_ref, sum_ref,
    fr_ref, gr_ref, fstrip_ref, gstrip_ref, fcorner_ref, gcorner_ref,
    fstrip_in, gstrip_in, strip_out,
    grads_ref, core_in0, core_in1, held0, held1, first0, first1, second0, second1, third0, third1,
    xs, gs, wqkvt, wqkvp, wprojt, wprojp, w1t, w1p, w2t, w2p, bias,
    s_norm1, s_inv1, s_n1, packed, attended, probs, s_norm2, s_inv2, s_n2, s_slope, s_hidden, s_z,
    dshift, s_dpre, s_dattn, dheads, dpacked, s_dmid,
    load, store, in_send, in_recv, out_send, out_recv, core_send, core_recv, send, recv,
):
    row, col = lax.axis_index("row"), lax.axis_index("col")
    n_row, n_col = lax.axis_size("row"), lax.axis_size("col")
    up, down = lax.rem(row + n_row - 1, n_row), lax.rem(row + 1, n_row)
    left, right = lax.rem(col + n_col - 1, n_col), lax.rem(col + 1, n_col)
    last_row, last_col = row == n_row - 1, col == n_col - 1
    factor = HD**-0.5
    core, z, y = lax.rem(row, 2), lax.rem(row // 2, SIDE), lax.rem(col, SIDE)
    x = (row // 8) * 2 + col // SIDE
    here = (x, y, z)

    def device(xyz, c):
        return ((xyz[0] // 2) * 8 + xyz[2] * 2 + c, lax.rem(xyz[0], 2) * SIDE + xyz[1])

    def along(axis, k):
        there = list(here)
        there[axis] = lax.rem(there[axis] + k, SIDE)
        return device(there, core)

    sibling = device(here, 1 - core)
    barrier = pltpu.get_barrier_semaphore()
    greeted = [sibling, (up, col), (row, left), (up, left), (down, col), (row, right)]
    greeted += [(down, right)] + [along(axis, k) for axis in range(3) for k in range(1, SIDE)]
    for peer in greeted:
        pl.semaphore_signal(barrier, inc=1, device_id=peer, device_id_type=MESH)

    hbm = (f_hbm, g_hbm, wqkv_hbm, wproj_hbm, w1_hbm, w2_hbm, wconv_hbm, g1_hbm, g2_hbm, pos_hbm)
    own = (f_ref, g_ref, wqkv_ref, wproj_ref, w1_ref, w2_ref, wconv_ref, g1_ref, g2_ref, pos_ref)
    loads = [pltpu.make_async_copy(s, t, load.at[i]) for i, (s, t) in enumerate(zip(hbm, own))]
    for c in loads:
        c.start()
    started = []

    def copy(src, dst, s, r, peer):
        c = pltpu.make_async_remote_copy(
            src_ref=src, dst_ref=dst, send_sem=s, recv_sem=r, device_id=peer, device_id_type=MESH
        )
        c.start()
        started.append(c)
        return c

    loads[0].wait()
    fs = f_ref[:, 0:16, :].astype(F32)[:, 0:8, :].reshape(ROWS // 2, 2, 8, C)
    pairs = jnp.where(iota((ROWS // 2, 8, C), 1) < 4, fs[:, 0], pltpu.roll(fs[:, 1], 4, 1))
    fstrip_in[...] = low(pairs.reshape(ROWS * 4, C))
    pl.semaphore_wait(barrier, len(greeted))
    f_arriving = [
        copy(fstrip_in.at[0:16], fcorner_ref, in_send.at[0], in_recv.at[0], (up, left)),
        copy(fstrip_in, fstrip_ref, in_send.at[1], in_recv.at[1], (row, left)),
        copy(f_ref.at[0:4], fr_ref, in_send.at[2], in_recv.at[2], (up, col)),
    ]
    loads[1].wait()
    cs = g_ref[:, 0:16, :].astype(F32)[:, 0:8, :]
    gstrip_in[...] = low(cs.reshape(ROWS * 8, C))
    g_arriving = [
        copy(gstrip_in.at[0:48], gcorner_ref, in_send.at[3], in_recv.at[3], (up, left)),
        copy(gstrip_in, gstrip_ref, in_send.at[4], in_recv.at[4], (row, left)),
        copy(g_ref.at[0:5], gr_ref, in_send.at[5], in_recv.at[5], (up, col)),
    ]

    sub = iota((8, C), 0)
    keep0 = jnp.where((sub == 3) & last_col, 0.0, 1.0)
    keep2 = jnp.where((sub == 4) & last_col, 0.0, 1.0)
    LASTB = NBLK - 1

    def put(target, i, rolled):
        whole = low(rolled[: LASTB * BLK])
        for b in range(LASTB):
            target[b, i * BLK : (i + 1) * BLK, :] = whole[b * BLK : (b + 1) * BLK]

    def put_last(target, i, body, last):
        target[LASTB, i * BLK : (i + 1) * BLK, :] = low(jnp.concatenate([body, last], axis=0))

    def put_x(i, v):
        put(xs, i, pltpu.roll(v, 60, 0))

    def put_x_last(i, v, extra):
        r = pltpu.roll(v, 12, 0)
        put_last(xs, i, r[:8], jnp.where(sub < 4, r[8:], extra))

    def put_g(i, v):
        for k, turn in enumerate((59, 60, 61)):
            put(gs.at[k], i, pltpu.roll(v, turn, 0))

    def put_g_last(i, v, extra):
        for k, n in enumerate((5, 4, 3)):
            r = pltpu.roll(v, 16 - n, 0)
            last = jnp.where(sub < 8 - n, r[8:], pltpu.roll(extra, 8 - n, 0))
            if k != 1:
                last = last * (keep0, keep2)[k // 2]
            put_last(gs.at[k], i, r[:8], last)

    for i in range(ROWS - 4):
        put_x(i, f_ref[i + 4].astype(F32))
    for i in range(ROWS - 3):
        put_g(i, g_ref[i + 3].astype(F32))

    for c in loads[2:]:
        c.wait()
    pad = eye(CP, C)
    sel, sel_one = spread(3 * CP, 3 * C, 0), spread(CP, C, 0)
    wq = low(nn(pad, wqkv_ref[...]))
    wqkvt[...] = low(nt(sel, wq))
    wqkvp[...] = low(nt(wq, sel))
    turned = low(nt(pad, wproj_ref[...]))
    wprojt[...] = low(nt(turned, sel_one))
    wprojp[...] = low(nt(sel_one, turned))
    w1p[...] = low(nn(pad, w1_ref[...]))
    w1t[...] = low(nt(eye(FF, FF), w1p[...]))
    w2t[...] = low(nn(pad, w2_ref[...]))
    w2p[...] = low(nt(eye(FF, FF), w2t[...]))
    gain1, gain2 = column(g1_ref), column(g2_ref)

    table = pos_ref[...]
    high = low(table)
    mid = low(table - high.astype(F32))
    rest_piece = low(table - high.astype(F32) - mid.astype(F32))
    entry, place = iota((225, 15 * BLK), 0), iota((225, 15 * BLK), 1)
    for kc in range(WIN):
        hit = entry == (place >> 4) * 15 + (place & 7) - kc + 7
        pick = low(jnp.where(hit, 1.0, 0.0))
        line = nn(high, pick) + nn(mid, pick) + nn(rest_piece, pick)
        for h in range(HEADS):
            for kr in range(WIN):
                start = (WIN - 1 - kr) * BLK
                at = kr * WIN + kc
                bias[h, at : at + 1, :] = line[h : h + 1, start : start + PAIR]
    dshift[...] = jnp.zeros_like(dshift)

    for c in f_arriving:
        c.wait_recv()
    quads = fstrip_ref[...].astype(F32).reshape(ROWS // 2, 8, C)
    corner = fcorner_ref[...].astype(F32).reshape(2, 8, C)

    def quad(source, i):
        return pltpu.roll(source[i // 2], 4, 0) if i % 2 == 0 else source[i // 2]

    for i in range(ROWS):
        if i < ROWS - 4:
            put_x_last(i, f_ref[i + 4, COLS - 16 :, :].astype(F32), quad(quads, i + 4))
        else:
            put_x(i, fr_ref[i - 28].astype(F32))
            put_x_last(i, fr_ref[i - 28, COLS - 16 :, :].astype(F32), quad(corner, i - 28))

    lane = iota((1, PAIR), 1)
    second = ((lane >> 3) & 1) == 1
    k_sub, q_lane = iota((WIN * WIN, PAIR), 0), iota((WIN * WIN, PAIR), 1)
    rows_differ = ((k_sub >> 5) & 1) != ((q_lane >> 6) & 1)
    cols_differ = (((k_sub >> 2) & 1) != ((q_lane >> 2) & 1)) & (((q_lane >> 3) & 1) == 1)
    tok = iota((1, TOK), 1) >> 4
    drop0 = (tok == 27) & last_row
    drop2 = (tok == 28) & last_row

    def forward(b, carry):
        x = nt(pad, xs[b])
        centred, inv1 = moments(x)
        normed1 = centred * inv1
        s_norm1[b] = normed1
        s_inv1[b] = inv1
        n1 = low(normed1 * gain1)
        s_n1[b] = n1
        packed[b] = low(nn(wqkvt[...], n1))
        col_flag = last_col & (b == NBLK - 1)

        units = [(a, j) for a in range(ROWS // WIN) for j in range(HEADS // 2)]
        scores = {}
        for a, j in units:
            lanes = slice(a * PAIR, (a + 1) * PAIR)
            q = packed[b, 64 * j : 64 * j + 64, lanes]
            k = packed[b, CP + 64 * j : CP + 64 * j + 64, lanes]
            scores[a, j] = tn(k, two_heads(q))
        soft = {}
        for a, j in units:
            row_flag = last_row & (a == ROWS // WIN - 1)
            mask = jnp.where((rows_differ & row_flag) | (cols_differ & col_flag), -100.0, 0.0)
            wide = []
            for s in range(2):
                sc = fold(scores[a, j][:, s * PAIR : (s + 1) * PAIR], second)
                sc = sc * factor + bias[2 * j + s] + mask
                e = jnp.exp(sc - jnp.max(sc, axis=0, keepdims=True))
                p = e * (1.0 / jnp.sum(e, axis=0, keepdims=True))
                probs[b, a, 2 * j + s] = p
                wide.append(unfold(p, second))
            soft[a, j] = jnp.concatenate(wide, axis=1)
        for a, j in units:
            lanes = slice(a * PAIR, (a + 1) * PAIR)
            v = packed[b, 2 * CP + 64 * j : 2 * CP + 64 * j + 64, lanes]
            attended[b, 64 * j : 64 * j + 64, lanes] = low(own_heads(nn(v, soft[a, j])))

        middle = x + nn(wprojt[...], attended[b])
        centred2, inv2 = moments(middle)
        normed2 = centred2 * inv2
        s_norm2[b] = normed2
        s_inv2[b] = inv2
        n2 = low(normed2 * gain2)
        s_n2[b] = n2
        pre = nn(w1t[...], n2)
        cdf, pdf = gelu_parts(pre)
        hidden = low(pre * cdf)
        s_hidden[b] = hidden
        s_slope[b] = cdf + pre * pdf
        z = middle + nn(w2t[...], hidden)
        s_z[1, b] = low(z)
        s_z[0, b] = low(jnp.where(drop0, 0.0, z))
        s_z[2, b] = low(jnp.where(drop2, 0.0, z))
        return carry

    lax.fori_loop(0, NBLK, forward, 0)

    for c in g_arriving:
        c.wait_recv()
    for i in range(ROWS + 2):
        if i < ROWS - 3:
            extra = gstrip_ref[(i + 3) * 8 : (i + 4) * 8, :]
            put_g_last(i, g_ref[i + 3, COLS - 16 :, :].astype(F32), extra.astype(F32))
        else:
            k = i - ROWS + 3
            put_g(i, gr_ref[k].astype(F32))
            extra = gcorner_ref[k * 8 : (k + 1) * 8, :]
            put_g_last(i, gr_ref[k, COLS - 16 :, :].astype(F32), extra.astype(F32))

    def tap(b, dy, dx):
        return gs[dx, b, (2 - dy) * BLK : (2 - dy) * BLK + TOK, :]

    def over_blocks(term):
        total = term(0)
        for b in range(1, NBLK):
            total = total + term(b)
        return total

    def put_tile(place, tile):
        grads_ref[place * CP : (place + 1) * CP, :] = low(tile)

    def put_pair(place, left, right):
        put_tile(place, jnp.concatenate([left, right], axis=1))

    held_back = None
    for t in range(9):
        total = over_blocks(lambda b: nn(s_z[t // 3, b], tap(b, t // 3, t % 3)))
        put_tile(t, total[:, :128])
        narrow = jnp.concatenate([total[:, 128:], jnp.zeros((CP, 256 - 12 - C), F32)], axis=1)
        narrow = narrow[:, :64]
        if t % 2 == 0:
            held_back = narrow
        else:
            put_pair(9 + t // 2, held_back, narrow)
    put_pair(13, held_back, jnp.zeros((CP, 64), F32))
    steps = (
        (core_in0, held0, first0, second0, third0),
        (core_in1, held1, first1, second1, third1),
    )
    flying = [{}, {}]

    def rows(start, size):
        return pl.ds(pl.multiple_of(start, 16), size)

    def at_part(g, c, p):
        return BASE[g] + c * HALVES[g] + p * PARTS[g]

    def go_core(g):
        flying[g]["core"] = [
            copy(
                grads_ref.at[rows(at_part(g, 1 - core, p), PARTS[g])],
                steps[g][0].at[p],
                core_send.at[g, p],
                core_recv.at[g, p],
                sibling,
            )
            for p in range(3)
        ]

    def go_first(g):
        core_in, held, first = steps[g][:3]
        flying[g]["first"] = []
        for p in range(3):
            flying[g]["core"][p].wait_recv()
            own = grads_ref[rows(at_part(g, core, p), PARTS[g]), :].astype(F32)
            held[p] = low(own + core_in[p].astype(F32))
            group = []
            for k in range(1, SIDE):
                share = lax.rem(here[p] + k, SIDE)
                group.append(
                    copy(
                        held.at[p, rows(share * SHARES[g], SHARES[g])],
                        first.at[p, k - 1],
                        send.at[g, 0, p, k - 1],
                        recv.at[g, 0, p, k - 1],
                        along(p, k),
                    )
                )
            flying[g]["first"].append(group)

    def spread_out(g, p, step, source, target, axis):
        target[p, here[axis]] = source
        return [
            copy(
                target.at[p, here[axis]],
                target.at[p, here[axis]],
                send.at[g, step, p, k - 1],
                recv.at[g, step, p, k - 1],
                along(axis, k),
            )
            for k in range(1, SIDE)
        ]

    def gathered(copies, target, p):
        for c in copies:
            c.wait_recv()
        total = target[p, 0].astype(F32)
        for k in range(1, SIDE):
            total = total + target[p, k].astype(F32)
        return low(total)

    def go_second(g):
        held, first, second_in = steps[g][1:4]
        flying[g]["second"] = []
        for p in range(3):
            total = held[p, rows(here[p] * SHARES[g], SHARES[g]), :].astype(F32)
            for k in range(1, SIDE):
                flying[g]["first"][p][k - 1].wait_recv()
                total = total + first[p, k - 1].astype(F32)
            flying[g]["second"].append(
                spread_out(g, p, 1, low(total), second_in, (p + 1) % 3)
            )

    def go_third(g):
        second_in, third_in = steps[g][3:5]
        flying[g]["third"] = []
        for p in range(3):
            total = gathered(flying[g]["second"][p], second_in, p)
            flying[g]["third"].append(spread_out(g, p, 2, total, third_in, (p + 2) % 3))

    def go_back(g):
        flying[g]["back"] = []
        for p in range(3):
            at = rows(at_part(g, core, p) + here[p] * SHARES[g], SHARES[g])
            sum_ref[at, :] = gathered(flying[g]["third"][p], steps[g][4], p)
            flying[g]["back"].append(
                [
                    copy(
                        sum_ref.at[at],
                        sum_ref.at[at],
                        send.at[g, 3, p, k - 1],
                        recv.at[g, 3, p, k - 1],
                        along(p, k),
                    )
                    for k in range(1, SIDE)
                ]
            )

    def go_end(g):
        flying[g]["end"] = []
        for p in range(3):
            for c in flying[g]["back"][p]:
                c.wait_recv()
            at = rows(at_part(g, core, p), PARTS[g])
            flying[g]["end"].append(
                copy(
                    sum_ref.at[at],
                    sum_ref.at[at],
                    core_send.at[g, 3 + p],
                    core_recv.at[g, 3 + p],
                    sibling,
                )
            )

    go_core(0)

    def conv_back(b, carry):
        total = None
        for dy in range(3):
            part = None
            for dx in range(3):
                product = nt(wconv_ref[3 * dy + dx], tap(b, dy, dx))
                part = product if part is None else part + product
            if dy != 1:
                part = jnp.where((drop0, drop2)[dy // 2], 0.0, part)
            total = part if total is None else total + part
        dshift[b, :C, :] = low(total)
        return carry

    def back_to_heads(b, carry):
        d_shift = dshift[b]
        d_pre = low(nn(w2p[...], d_shift) * s_slope[b])
        s_dpre[b] = d_pre
        d_middle = d_shift.astype(F32) + norm_back(
            nn(w1p[...], d_pre), s_norm2[b], s_inv2[b], gain2
        )
        s_dmid[b] = d_middle
        d_attn = low(d_middle)
        s_dattn[b] = d_attn
        dheads[b] = low(nn(wprojp[...], d_attn))
        return carry

    lax.fori_loop(0, NBLK, conv_back, 0)
    go_first(0)
    lax.fori_loop(0, NBLK, back_to_heads, 0)

    fc2 = over_blocks(lambda b: nt(dshift[b], s_hidden[b]))
    fc1 = over_blocks(lambda b: nt(s_n2[b], s_dpre[b]))
    for place, total in ((14, fc2), (17, fc1)):
        put_tile(place, total[:, :128])
        put_tile(place + 1, total[:, 128:256])
        put_pair(place + 2, total[:, 256:], jnp.zeros((CP, 384 - FF), F32))
    proj = over_blocks(lambda b: nt(attended[b], s_dattn[b]))
    put_tile(20, proj[:, :128])

    def heads_back(b):
        units = [(a, j) for a in range(ROWS // WIN) for j in range(HEADS // 2)]

        def part(ref, third, a, j):
            top = third * CP + 64 * j
            return ref[b, top : top + 64, a * PAIR : (a + 1) * PAIR]

        d_probs = {}
        for a, j in units:
            d_probs[a, j] = tn(part(packed, 2, a, j), two_heads(part(dheads, 0, a, j)))
        p_all, s_all = {}, {}
        for a, j in units:
            p_wide, s_wide = [], []
            for s in range(2):
                p = probs[b, a, 2 * j + s]
                dp = fold(d_probs[a, j][:, s * PAIR : (s + 1) * PAIR], second)
                ds = p * (dp - jnp.sum(p * dp, axis=0, keepdims=True)) * factor
                p_wide.append(unfold(p, second))
                s_wide.append(unfold(ds, second))
            p_all[a, j], s_all[a, j] = p_wide, s_wide
        for a, j in units:
            lanes = slice(a * PAIR, (a + 1) * PAIR)
            dv = nt(part(dheads, 0, a, j), jnp.concatenate(p_all[a, j], axis=0))
            dq = nn(part(packed, 1, a, j), jnp.concatenate(s_all[a, j], axis=1))
            dk = nt(part(packed, 0, a, j), jnp.concatenate(s_all[a, j], axis=0))
            dpacked[b, 64 * j : 64 * j + 64, lanes] = low(own_heads(dq))
            dpacked[b, CP + 64 * j : CP + 64 * j + 64, lanes] = low(own_heads(dk))
            dpacked[b, 2 * CP + 64 * j : 2 * CP + 64 * j + 64, lanes] = low(own_heads(dv))

    heads_back(0)
    heads_back(1)
    go_second(0)
    heads_back(2)
    heads_back(3)
    qkv = over_blocks(lambda b: nt(s_n1[b], dpacked[b]))
    for i in range(4):
        put_tile(21 + i, qkv[:, i * 128 : (i + 1) * 128])
    put_pair(25, proj[:, 128:192], qkv[:, 512:576])
    go_core(1)

    ones_pair = eye(PAIR, PAIR)

    def inputs_back(b):
        d_in = s_dmid[b] + norm_back(nn(wqkvp[...], dpacked[b]), s_norm1[b], s_inv1[b], gain1)
        d_low = low(d_in)
        for a in range(ROWS // WIN):
            natural = nt(ones_pair, d_low[:, a * PAIR : (a + 1) * PAIR])
            d_ref[b, a * PAIR : (a + 1) * PAIR, :] = low(natural[:, :C])

    inputs_back(NBLK - 1)
    go_first(1)
    edge = d_ref[NBLK - 1].astype(F32).reshape(ROWS, 2, 8, C)[:, 1]
    strip_out[...] = low(edge.reshape(ROWS * 8, C))
    leaving = [
        copy(strip_out.at[224:256], hc_ref, out_send.at[2], out_recv.at[2], (down, right)),
        copy(strip_out, hs_ref, out_send.at[1], out_recv.at[1], (row, right)),
    ]
    inputs_back(0)
    inputs_back(1)
    inputs_back(2)
    leaving.append(
        copy(d_ref.at[:, 448:512, :], hr_ref, out_send.at[0], out_recv.at[0], (down, col))
    )
    stores = [pltpu.make_async_copy(d_ref, d_hbm, store.at[0])]
    stores[0].start()
    go_third(0)
    go_second(1)
    go_back(0)
    go_third(1)
    go_end(0)
    go_back(1)

    def keep(g):
        for c in flying[g]["end"]:
            c.wait_recv()
        at = slice(BASE[g], BASE[g] + TILES[g] * CP)
        stores.append(pltpu.make_async_copy(sum_ref.at[at], sum_hbm.at[at], store.at[1 + g]))
        stores[-1].start()

    keep(0)
    go_end(1)
    keep(1)
    for c in leaving:
        c.wait_recv()
    for c in started:
        c.wait_send()
    for c in stores:
        c.wait()


def call_layer(features, cotangent, w_qkv, w_proj, w_fc1, w_fc2_t, w_conv, g1, g2, table):
    blocks = ROWS // WIN
    reductions = []
    for sizes in (
        (3, PARTS),
        (3, PARTS),
        ((3, SIDE - 1), SHARES),
        ((3, SIDE), SHARES),
        ((3, SIDE), SHARES),
    ):
        lead, lengths = sizes
        lead = lead if isinstance(lead, tuple) else (lead,)
        reductions += [VMEM((*lead, n, 128), BF) for n in lengths]
    inputs = (features, cotangent, w_qkv, w_proj, w_fc1, w_fc2_t, w_conv, g1, g2, table)
    scratch = [VMEM(v.shape, v.dtype) for v in inputs]
    scratch += [
        VMEM((NBLK, TOK, C), BF),
        VMEM((GROWS, 128), BF),
        VMEM((4, COLS, C), BF),
        VMEM((5, COLS, C), BF),
        VMEM((ROWS * 4, C), BF),
        VMEM((ROWS * 8, C), BF),
        VMEM((16, C), BF),
        VMEM((48, C), BF),
        VMEM((ROWS * 4, C), BF),
        VMEM((ROWS * 8, C), BF),
        VMEM((256, C), BF),
        VMEM((GROWS, 128), BF),
        *reductions,
        VMEM((NBLK, TOK, C), BF),
        VMEM((3, NBLK, (ROWS + 2) * BLK, C), BF),
        VMEM((3 * CP, CP), BF),
        VMEM((CP, 3 * CP), BF),
        VMEM((CP, CP), BF),
        VMEM((CP, CP), BF),
        VMEM((FF, CP), BF),
        VMEM((CP, FF), BF),
        VMEM((CP, FF), BF),
        VMEM((FF, CP), BF),
        VMEM((HEADS, WIN * WIN, PAIR), F32),
        VMEM((NBLK, CP, TOK), F32),
        VMEM((NBLK, 1, TOK), F32),
        VMEM((NBLK, CP, TOK), BF),
        VMEM((NBLK, 3 * CP, TOK), BF),
        VMEM((NBLK, CP, TOK), BF),
        VMEM((NBLK, blocks, HEADS, WIN * WIN, PAIR), F32),
        VMEM((NBLK, CP, TOK), F32),
        VMEM((NBLK, 1, TOK), F32),
        VMEM((NBLK, CP, TOK), BF),
        VMEM((NBLK, FF, TOK), F32),
        VMEM((NBLK, FF, TOK), BF),
        VMEM((3, NBLK, CP, TOK), BF),
        VMEM((NBLK, CP, TOK), BF),
        VMEM((NBLK, FF, TOK), BF),
        VMEM((NBLK, CP, TOK), BF),
        VMEM((NBLK, CP, TOK), BF),
        VMEM((NBLK, 3 * CP, TOK), BF),
        VMEM((NBLK, CP, TOK), F32),
        pltpu.SemaphoreType.DMA((10,)),
        pltpu.SemaphoreType.DMA((3,)),
        pltpu.SemaphoreType.DMA((6,)),
        pltpu.SemaphoreType.DMA((6,)),
        pltpu.SemaphoreType.DMA((3,)),
        pltpu.SemaphoreType.DMA((3,)),
        pltpu.SemaphoreType.DMA((2, 6)),
        pltpu.SemaphoreType.DMA((2, 6)),
        pltpu.SemaphoreType.DMA((2, 4, 3, SIDE - 1)),
        pltpu.SemaphoreType.DMA((2, 4, 3, SIDE - 1)),
    ]
    return pl.pallas_call(
        layer,
        out_shape=(
            jax.ShapeDtypeStruct((NBLK, TOK, C), BF),
            jax.ShapeDtypeStruct((GROWS, 128), BF),
            jax.ShapeDtypeStruct((NBLK, 64, C), BF),
            jax.ShapeDtypeStruct((256, C), BF),
            jax.ShapeDtypeStruct((32, C), BF),
        ),
        in_specs=[pl.BlockSpec(memory_space=pl.ANY)] * 10,
        out_specs=[pl.BlockSpec(memory_space=pl.ANY)] * 2 + [pl.BlockSpec(memory_space=VMEM)] * 3,
        scratch_shapes=scratch,
        compiler_params=pltpu.CompilerParams(
            collective_id=0, has_side_effects=True, vmem_limit_bytes=60 * 2**20
        ),
        name="layer",
    )(*inputs)


def results(
    d_hbm, hr_hbm, hs_hbm, hc_hbm, sum_hbm,
    out_ref, qkv_ref, proj_ref, fc1_ref, fc2_ref, conv_ref,
    d_ref, hr_ref, hs_ref, hc_ref, sum_ref, load,
):
    hbm = (sum_hbm, d_hbm, hr_hbm, hs_hbm, hc_hbm)
    own = (sum_ref, d_ref, hr_ref, hs_ref, hc_ref)
    loads = [pltpu.make_async_copy(s, t, load.at[i]) for i, (s, t) in enumerate(zip(hbm, own))]
    for c in loads:
        c.start()
    for c in loads:
        c.wait()
    sub = iota((8, C), 0)
    extras = hs_ref[...].astype(F32).reshape(ROWS, 8, C)
    corners = hc_ref[...].astype(F32).reshape(4, 8, C)
    for i in range(ROWS):
        if i < 4:
            pieces = [hr_ref[b, i * BLK : (i + 1) * BLK, :] for b in range(NBLK)]
            extra = corners[i]
        else:
            pieces = [d_ref[b, (i - 4) * BLK : (i - 3) * BLK, :] for b in range(NBLK)]
            extra = extras[i - 4]
        v = pltpu.roll(jnp.concatenate(pieces, axis=0).astype(F32), 4, 0)
        head = jnp.where(sub < 4, pltpu.roll(extra, 4, 0), v[:8])
        out_ref[i] = low(jnp.concatenate([head, v[8:]], axis=0))

    scale = 1.0 / math.sqrt(ROWS * COLS * lax.axis_size("row") * lax.axis_size("col"))

    def full(i):
        return sum_ref[i * CP : (i + 1) * CP, :]

    def rest(i):
        return full(9 + i // 2)[:, 64 * (i % 2) : 64 * (i % 2) + 64]

    def square(i, r):
        return jnp.concatenate([full(i), rest(r)], axis=1)

    for t in range(9):
        conv_ref[t] = square(t, t).astype(F32)[:C, :C] * scale
    proj_ref[...] = nn(spread(CP, C, 1), jnp.concatenate([full(20), full(25)[:, :64]], axis=1))[:, :C] * scale
    fc2 = jnp.concatenate([full(14), full(15), full(16)], axis=1).astype(F32)
    fc2_ref[...] = fc2[:C, :FF] * scale
    fc1 = jnp.concatenate([full(17), full(18), full(19)], axis=1).astype(F32)
    fc1_ref[...] = fc1[:C, :FF] * scale
    qkv = jnp.concatenate([full(21), full(22), full(23), full(24), full(25)[:, 64:]], axis=1)
    qkv_ref[...] = nn(qkv, spread(3 * CP, 3 * C, 0))[:C] * scale


def call_results(d_shifted, halo, sums):
    return pl.pallas_call(
        results,
        out_shape=(
            jax.ShapeDtypeStruct((ROWS, COLS, C), BF),
            jax.ShapeDtypeStruct((C, 3 * C), F32),
            jax.ShapeDtypeStruct((C, C), F32),
            jax.ShapeDtypeStruct((C, FF), F32),
            jax.ShapeDtypeStruct((C, FF), F32),
            jax.ShapeDtypeStruct((9, C, C), F32),
        ),
        in_specs=[pl.BlockSpec(memory_space=pl.ANY)] * 5,
        out_specs=[pl.BlockSpec(memory_space=VMEM)] * 6,
        scratch_shapes=[
            *(VMEM(v.shape, v.dtype) for v in (d_shifted, *halo, sums)),
            pltpu.SemaphoreType.DMA((5,)),
        ],
        compiler_params=pltpu.CompilerParams(vmem_limit_bytes=32 * 2**20),
        name="results",
    )(d_shifted, *halo, sums)


def local(features, cotangent, w_qkv, w_proj, w_fc1, w_fc2, w_conv, gain_attn, gain_mlp, pos_table):
    d_shifted, sums, *halo = call_layer(
        features,
        cotangent,
        w_qkv,
        w_proj,
        w_fc1,
        w_fc2.T,
        w_conv,
        gain_attn.reshape(1, C),
        gain_mlp.reshape(1, C),
        pos_table.T,
    )
    d_features, qkv, proj, fc1, fc2, conv = call_results(d_shifted, halo, sums)
    return d_features, qkv, proj, fc1, fc2.T, conv


def solution(mesh):
    return jax.shard_map(
        local,
        mesh=mesh,
        in_specs=(P("row", "col", None), P("row", "col", None)) + (P(),) * 8,
        out_specs=(P("row", "col", None),) + (P(),) * 5,
        check_vma=False,
    )
```

```python
import math

import jax
import jax.numpy as jnp
from jax import lax
from jax.experimental import pallas as pl
from jax.experimental.pallas import tpu as pltpu
from jax.sharding import PartitionSpec as P

C = 180
CP = 192
HEADS = 6
HD = 30
HP = 32
FF = 360
WIN = 8
SHIFT = 4
ROWS = 32
COLS = 64
BLK = 16
NBLK = COLS // BLK
TOK = ROWS * BLK
PAIR = WIN * BLK
SIDE = 4
TILES = (14, 8, 6)
BASE = (0, TILES[0] * CP, (TILES[0] + TILES[1]) * CP)
GROWS = sum(TILES) * CP
HALVES = tuple(t * CP // 2 for t in TILES)
PARTS = tuple(h // 3 for h in HALVES)
SHARES = tuple(p // SIDE for p in PARTS)
BF = jnp.bfloat16
F32 = jnp.float32
MESH = pl.DeviceIdType.MESH
VMEM = pltpu.VMEM


def iota(shape, dim):
    return lax.broadcasted_iota(jnp.int32, shape, dim)


def nn(a, b):
    return lax.dot_general(a, b, (((1,), (0,)), ((), ())), preferred_element_type=F32)


def nt(a, b):
    return lax.dot_general(a, b, (((1,), (1,)), ((), ())), preferred_element_type=F32)


def low(a):
    return a.astype(BF)


def eye(rows, cols):
    return low(jnp.where(iota((rows, cols), 0) == iota((rows, cols), 1), 1.0, 0.0))


def spread(padded, plain, pad_dim):
    shape = (padded, plain) if pad_dim == 0 else (plain, padded)
    p = iota(shape, pad_dim)
    c = iota(shape, 1 - pad_dim)
    hit = ((p & (HP - 1)) < HD) & (c == (p >> 5) * HD + (p & (HP - 1)))
    return low(jnp.where(hit, 1.0, 0.0))


def column(gain_ref):
    wide = jnp.where(iota((CP, C), 0) == iota((CP, C), 1), gain_ref[...], 0.0)
    return jnp.sum(wide, axis=1, keepdims=True)


def moments(values):
    mean = jnp.sum(values[:C], axis=0, keepdims=True) * (1.0 / C)
    centred = values - mean
    inner = centred[:C]
    var = jnp.sum(inner * inner, axis=0, keepdims=True) * (1.0 / C)
    return centred, lax.rsqrt(var + 1e-05)


def norm_back(upstream, normed, inverse, gain):
    scaled = upstream * gain
    first = jnp.sum(scaled, axis=0, keepdims=True) * (1.0 / C)
    second = jnp.sum(scaled * normed, axis=0, keepdims=True) * (1.0 / C)
    return inverse * (scaled - first - normed * second)


def gelu_parts(x):
    u = jnp.abs(x) * math.sqrt(0.5)
    t = 1.0 / (1.0 + 0.3275911 * u)
    e = jnp.exp(-u * u)
    poly = t * (
        0.254829592
        + t * (-0.284496736 + t * (1.421413741 + t * (-1.453152027 + t * 1.061405429)))
    )
    tail = 0.5 * poly * e
    cdf = jnp.where(x >= 0.0, 1.0 - tail, tail)
    return cdf, e * (1.0 / math.sqrt(2.0 * math.pi))


def fold(scores, second):
    parts = scores.reshape(WIN, 2, WIN, PAIR)
    return jnp.where(second, parts[:, 1], parts[:, 0]).reshape(WIN * WIN, PAIR)


def unfold(probs, second):
    parts = probs.reshape(WIN, WIN, PAIR)
    zero = jnp.zeros_like(parts)
    both = jnp.stack([jnp.where(second, zero, parts), jnp.where(second, parts, zero)], axis=1)
    return low(both.reshape(PAIR, PAIR))


def two_heads(block):
    zero = jnp.zeros((HP, PAIR), BF)
    top = jnp.concatenate([block[:HP], zero], axis=1)
    return jnp.concatenate([top, jnp.concatenate([zero, block[HP:]], axis=1)], axis=0)


def own_heads(product):
    return jnp.concatenate([product[:HP, :PAIR], product[HP:, PAIR:]], axis=0)


def tn(a, b):
    return lax.dot_general(a, b, (((0,), (0,)), ((), ())), preferred_element_type=F32)


def layer(
    f_hbm, g_hbm, wqkv_hbm, wproj_hbm, w1_hbm, w2_hbm, wconv_hbm, g1_hbm, g2_hbm, pos_hbm,
    d_hbm, sum_hbm, hr_ref, hs_ref, hc_ref,
    f_ref, g_ref, wqkv_ref, wproj_ref, w1_ref, w2_ref, wconv_ref, g1_ref, g2_ref, pos_ref,
    d_ref, sum_ref,
    fr_ref, gr_ref, fstrip_ref, gstrip_ref, fcorner_ref, gcorner_ref,
    fstrip_in, gstrip_in, strip_out,
    grads_ref, first0, first1, first2, second0, second1, second2, third0, third1, third2,
    xs, gs, wqkvt, wqkvp, wprojt, wprojp, w1t, w1p, w2t, w2p, bias,
    s_norm1, s_inv1, s_n1, packed, attended, probs, s_norm2, s_inv2, s_n2, s_slope, s_hidden, s_z,
    dshift, s_dpre, s_dattn, dheads, dpacked, s_dmid,
    load, store, in_send, in_recv, out_send, out_recv, send, recv,
):
    row, col = lax.axis_index("row"), lax.axis_index("col")
    n_row, n_col = lax.axis_size("row"), lax.axis_size("col")
    up, down = lax.rem(row + n_row - 1, n_row), lax.rem(row + 1, n_row)
    left, right = lax.rem(col + n_col - 1, n_col), lax.rem(col + 1, n_col)
    last_row, last_col = row == n_row - 1, col == n_col - 1
    factor = HD**-0.5
    core, z, y = lax.rem(row, 2), lax.rem(row // 2, SIDE), lax.rem(col, SIDE)
    x = (row // 8) * 2 + col // SIDE
    here = (x, y, z)

    def device(xyz, c):
        return ((xyz[0] // 2) * 8 + xyz[2] * 2 + c, lax.rem(xyz[0], 2) * SIDE + xyz[1])

    def along(axis, k, other):
        there = list(here)
        there[axis] = lax.rem(there[axis] + k, SIDE)
        return device(there, 1 - core if other else core)

    sibling = device(here, 1 - core)
    seven = [(k, other) for k in range(SIDE) for other in (0, 1) if k + other > 0]
    barrier = pltpu.get_barrier_semaphore()
    greeted = [sibling, (up, col), (row, left), (up, left), (down, col), (row, right)]
    greeted += [(down, right)]
    greeted += [along(axis, k, o) for axis in range(3) for k, o in seven if k > 0]
    for peer in greeted:
        pl.semaphore_signal(barrier, inc=1, device_id=peer, device_id_type=MESH)

    hbm = (f_hbm, g_hbm, wqkv_hbm, wproj_hbm, w1_hbm, w2_hbm, wconv_hbm, g1_hbm, g2_hbm, pos_hbm)
    own = (f_ref, g_ref, wqkv_ref, wproj_ref, w1_ref, w2_ref, wconv_ref, g1_ref, g2_ref, pos_ref)
    loads = [pltpu.make_async_copy(s, t, load.at[i]) for i, (s, t) in enumerate(zip(hbm, own))]
    for c in loads:
        c.start()
    started = []

    def copy(src, dst, s, r, peer):
        c = pltpu.make_async_remote_copy(
            src_ref=src, dst_ref=dst, send_sem=s, recv_sem=r, device_id=peer, device_id_type=MESH
        )
        c.start()
        started.append(c)
        return c

    loads[0].wait()
    fs = f_ref[:, 0:16, :].astype(F32)[:, 0:8, :].reshape(ROWS // 2, 2, 8, C)
    pairs = jnp.where(iota((ROWS // 2, 8, C), 1) < 4, fs[:, 0], pltpu.roll(fs[:, 1], 4, 1))
    fstrip_in[...] = low(pairs.reshape(ROWS * 4, C))
    pl.semaphore_wait(barrier, len(greeted))
    f_arriving = [
        copy(fstrip_in.at[0:16], fcorner_ref, in_send.at[0], in_recv.at[0], (up, left)),
        copy(fstrip_in, fstrip_ref, in_send.at[1], in_recv.at[1], (row, left)),
        copy(f_ref.at[0:4], fr_ref, in_send.at[2], in_recv.at[2], (up, col)),
    ]
    loads[1].wait()
    cs = g_ref[:, 0:16, :].astype(F32)[:, 0:8, :]
    gstrip_in[...] = low(cs.reshape(ROWS * 8, C))
    g_arriving = [
        copy(gstrip_in.at[0:48], gcorner_ref, in_send.at[3], in_recv.at[3], (up, left)),
        copy(gstrip_in, gstrip_ref, in_send.at[4], in_recv.at[4], (row, left)),
        copy(g_ref.at[0:5], gr_ref, in_send.at[5], in_recv.at[5], (up, col)),
    ]

    sub = iota((8, C), 0)
    keep0 = jnp.where((sub == 3) & last_col, 0.0, 1.0)
    keep2 = jnp.where((sub == 4) & last_col, 0.0, 1.0)
    LASTB = NBLK - 1

    def put(target, i, rolled):
        whole = low(rolled[: LASTB * BLK])
        for b in range(LASTB):
            target[b, i * BLK : (i + 1) * BLK, :] = whole[b * BLK : (b + 1) * BLK]

    def put_last(target, i, body, last):
        target[LASTB, i * BLK : (i + 1) * BLK, :] = low(jnp.concatenate([body, last], axis=0))

    def put_x(i, v):
        put(xs, i, pltpu.roll(v, 60, 0))

    def put_x_last(i, v, extra):
        r = pltpu.roll(v, 12, 0)
        put_last(xs, i, r[:8], jnp.where(sub < 4, r[8:], extra))

    def put_g(i, v):
        for k, turn in enumerate((59, 60, 61)):
            put(gs.at[k], i, pltpu.roll(v, turn, 0))

    def put_g_last(i, v, extra):
        for k, n in enumerate((5, 4, 3)):
            r = pltpu.roll(v, 16 - n, 0)
            last = jnp.where(sub < 8 - n, r[8:], pltpu.roll(extra, 8 - n, 0))
            if k != 1:
                last = last * (keep0, keep2)[k // 2]
            put_last(gs.at[k], i, r[:8], last)

    for i in range(ROWS - 4):
        put_x(i, f_ref[i + 4].astype(F32))
    for i in range(ROWS - 3):
        put_g(i, g_ref[i + 3].astype(F32))

    for c in loads[2:]:
        c.wait()
    pad = eye(CP, C)
    sel, sel_one = spread(3 * CP, 3 * C, 0), spread(CP, C, 0)
    wq = low(nn(pad, wqkv_ref[...]))
    wqkvt[...] = low(nt(sel, wq))
    wqkvp[...] = low(nt(wq, sel))
    turned = low(nt(pad, wproj_ref[...]))
    wprojt[...] = low(nt(turned, sel_one))
    wprojp[...] = low(nt(sel_one, turned))
    w1p[...] = low(nn(pad, w1_ref[...]))
    w1t[...] = low(nt(eye(FF, FF), w1p[...]))
    w2t[...] = low(nn(pad, w2_ref[...]))
    w2p[...] = low(nt(eye(FF, FF), w2t[...]))
    gain1, gain2 = column(g1_ref), column(g2_ref)

    table = pos_ref[...]
    high = low(table)
    mid = low(table - high.astype(F32))
    rest_piece = low(table - high.astype(F32) - mid.astype(F32))
    entry, place = iota((225, 15 * BLK), 0), iota((225, 15 * BLK), 1)
    for kc in range(WIN):
        hit = entry == (place >> 4) * 15 + (place & 7) - kc + 7
        pick = low(jnp.where(hit, 1.0, 0.0))
        line = nn(high, pick) + nn(mid, pick) + nn(rest_piece, pick)
        for h in range(HEADS):
            for kr in range(WIN):
                start = (WIN - 1 - kr) * BLK
                at = kr * WIN + kc
                bias[h, at : at + 1, :] = line[h : h + 1, start : start + PAIR]
    dshift[...] = jnp.zeros_like(dshift)

    f_arriving[2].wait_recv()
    for i in range(ROWS - 4, ROWS):
        put_x(i, fr_ref[i - 28].astype(F32))

    def last_block():
        f_arriving[1].wait_recv()
        f_arriving[0].wait_recv()
        quads = fstrip_ref[...].astype(F32).reshape(ROWS // 2, 8, C)
        corner = fcorner_ref[...].astype(F32).reshape(2, 8, C)

        def quad(source, i):
            return pltpu.roll(source[i // 2], 4, 0) if i % 2 == 0 else source[i // 2]

        for i in range(ROWS):
            if i < ROWS - 4:
                put_x_last(i, f_ref[i + 4, COLS - 16 :, :].astype(F32), quad(quads, i + 4))
            else:
                put_x_last(i, fr_ref[i - 28, COLS - 16 :, :].astype(F32), quad(corner, i - 28))

    lane = iota((1, PAIR), 1)
    second = ((lane >> 3) & 1) == 1
    k_sub, q_lane = iota((WIN * WIN, PAIR), 0), iota((WIN * WIN, PAIR), 1)
    rows_differ = ((k_sub >> 5) & 1) != ((q_lane >> 6) & 1)
    cols_differ = (((k_sub >> 2) & 1) != ((q_lane >> 2) & 1)) & (((q_lane >> 3) & 1) == 1)
    tok = iota((1, TOK), 1) >> 4
    drop0 = (tok == 27) & last_row
    drop2 = (tok == 28) & last_row

    def forward(step, carry):
        bs = (2 * step, 2 * step + 1)
        pl.when(step == 1)(last_block)
        xv = [nt(pad, xs[b]) for b in bs]
        for b, x in zip(bs, xv):
            centred, inv1 = moments(x)
            normed1 = centred * inv1
            s_norm1[b] = normed1
            s_inv1[b] = inv1
            s_n1[b] = low(normed1 * gain1)
        for b in bs:
            packed[b] = low(nn(wqkvt[...], s_n1[b]))
        units = [(b, a, j) for b in bs for a in range(ROWS // WIN) for j in range(HEADS // 2)]

        def part(b, third, a, j):
            top = third * CP + 64 * j
            return packed[b, top : top + 64, a * PAIR : (a + 1) * PAIR]

        scores = [tn(part(b, 1, a, j), two_heads(part(b, 0, a, j))) for b, a, j in units]
        soft = []
        for (b, a, j), score in zip(units, scores):
            row_flag = last_row & (a == ROWS // WIN - 1)
            col_flag = last_col & (b == NBLK - 1)
            mask = jnp.where((rows_differ & row_flag) | (cols_differ & col_flag), -100.0, 0.0)
            wide = []
            for s in range(2):
                sc = fold(score[:, s * PAIR : (s + 1) * PAIR], second)
                sc = sc * factor + bias[2 * j + s] + mask
                e = jnp.exp(sc - jnp.max(sc, axis=0, keepdims=True))
                p = e * (1.0 / jnp.sum(e, axis=0, keepdims=True))
                probs[b, a, 2 * j + s] = p
                wide.append(unfold(p, second))
            soft.append(jnp.concatenate(wide, axis=1))
        for (b, a, j), wide in zip(units, soft):
            o = nn(part(b, 2, a, j), wide)
            attended[b, 64 * j : 64 * j + 64, a * PAIR : (a + 1) * PAIR] = low(own_heads(o))

        middles = [x + nn(wprojt[...], attended[b]) for b, x in zip(bs, xv)]
        for b, middle in zip(bs, middles):
            centred2, inv2 = moments(middle)
            normed2 = centred2 * inv2
            s_norm2[b] = normed2
            s_inv2[b] = inv2
            s_n2[b] = low(normed2 * gain2)
        pres = [nn(w1t[...], s_n2[b]) for b in bs]
        for b, pre in zip(bs, pres):
            cdf, pdf = gelu_parts(pre)
            s_hidden[b] = low(pre * cdf)
            s_slope[b] = cdf + pre * pdf
        for b, middle in zip(bs, middles):
            z = middle + nn(w2t[...], s_hidden[b])
            s_z[1, b] = low(z)
            s_z[0, b] = low(jnp.where(drop0, 0.0, z))
            s_z[2, b] = low(jnp.where(drop2, 0.0, z))
        return carry

    lax.fori_loop(0, NBLK // 2, forward, 0)

    for c in g_arriving:
        c.wait_recv()
    for i in range(ROWS + 2):
        if i < ROWS - 3:
            extra = gstrip_ref[(i + 3) * 8 : (i + 4) * 8, :]
            put_g_last(i, g_ref[i + 3, COLS - 16 :, :].astype(F32), extra.astype(F32))
        else:
            k = i - ROWS + 3
            put_g(i, gr_ref[k].astype(F32))
            extra = gcorner_ref[k * 8 : (k + 1) * 8, :]
            put_g_last(i, gr_ref[k, COLS - 16 :, :].astype(F32), extra.astype(F32))

    def tap(b, dy, dx):
        return gs[dx, b, (2 - dy) * BLK : (2 - dy) * BLK + TOK, :]

    def over_blocks(term):
        total = term(0)
        for b in range(1, NBLK):
            total = total + term(b)
        return total

    def put_tile(place, tile):
        grads_ref[place * CP : (place + 1) * CP, :] = low(tile)

    def put_pair(place, left, right):
        put_tile(place, jnp.concatenate([left, right], axis=1))

    held_back = None
    for t in range(9):
        total = over_blocks(lambda b: nn(s_z[t // 3, b], tap(b, t // 3, t % 3)))
        put_tile(t, total[:, :128])
        narrow = jnp.concatenate([total[:, 128:], jnp.zeros((CP, 256 - 12 - C), F32)], axis=1)
        narrow = narrow[:, :64]
        if t % 2 == 0:
            held_back = narrow
        else:
            put_pair(9 + t // 2, held_back, narrow)
    put_pair(13, held_back, jnp.zeros((CP, 64), F32))
    steps = ((first0, second0, third0), (first1, second1, third1), (first2, second2, third2))
    flying = [{}, {}, {}]

    def rows(start, size):
        return pl.ds(pl.multiple_of(start, 16), size)

    def share_rows(g, c, p, share):
        at = BASE[g] + c * HALVES[g] + p * PARTS[g] + share * SHARES[g]
        return rows(at, SHARES[g])

    def go_first(g):
        flying[g]["first"] = [
            [
                copy(
                    grads_ref.at[
                        share_rows(g, 1 - core if o else core, p, lax.rem(here[p] + k, SIDE))
                    ],
                    steps[g][0].at[p, i],
                    send.at[g, 0, p, i],
                    recv.at[g, 0, p, i],
                    along(p, k, o),
                )
                for i, (k, o) in enumerate(seven)
            ]
            for p in range(3)
        ]

    def spread_out(g, p, step, source, axis):
        target = steps[g][step]
        target[p, here[axis]] = source
        return [
            copy(
                target.at[p, here[axis]],
                target.at[p, here[axis]],
                send.at[g, step, p, k - 1],
                recv.at[g, step, p, k - 1],
                along(axis, k, 0),
            )
            for k in range(1, SIDE)
        ]

    def gathered(copies, target, p):
        for c in copies:
            c.wait_recv()
        total = target[p, 0].astype(F32)
        for k in range(1, SIDE):
            total = total + target[p, k].astype(F32)
        return low(total)

    def go_second(g):
        flying[g]["second"] = []
        for p in range(3):
            total = grads_ref[share_rows(g, core, p, here[p]), :].astype(F32)
            for i in range(len(seven)):
                flying[g]["first"][p][i].wait_recv()
                total = total + steps[g][0][p, i].astype(F32)
            flying[g]["second"].append(spread_out(g, p, 1, low(total), (p + 1) % 3))

    def go_third(g):
        flying[g]["third"] = []
        for p in range(3):
            total = gathered(flying[g]["second"][p], steps[g][1], p)
            flying[g]["third"].append(spread_out(g, p, 2, total, (p + 2) % 3))

    def go_back(g):
        flying[g]["end"] = []
        for p in range(3):
            at = share_rows(g, core, p, here[p])
            sum_ref[at, :] = gathered(flying[g]["third"][p], steps[g][2], p)
            flying[g]["end"] += [
                copy(
                    sum_ref.at[at],
                    sum_ref.at[at],
                    send.at[g, 3, p, i],
                    recv.at[g, 3, p, i],
                    along(p, k, o),
                )
                for i, (k, o) in enumerate(seven)
            ]

    go_first(0)

    def conv_back(b, carry):
        total = None
        for dy in range(3):
            part = None
            for dx in range(3):
                product = nt(wconv_ref[3 * dy + dx], tap(b, dy, dx))
                part = product if part is None else part + product
            if dy != 1:
                part = jnp.where((drop0, drop2)[dy // 2], 0.0, part)
            total = part if total is None else total + part
        dshift[b, :C, :] = low(total)
        return carry

    def back_to_heads(step, carry):
        bs = (2 * step, 2 * step + 1)
        d_pres = [low(nn(w2p[...], dshift[b]) * s_slope[b]) for b in bs]
        d_middles = []
        for b, d_pre in zip(bs, d_pres):
            s_dpre[b] = d_pre
            d_middle = dshift[b].astype(F32) + norm_back(
                nn(w1p[...], d_pre), s_norm2[b], s_inv2[b], gain2
            )
            s_dmid[b] = d_middle
            d_middles.append(low(d_middle))
        for b, d_attn in zip(bs, d_middles):
            s_dattn[b] = d_attn
            dheads[b] = low(nn(wprojp[...], d_attn))
        return carry

    lax.fori_loop(0, NBLK, conv_back, 0)
    lax.fori_loop(0, NBLK // 2, back_to_heads, 0)
    go_second(0)

    fc2 = over_blocks(lambda b: nt(dshift[b], s_hidden[b]))
    fc1 = over_blocks(lambda b: nt(s_n2[b], s_dpre[b]))
    for place, total in ((14, fc2), (17, fc1)):
        put_tile(place, total[:, :128])
        put_tile(place + 1, total[:, 128:256])
        put_pair(place + 2, total[:, 256:], jnp.zeros((CP, 384 - FF), F32))
    proj = over_blocks(lambda b: nt(attended[b], s_dattn[b]))
    put_tile(20, proj[:, :128])
    put_pair(21, proj[:, 128:192], jnp.zeros((CP, 64), F32))
    go_first(1)

    def heads_back(b):
        units = [(a, j) for a in range(ROWS // WIN) for j in range(HEADS // 2)]

        def part(ref, third, a, j):
            top = third * CP + 64 * j
            return ref[b, top : top + 64, a * PAIR : (a + 1) * PAIR]

        d_probs = {}
        for a, j in units:
            d_probs[a, j] = tn(part(packed, 2, a, j), two_heads(part(dheads, 0, a, j)))
        p_all, s_all = {}, {}
        for a, j in units:
            p_wide, s_wide = [], []
            for s in range(2):
                p = probs[b, a, 2 * j + s]
                dp = fold(d_probs[a, j][:, s * PAIR : (s + 1) * PAIR], second)
                ds = p * (dp - jnp.sum(p * dp, axis=0, keepdims=True)) * factor
                p_wide.append(unfold(p, second))
                s_wide.append(unfold(ds, second))
            p_all[a, j], s_all[a, j] = p_wide, s_wide
        for a, j in units:
            lanes = slice(a * PAIR, (a + 1) * PAIR)
            dv = nt(part(dheads, 0, a, j), jnp.concatenate(p_all[a, j], axis=0))
            dq = nn(part(packed, 1, a, j), jnp.concatenate(s_all[a, j], axis=1))
            dk = nt(part(packed, 0, a, j), jnp.concatenate(s_all[a, j], axis=0))
            dpacked[b, 64 * j : 64 * j + 64, lanes] = low(own_heads(dq))
            dpacked[b, CP + 64 * j : CP + 64 * j + 64, lanes] = low(own_heads(dk))
            dpacked[b, 2 * CP + 64 * j : 2 * CP + 64 * j + 64, lanes] = low(own_heads(dv))

    heads_back(0)
    heads_back(1)
    go_third(0)
    heads_back(2)
    heads_back(3)
    qkv = over_blocks(lambda b: nt(s_n1[b], dpacked[b]))
    for i in range(4):
        put_tile(22 + i, qkv[:, i * 128 : (i + 1) * 128])
    put_pair(26, qkv[:, 512:576], jnp.zeros((CP, 64), F32))
    put_tile(27, jnp.zeros((CP, 128), F32))
    go_first(2)
    go_second(1)

    ones_pair = eye(PAIR, PAIR)

    def inputs_back(b):
        d_in = s_dmid[b] + norm_back(nn(wqkvp[...], dpacked[b]), s_norm1[b], s_inv1[b], gain1)
        d_low = low(d_in)
        for a in range(ROWS // WIN):
            natural = nt(ones_pair, d_low[:, a * PAIR : (a + 1) * PAIR])
            d_ref[b, a * PAIR : (a + 1) * PAIR, :] = low(natural[:, :C])

    inputs_back(NBLK - 1)
    edge = d_ref[NBLK - 1].astype(F32).reshape(ROWS, 2, 8, C)[:, 1]
    strip_out[...] = low(edge.reshape(ROWS * 8, C))
    leaving = [
        copy(strip_out.at[224:256], hc_ref, out_send.at[2], out_recv.at[2], (down, right)),
        copy(strip_out, hs_ref, out_send.at[1], out_recv.at[1], (row, right)),
    ]
    inputs_back(0)
    inputs_back(1)
    inputs_back(2)
    leaving.append(
        copy(d_ref.at[:, 448:512, :], hr_ref, out_send.at[0], out_recv.at[0], (down, col))
    )
    stores = [pltpu.make_async_copy(d_ref, d_hbm, store.at[0])]
    stores[0].start()

    def keep(g):
        for c in flying[g]["end"]:
            c.wait_recv()
        at = slice(BASE[g], BASE[g] + TILES[g] * CP)
        stores.append(pltpu.make_async_copy(sum_ref.at[at], sum_hbm.at[at], store.at[1 + g]))
        stores[-1].start()

    go_back(0)
    go_second(2)
    go_third(1)
    go_third(2)
    go_back(1)
    keep(0)
    go_back(2)
    keep(1)
    keep(2)
    for c in leaving:
        c.wait_recv()
    for c in started:
        c.wait_send()
    for c in stores:
        c.wait()


def call_layer(features, cotangent, w_qkv, w_proj, w_fc1, w_fc2_t, w_conv, g1, g2, table):
    blocks = ROWS // WIN
    reductions = []
    for slots in (2 * SIDE - 1, SIDE, SIDE):
        reductions += [VMEM((3, slots, n, 128), BF) for n in SHARES]
    inputs = (features, cotangent, w_qkv, w_proj, w_fc1, w_fc2_t, w_conv, g1, g2, table)
    scratch = [VMEM(v.shape, v.dtype) for v in inputs]
    scratch += [
        VMEM((NBLK, TOK, C), BF),
        VMEM((GROWS, 128), BF),
        VMEM((4, COLS, C), BF),
        VMEM((5, COLS, C), BF),
        VMEM((ROWS * 4, C), BF),
        VMEM((ROWS * 8, C), BF),
        VMEM((16, C), BF),
        VMEM((48, C), BF),
        VMEM((ROWS * 4, C), BF),
        VMEM((ROWS * 8, C), BF),
        VMEM((256, C), BF),
        VMEM((GROWS, 128), BF),
        *reductions,
        VMEM((NBLK, TOK, C), BF),
        VMEM((3, NBLK, (ROWS + 2) * BLK, C), BF),
        VMEM((3 * CP, CP), BF),
        VMEM((CP, 3 * CP), BF),
        VMEM((CP, CP), BF),
        VMEM((CP, CP), BF),
        VMEM((FF, CP), BF),
        VMEM((CP, FF), BF),
        VMEM((CP, FF), BF),
        VMEM((FF, CP), BF),
        VMEM((HEADS, WIN * WIN, PAIR), F32),
        VMEM((NBLK, CP, TOK), F32),
        VMEM((NBLK, 1, TOK), F32),
        VMEM((NBLK, CP, TOK), BF),
        VMEM((NBLK, 3 * CP, TOK), BF),
        VMEM((NBLK, CP, TOK), BF),
        VMEM((NBLK, blocks, HEADS, WIN * WIN, PAIR), F32),
        VMEM((NBLK, CP, TOK), F32),
        VMEM((NBLK, 1, TOK), F32),
        VMEM((NBLK, CP, TOK), BF),
        VMEM((NBLK, FF, TOK), F32),
        VMEM((NBLK, FF, TOK), BF),
        VMEM((3, NBLK, CP, TOK), BF),
        VMEM((NBLK, CP, TOK), BF),
        VMEM((NBLK, FF, TOK), BF),
        VMEM((NBLK, CP, TOK), BF),
        VMEM((NBLK, CP, TOK), BF),
        VMEM((NBLK, 3 * CP, TOK), BF),
        VMEM((NBLK, CP, TOK), F32),
        pltpu.SemaphoreType.DMA((10,)),
        pltpu.SemaphoreType.DMA((4,)),
        pltpu.SemaphoreType.DMA((6,)),
        pltpu.SemaphoreType.DMA((6,)),
        pltpu.SemaphoreType.DMA((3,)),
        pltpu.SemaphoreType.DMA((3,)),
        pltpu.SemaphoreType.DMA((3, 4, 3, 2 * SIDE - 1)),
        pltpu.SemaphoreType.DMA((3, 4, 3, 2 * SIDE - 1)),
    ]
    return pl.pallas_call(
        layer,
        out_shape=(
            jax.ShapeDtypeStruct((NBLK, TOK, C), BF),
            jax.ShapeDtypeStruct((GROWS, 128), BF),
            jax.ShapeDtypeStruct((NBLK, 64, C), BF),
            jax.ShapeDtypeStruct((256, C), BF),
            jax.ShapeDtypeStruct((32, C), BF),
        ),
        in_specs=[pl.BlockSpec(memory_space=pl.ANY)] * 10,
        out_specs=[pl.BlockSpec(memory_space=pl.ANY)] * 2 + [pl.BlockSpec(memory_space=VMEM)] * 3,
        scratch_shapes=scratch,
        compiler_params=pltpu.CompilerParams(
            collective_id=0, has_side_effects=True, vmem_limit_bytes=60 * 2**20
        ),
        name="layer",
    )(*inputs)


def results(
    d_hbm, hr_hbm, hs_hbm, hc_hbm, sum_hbm,
    out_hbm, qkv_hbm, proj_hbm, fc1_hbm, fc2_hbm, conv_hbm,
    d_ref, hr_ref, hs_ref, hc_ref, sum_ref,
    out_ref, qkv_ref, proj_ref, fc1_ref, fc2_ref, conv_ref, load, store,
):
    hbm = (hr_hbm, hs_hbm, hc_hbm, d_hbm, sum_hbm)
    own = (hr_ref, hs_ref, hc_ref, d_ref, sum_ref)
    loads = [pltpu.make_async_copy(s, t, load.at[i]) for i, (s, t) in enumerate(zip(hbm, own))]
    for c in loads:
        c.start()
    stores = []

    def keep(source, target):
        stores.append(pltpu.make_async_copy(source, target, store.at[len(stores)]))
        stores[-1].start()

    for c in loads[:4]:
        c.wait()
    sub = iota((8, C), 0)
    extras = hs_ref[...].astype(F32).reshape(ROWS, 8, C)
    corners = hc_ref[...].astype(F32).reshape(4, 8, C)
    for i in range(ROWS):
        if i < 4:
            pieces = [hr_ref[b, i * BLK : (i + 1) * BLK, :] for b in range(NBLK)]
            extra = corners[i]
        else:
            pieces = [d_ref[b, (i - 4) * BLK : (i - 3) * BLK, :] for b in range(NBLK)]
            extra = extras[i - 4]
        v = pltpu.roll(jnp.concatenate(pieces, axis=0).astype(F32), 4, 0)
        head = jnp.where(sub < 4, pltpu.roll(extra, 4, 0), v[:8])
        out_ref[i] = low(jnp.concatenate([head, v[8:]], axis=0))

    keep(out_ref, out_hbm)
    loads[4].wait()
    scale = 1.0 / math.sqrt(ROWS * COLS * lax.axis_size("row") * lax.axis_size("col"))

    def full(i):
        return sum_ref[i * CP : (i + 1) * CP, :]

    def rest(i):
        return full(9 + i // 2)[:, 64 * (i % 2) : 64 * (i % 2) + 64]

    def square(i, r):
        return jnp.concatenate([full(i), rest(r)], axis=1)

    for t in range(9):
        conv_ref[t] = square(t, t).astype(F32)[:C, :C] * scale
    keep(conv_ref, conv_hbm)
    proj_ref[...] = nn(spread(CP, C, 1), jnp.concatenate([full(20), full(21)[:, :64]], axis=1))[:, :C] * scale
    keep(proj_ref, proj_hbm)
    fc2 = jnp.concatenate([full(14), full(15), full(16)], axis=1).astype(F32)
    fc2_ref[...] = fc2[:C, :FF] * scale
    keep(fc2_ref, fc2_hbm)
    fc1 = jnp.concatenate([full(17), full(18), full(19)], axis=1).astype(F32)
    fc1_ref[...] = fc1[:C, :FF] * scale
    keep(fc1_ref, fc1_hbm)
    qkv = jnp.concatenate([full(22), full(23), full(24), full(25), full(26)[:, :64]], axis=1)
    qkv_ref[...] = nn(qkv, spread(3 * CP, 3 * C, 0))[:C] * scale
    keep(qkv_ref, qkv_hbm)
    for c in stores:
        c.wait()


def call_results(d_shifted, halo, sums):
    operands = (d_shifted, *halo, sums)
    shapes = (
        jax.ShapeDtypeStruct((ROWS, COLS, C), BF),
        jax.ShapeDtypeStruct((C, 3 * C), F32),
        jax.ShapeDtypeStruct((C, C), F32),
        jax.ShapeDtypeStruct((C, FF), F32),
        jax.ShapeDtypeStruct((C, FF), F32),
        jax.ShapeDtypeStruct((9, C, C), F32),
    )
    return pl.pallas_call(
        results,
        out_shape=shapes,
        in_specs=[pl.BlockSpec(memory_space=pl.ANY)] * 5,
        out_specs=[pl.BlockSpec(memory_space=pl.ANY)] * 6,
        scratch_shapes=[
            *(VMEM(v.shape, v.dtype) for v in operands + shapes),
            pltpu.SemaphoreType.DMA((5,)),
            pltpu.SemaphoreType.DMA((6,)),
        ],
        compiler_params=pltpu.CompilerParams(vmem_limit_bytes=60 * 2**20),
        name="results",
    )(*operands)


def local(features, cotangent, w_qkv, w_proj, w_fc1, w_fc2, w_conv, gain_attn, gain_mlp, pos_table):
    d_shifted, sums, *halo = call_layer(
        features,
        cotangent,
        w_qkv,
        w_proj,
        w_fc1,
        w_fc2.T,
        w_conv,
        gain_attn.reshape(1, C),
        gain_mlp.reshape(1, C),
        pos_table.T,
    )
    d_features, qkv, proj, fc1, fc2, conv = call_results(d_shifted, halo, sums)
    return d_features, qkv, proj, fc1, fc2.T, conv


def solution(mesh):
    return jax.shard_map(
        local,
        mesh=mesh,
        in_specs=(P("row", "col", None), P("row", "col", None)) + (P(),) * 8,
        out_specs=(P("row", "col", None),) + (P(),) * 5,
        check_vma=False,
    )
```

```python
import math

import jax
import jax.numpy as jnp
from jax import lax
from jax.experimental import pallas as pl
from jax.experimental.pallas import tpu as pltpu
from jax.sharding import PartitionSpec as P

C = 180
CP = 192
HEADS = 6
HD = 30
HP = 32
FF = 360
WIN = 8
SHIFT = 4
ROWS = 32
COLS = 64
BLK = 16
NBLK = COLS // BLK
TOK = ROWS * BLK
PAIR = WIN * BLK
UT = TOK // 2
UNITS = 8
PAIRS = UT // PAIR
SIDE = 4
TILES = (14, 8, 6)
BASE = (0, TILES[0] * CP, (TILES[0] + TILES[1]) * CP)
GROWS = sum(TILES) * CP
HALVES = tuple(t * CP // 2 for t in TILES)
PARTS = tuple(h // 3 for h in HALVES)
SHARES = tuple(p // SIDE for p in PARTS)
BF = jnp.bfloat16
F32 = jnp.float32
MESH = pl.DeviceIdType.MESH
VMEM = pltpu.VMEM


def iota(shape, dim):
    return lax.broadcasted_iota(jnp.int32, shape, dim)


def nn(a, b):
    return lax.dot_general(a, b, (((1,), (0,)), ((), ())), preferred_element_type=F32)


def nt(a, b):
    return lax.dot_general(a, b, (((1,), (1,)), ((), ())), preferred_element_type=F32)


def low(a):
    return a.astype(BF)


def eye(rows, cols):
    return low(jnp.where(iota((rows, cols), 0) == iota((rows, cols), 1), 1.0, 0.0))


def spread(padded, plain, pad_dim):
    shape = (padded, plain) if pad_dim == 0 else (plain, padded)
    p = iota(shape, pad_dim)
    c = iota(shape, 1 - pad_dim)
    hit = ((p & (HP - 1)) < HD) & (c == (p >> 5) * HD + (p & (HP - 1)))
    return low(jnp.where(hit, 1.0, 0.0))


def column(gain_ref):
    wide = jnp.where(iota((CP, C), 0) == iota((CP, C), 1), gain_ref[...], 0.0)
    return jnp.sum(wide, axis=1, keepdims=True)


def moments(values):
    mean = jnp.sum(values[:C], axis=0, keepdims=True) * (1.0 / C)
    centred = values - mean
    inner = centred[:C]
    var = jnp.sum(inner * inner, axis=0, keepdims=True) * (1.0 / C)
    return centred, lax.rsqrt(var + 1e-05)


def norm_back(upstream, normed, inverse, gain):
    scaled = upstream * gain
    first = jnp.sum(scaled, axis=0, keepdims=True) * (1.0 / C)
    second = jnp.sum(scaled * normed, axis=0, keepdims=True) * (1.0 / C)
    return inverse * (scaled - first - normed * second)


def gelu_parts(x):
    u = jnp.abs(x) * math.sqrt(0.5)
    t = 1.0 / (1.0 + 0.3275911 * u)
    e = jnp.exp(-u * u)
    poly = t * (
        0.254829592
        + t * (-0.284496736 + t * (1.421413741 + t * (-1.453152027 + t * 1.061405429)))
    )
    tail = 0.5 * poly * e
    cdf = jnp.where(x >= 0.0, 1.0 - tail, tail)
    return cdf, e * (1.0 / math.sqrt(2.0 * math.pi))


def fold(scores, second):
    parts = scores.reshape(WIN, 2, WIN, PAIR)
    return jnp.where(second, parts[:, 1], parts[:, 0]).reshape(WIN * WIN, PAIR)


def unfold(probs, second):
    parts = probs.reshape(WIN, WIN, PAIR)
    zero = jnp.zeros_like(parts)
    both = jnp.stack([jnp.where(second, zero, parts), jnp.where(second, parts, zero)], axis=1)
    return low(both.reshape(PAIR, PAIR))


def two_heads(block):
    zero = jnp.zeros((HP, PAIR), BF)
    top = jnp.concatenate([block[:HP], zero], axis=1)
    return jnp.concatenate([top, jnp.concatenate([zero, block[HP:]], axis=1)], axis=0)


def own_heads(product):
    return jnp.concatenate([product[:HP, :PAIR], product[HP:, PAIR:]], axis=0)


def tn(a, b):
    return lax.dot_general(a, b, (((0,), (0,)), ((), ())), preferred_element_type=F32)


def layer(
    f_hbm, g_hbm, wqkv_hbm, wproj_hbm, w1_hbm, w2_hbm, wconv_hbm, g1_hbm, g2_hbm, pos_hbm,
    d_hbm, sum_hbm, hr_ref, hs_ref, hc_ref,
    f_ref, g_ref, wqkv_ref, wproj_ref, w1_ref, w2_ref, wconv_ref, g1_ref, g2_ref, pos_ref,
    d_ref, sum_ref,
    fr_ref, gr_ref, fstrip_ref, gstrip_ref, fcorner_ref, gcorner_ref,
    fstrip_in, gstrip_in, strip_out,
    grads_ref, core0, core1, held0, held1, first0, first1, first2, second0, second1, second2, third0, third1, third2,
    xs, gs, wqkvt, wqkvp, wprojt, wprojp, w1t, w1p, w2t, w2p, bias,
    s_norm1, s_inv1, s_n1, packed, attended, probs, s_norm2, s_inv2, s_n2, s_slope, s_hidden, s_z,
    dshift, s_dpre, s_dattn, dheads, dpacked, s_dmid,
    load, store, in_send, in_recv, out_send, out_recv, core_send, core_recv, send, recv,
):
    row, col = lax.axis_index("row"), lax.axis_index("col")
    n_row, n_col = lax.axis_size("row"), lax.axis_size("col")
    up, down = lax.rem(row + n_row - 1, n_row), lax.rem(row + 1, n_row)
    left, right = lax.rem(col + n_col - 1, n_col), lax.rem(col + 1, n_col)
    last_row, last_col = row == n_row - 1, col == n_col - 1
    factor = HD**-0.5
    core, z, y = lax.rem(row, 2), lax.rem(row // 2, SIDE), lax.rem(col, SIDE)
    x = (row // 8) * 2 + col // SIDE
    here = (x, y, z)

    def device(xyz, c):
        return ((xyz[0] // 2) * 8 + xyz[2] * 2 + c, lax.rem(xyz[0], 2) * SIDE + xyz[1])

    def along(axis, k, other):
        there = list(here)
        there[axis] = lax.rem(there[axis] + k, SIDE)
        return device(there, 1 - core if other else core)

    sibling = device(here, 1 - core)
    seven = [(k, other) for k in range(SIDE) for other in (0, 1) if k + other > 0]
    barrier = pltpu.get_barrier_semaphore()
    greeted = [sibling, (up, col), (row, left), (up, left), (down, col), (row, right)]
    greeted += [(down, right)]
    greeted += [along(axis, k, o) for axis in range(3) for k, o in seven if k > 0]
    for peer in greeted:
        pl.semaphore_signal(barrier, inc=1, device_id=peer, device_id_type=MESH)

    hbm = (f_hbm, g_hbm, wqkv_hbm, wproj_hbm, w1_hbm, w2_hbm, wconv_hbm, g1_hbm, g2_hbm, pos_hbm)
    own = (f_ref, g_ref, wqkv_ref, wproj_ref, w1_ref, w2_ref, wconv_ref, g1_ref, g2_ref, pos_ref)
    loads = [pltpu.make_async_copy(s, t, load.at[i]) for i, (s, t) in enumerate(zip(hbm, own))]
    for c in loads:
        c.start()
    started = []

    def copy(src, dst, s, r, peer):
        c = pltpu.make_async_remote_copy(
            src_ref=src, dst_ref=dst, send_sem=s, recv_sem=r, device_id=peer, device_id_type=MESH
        )
        c.start()
        started.append(c)
        return c

    loads[0].wait()
    fs = f_ref[:, 0:16, :].astype(F32)[:, 0:8, :].reshape(ROWS // 2, 2, 8, C)
    pairs = jnp.where(iota((ROWS // 2, 8, C), 1) < 4, fs[:, 0], pltpu.roll(fs[:, 1], 4, 1))
    fstrip_in[...] = low(pairs.reshape(ROWS * 4, C))
    pl.semaphore_wait(barrier, len(greeted))
    f_arriving = [
        copy(fstrip_in.at[0:16], fcorner_ref, in_send.at[0], in_recv.at[0], (up, left)),
        copy(fstrip_in, fstrip_ref, in_send.at[1], in_recv.at[1], (row, left)),
        copy(f_ref.at[0:4], fr_ref, in_send.at[2], in_recv.at[2], (up, col)),
    ]
    loads[1].wait()
    cs = g_ref[:, 0:16, :].astype(F32)[:, 0:8, :]
    gstrip_in[...] = low(cs.reshape(ROWS * 8, C))
    g_arriving = [
        copy(gstrip_in.at[0:48], gcorner_ref, in_send.at[3], in_recv.at[3], (up, left)),
        copy(gstrip_in, gstrip_ref, in_send.at[4], in_recv.at[4], (row, left)),
        copy(g_ref.at[0:5], gr_ref, in_send.at[5], in_recv.at[5], (up, col)),
    ]

    sub = iota((8, C), 0)
    keep0 = jnp.where((sub == 3) & last_col, 0.0, 1.0)
    keep2 = jnp.where((sub == 4) & last_col, 0.0, 1.0)
    LASTB = NBLK - 1

    def put(target, i, rolled):
        whole = low(rolled[: LASTB * BLK])
        for b in range(LASTB):
            target[b, i * BLK : (i + 1) * BLK, :] = whole[b * BLK : (b + 1) * BLK]

    def put_last(target, i, body, last):
        target[LASTB, i * BLK : (i + 1) * BLK, :] = low(jnp.concatenate([body, last], axis=0))

    def put_x(i, v):
        put(xs, i, pltpu.roll(v, 60, 0))

    def put_x_last(i, v, extra):
        r = pltpu.roll(v, 12, 0)
        put_last(xs, i, r[:8], jnp.where(sub < 4, r[8:], extra))

    def put_g(i, v):
        for k, turn in enumerate((59, 60, 61)):
            put(gs.at[k], i, pltpu.roll(v, turn, 0))

    def put_g_last(i, v, extra):
        for k, n in enumerate((5, 4, 3)):
            r = pltpu.roll(v, 16 - n, 0)
            last = jnp.where(sub < 8 - n, r[8:], pltpu.roll(extra, 8 - n, 0))
            if k != 1:
                last = last * (keep0, keep2)[k // 2]
            put_last(gs.at[k], i, r[:8], last)

    for i in range(ROWS - 4):
        put_x(i, f_ref[i + 4].astype(F32))
    for i in range(ROWS - 3):
        put_g(i, g_ref[i + 3].astype(F32))

    for c in loads[2:]:
        c.wait()
    pad = eye(CP, C)
    sel, sel_one = spread(3 * CP, 3 * C, 0), spread(CP, C, 0)
    wq = low(nn(pad, wqkv_ref[...]))
    wqkvt[...] = low(nt(sel, wq))
    wqkvp[...] = low(nt(wq, sel))
    turned = low(nt(pad, wproj_ref[...]))
    wprojt[...] = low(nt(turned, sel_one))
    wprojp[...] = low(nt(sel_one, turned))
    w1p[...] = low(nn(pad, w1_ref[...]))
    w1t[...] = low(nt(eye(FF, FF), w1p[...]))
    w2t[...] = low(nn(pad, w2_ref[...]))
    w2p[...] = low(nt(eye(FF, FF), w2t[...]))
    gain1, gain2 = column(g1_ref), column(g2_ref)

    table = pos_ref[...]
    high = low(table)
    mid = low(table - high.astype(F32))
    rest_piece = low(table - high.astype(F32) - mid.astype(F32))
    entry, place = iota((225, 15 * BLK), 0), iota((225, 15 * BLK), 1)
    for kc in range(WIN):
        hit = entry == (place >> 4) * 15 + (place & 7) - kc + 7
        pick = low(jnp.where(hit, 1.0, 0.0))
        line = nn(high, pick) + nn(mid, pick) + nn(rest_piece, pick)
        for h in range(HEADS):
            for kr in range(WIN):
                start = (WIN - 1 - kr) * BLK
                at = kr * WIN + kc
                bias[h, at : at + 1, :] = line[h : h + 1, start : start + PAIR]
    dshift[...] = jnp.zeros_like(dshift)

    def last_rows():
        f_arriving[2].wait_recv()
        for i in range(ROWS - 4, ROWS):
            put_x(i, fr_ref[i - 28].astype(F32))

    def last_block():
        f_arriving[1].wait_recv()
        f_arriving[0].wait_recv()
        quads = fstrip_ref[...].astype(F32).reshape(ROWS // 2, 8, C)
        corner = fcorner_ref[...].astype(F32).reshape(2, 8, C)

        def quad(source, i):
            return pltpu.roll(source[i // 2], 4, 0) if i % 2 == 0 else source[i // 2]

        for i in range(ROWS):
            if i < ROWS - 4:
                put_x_last(i, f_ref[i + 4, COLS - 16 :, :].astype(F32), quad(quads, i + 4))
            else:
                put_x_last(i, fr_ref[i - 28, COLS - 16 :, :].astype(F32), quad(corner, i - 28))

    lane = iota((1, PAIR), 1)
    second = ((lane >> 3) & 1) == 1
    k_sub, q_lane = iota((WIN * WIN, PAIR), 0), iota((WIN * WIN, PAIR), 1)
    rows_differ = ((k_sub >> 5) & 1) != ((q_lane >> 6) & 1)
    cols_differ = (((k_sub >> 2) & 1) != ((q_lane >> 2) & 1)) & (((q_lane >> 3) & 1) == 1)
    tok = iota((1, UT), 1) >> 4

    def place_of(u):
        t = u // 6
        return (1 - t) * (u % 3) + 3 * t, (1 - t) * (u // 3) + t * (u - 6)

    def lines(start, size):
        return pl.ds(start if isinstance(start, int) else pl.multiple_of(start, 16), size)

    def drops(half):
        return (tok == 27 - 16 * half) & last_row, (tok == 28 - 16 * half) & last_row

    def forward(*bs):
        at = [place_of(u) for u in bs]
        xv = [nt(pad, xs[b, lines(half * UT, UT), :]) for b, half in at]
        for b, x in zip(bs, xv):
            centred, inv1 = moments(x)
            normed1 = centred * inv1
            s_norm1[b] = normed1
            s_inv1[b] = inv1
            s_n1[b] = low(normed1 * gain1)
        for b in bs:
            packed[b] = low(nn(wqkvt[...], s_n1[b]))
        units = [(b, a, j) for b in bs for a in range(PAIRS) for j in range(HEADS // 2)]

        def part(b, third, a, j):
            top = third * CP + 64 * j
            return packed[b, top : top + 64, a * PAIR : (a + 1) * PAIR]

        scores = [tn(part(b, 1, a, j), two_heads(part(b, 0, a, j))) for b, a, j in units]
        soft = []
        for (b, a, j), score in zip(units, scores):
            block, half = place_of(b)
            row_flag = last_row & (half * PAIRS + a == ROWS // WIN - 1)
            col_flag = last_col & (block == NBLK - 1)
            mask = jnp.where((rows_differ & row_flag) | (cols_differ & col_flag), -100.0, 0.0)
            wide = []
            for s in range(2):
                sc = fold(score[:, s * PAIR : (s + 1) * PAIR], second)
                sc = sc * factor + bias[2 * j + s] + mask
                e = jnp.exp(sc - jnp.max(sc, axis=0, keepdims=True))
                p = e * (1.0 / jnp.sum(e, axis=0, keepdims=True))
                probs[b, a, 2 * j + s] = p
                wide.append(unfold(p, second))
            soft.append(jnp.concatenate(wide, axis=1))
        for (b, a, j), wide in zip(units, soft):
            o = nn(part(b, 2, a, j), wide)
            attended[b, 64 * j : 64 * j + 64, a * PAIR : (a + 1) * PAIR] = low(own_heads(o))

        middles = [x + nn(wprojt[...], attended[b]) for b, x in zip(bs, xv)]
        for b, middle in zip(bs, middles):
            centred2, inv2 = moments(middle)
            normed2 = centred2 * inv2
            s_norm2[b] = normed2
            s_inv2[b] = inv2
            s_n2[b] = low(normed2 * gain2)
        pres = [nn(w1t[...], s_n2[b]) for b in bs]
        for b, pre in zip(bs, pres):
            cdf, pdf = gelu_parts(pre)
            s_hidden[b] = low(pre * cdf)
            s_slope[b] = cdf + pre * pdf
        for b, (_, half), middle in zip(bs, at, middles):
            drop0, drop2 = drops(half)
            z = middle + nn(w2t[...], s_hidden[b])
            s_z[1, b] = low(z)
            s_z[0, b] = low(jnp.where(drop0, 0.0, z))
            s_z[2, b] = low(jnp.where(drop2, 0.0, z))

    forward(0, 1, 2)
    last_rows()
    last_block()
    forward(3, 4, 5, 6, 7)

    for c in g_arriving:
        c.wait_recv()
    for i in range(ROWS + 2):
        if i < ROWS - 3:
            extra = gstrip_ref[(i + 3) * 8 : (i + 4) * 8, :]
            put_g_last(i, g_ref[i + 3, COLS - 16 :, :].astype(F32), extra.astype(F32))
        else:
            k = i - ROWS + 3
            put_g(i, gr_ref[k].astype(F32))
            extra = gcorner_ref[k * 8 : (k + 1) * 8, :]
            put_g_last(i, gr_ref[k, COLS - 16 :, :].astype(F32), extra.astype(F32))

    def tap(b, dy, dx):
        return gs[dx, b, (2 - dy) * BLK : (2 - dy) * BLK + TOK, :]

    def halves(b):
        return (b, b + 3) if b < NBLK - 1 else (6, 7)

    def both(ref, b):
        return jnp.concatenate([ref[u] for u in halves(b)], axis=1)

    def over_blocks(term):
        total = term(0)
        for b in range(1, NBLK):
            total = total + term(b)
        return total

    def put_tile(place, tile):
        grads_ref[place * CP : (place + 1) * CP, :] = low(tile)

    def put_pair(place, left, right):
        put_tile(place, jnp.concatenate([left, right], axis=1))

    held_back = None
    for t in range(9):
        total = over_blocks(lambda b: nn(both(s_z.at[t // 3], b), tap(b, t // 3, t % 3)))
        put_tile(t, total[:, :128])
        narrow = jnp.concatenate([total[:, 128:], jnp.zeros((CP, 256 - 12 - C), F32)], axis=1)
        narrow = narrow[:, :64]
        if t % 2 == 0:
            held_back = narrow
        else:
            put_pair(9 + t // 2, held_back, narrow)
    put_pair(13, held_back, jnp.zeros((CP, 64), F32))
    steps = ((first0, second0, third0), (first1, second1, third1), (first2, second2, third2))
    staged = ((core0, held0), (core1, held1))
    flying = [{}, {}, {}]

    def rows(start, size):
        return pl.ds(pl.multiple_of(start, 16), size)

    def share_rows(g, c, p, share):
        at = BASE[g] + c * HALVES[g] + p * PARTS[g] + share * SHARES[g]
        return rows(at, SHARES[g])

    def part_rows(g, c, p):
        return rows(BASE[g] + c * HALVES[g] + p * PARTS[g], PARTS[g])

    def go_core(g):
        flying[g]["core"] = [
            copy(
                grads_ref.at[part_rows(g, 1 - core, p)],
                staged[g][0].at[p],
                core_send.at[g, p],
                core_recv.at[g, p],
                sibling,
            )
            for p in range(3)
        ]

    def go_first(g):
        if g < 2:
            flying[g]["first"] = []
            for p in range(3):
                flying[g]["core"][p].wait_recv()
                total = grads_ref[part_rows(g, core, p), :].astype(F32)
                staged[g][1][p] = low(total + staged[g][0][p].astype(F32))
                group = []
                for k in range(1, SIDE):
                    share = lax.rem(here[p] + k, SIDE)
                    group.append(
                        copy(
                            staged[g][1].at[p, rows(share * SHARES[g], SHARES[g])],
                            steps[g][0].at[p, k - 1],
                            send.at[g, 0, p, k - 1],
                            recv.at[g, 0, p, k - 1],
                            along(p, k, 0),
                        )
                    )
                flying[g]["first"].append(group)
            return
        flying[g]["first"] = [
            [
                copy(
                    grads_ref.at[
                        share_rows(g, 1 - core if o else core, p, lax.rem(here[p] + k, SIDE))
                    ],
                    steps[g][0].at[p, i],
                    send.at[g, 0, p, i],
                    recv.at[g, 0, p, i],
                    along(p, k, o),
                )
                for i, (k, o) in enumerate(seven)
            ]
            for p in range(3)
        ]

    def spread_out(g, p, step, source, axis):
        target = steps[g][step]
        target[p, here[axis]] = source
        return [
            copy(
                target.at[p, here[axis]],
                target.at[p, here[axis]],
                send.at[g, step, p, k - 1],
                recv.at[g, step, p, k - 1],
                along(axis, k, 0),
            )
            for k in range(1, SIDE)
        ]

    def gathered(copies, target, p):
        for c in copies:
            c.wait_recv()
        total = target[p, 0].astype(F32)
        for k in range(1, SIDE):
            total = total + target[p, k].astype(F32)
        return low(total)

    def go_second(g):
        flying[g]["second"] = []
        for p in range(3):
            if g < 2:
                total = staged[g][1][p, rows(here[p] * SHARES[g], SHARES[g]), :].astype(F32)
            else:
                total = grads_ref[share_rows(g, core, p, here[p]), :].astype(F32)
            for i in range(len(flying[g]["first"][p])):
                flying[g]["first"][p][i].wait_recv()
                total = total + steps[g][0][p, i].astype(F32)
            flying[g]["second"].append(spread_out(g, p, 1, low(total), (p + 1) % 3))

    def go_third(g):
        flying[g]["third"] = []
        for p in range(3):
            total = gathered(flying[g]["second"][p], steps[g][1], p)
            flying[g]["third"].append(spread_out(g, p, 2, total, (p + 2) % 3))

    def go_back(g):
        flying[g]["back"] = []
        partners = [(k, 0) for k in range(1, SIDE)] if g < 2 else seven
        for p in range(3):
            at = share_rows(g, core, p, here[p])
            sum_ref[at, :] = gathered(flying[g]["third"][p], steps[g][2], p)
            flying[g]["back"].append(
                [
                    copy(
                        sum_ref.at[at],
                        sum_ref.at[at],
                        send.at[g, 3, p, i],
                        recv.at[g, 3, p, i],
                        along(p, k, o),
                    )
                    for i, (k, o) in enumerate(partners)
                ]
            )

    def go_end(g):
        flying[g]["end"] = []
        for p in range(3):
            for c in flying[g]["back"][p]:
                c.wait_recv()
            if g < 2:
                at = part_rows(g, core, p)
                flying[g]["end"].append(
                    copy(
                        sum_ref.at[at],
                        sum_ref.at[at],
                        core_send.at[g, 3 + p],
                        core_recv.at[g, 3 + p],
                        sibling,
                    )
                )

    go_core(0)

    line = iota((1, TOK), 1) >> 4

    def conv_back(b):
        total = None
        for dy in range(3):
            part = None
            for dx in range(3):
                product = nt(wconv_ref[3 * dy + dx], tap(b, dy, dx))
                part = product if part is None else part + product
            if dy != 1:
                part = jnp.where((line == (27, 28)[dy // 2]) & last_row, 0.0, part)
            total = part if total is None else total + part
        for i, u in enumerate(halves(b)):
            dshift[u, :C, :] = low(total[:, i * UT : (i + 1) * UT])

    def back_to_heads(step, carry):
        bs = [4 * step + i for i in range(4)]
        d_pres = [low(nn(w2p[...], dshift[b]) * s_slope[b]) for b in bs]
        d_middles = []
        for b, d_pre in zip(bs, d_pres):
            s_dpre[b] = d_pre
            d_middle = dshift[b].astype(F32) + norm_back(
                nn(w1p[...], d_pre), s_norm2[b], s_inv2[b], gain2
            )
            s_dmid[b] = d_middle
            d_middles.append(low(d_middle))
        for b, d_attn in zip(bs, d_middles):
            s_dattn[b] = d_attn
            dheads[b] = low(nn(wprojp[...], d_attn))
        return carry

    conv_back(0)
    conv_back(1)
    go_first(0)
    conv_back(2)
    conv_back(3)
    lax.fori_loop(0, 2, back_to_heads, 0)
    go_second(0)

    fc2 = over_blocks(lambda b: nt(both(dshift, b), both(s_hidden, b)))
    fc1 = over_blocks(lambda b: nt(both(s_n2, b), both(s_dpre, b)))
    for place, total in ((14, fc2), (17, fc1)):
        put_tile(place, total[:, :128])
        put_tile(place + 1, total[:, 128:256])
        put_pair(place + 2, total[:, 256:], jnp.zeros((CP, 384 - FF), F32))
    proj = over_blocks(lambda b: nt(both(attended, b), both(s_dattn, b)))
    put_tile(20, proj[:, :128])
    put_pair(21, proj[:, 128:192], jnp.zeros((CP, 64), F32))
    go_core(1)

    def heads_back(step):
        units = [
            (u, a, j)
            for u in (2 * step, 2 * step + 1)
            for a in range(PAIRS)
            for j in range(HEADS // 2)
        ]

        def part(ref, u, third, a, j):
            top = third * CP + 64 * j
            return ref[u, top : top + 64, a * PAIR : (a + 1) * PAIR]

        d_probs = [
            tn(part(packed, u, 2, a, j), two_heads(part(dheads, u, 0, a, j))) for u, a, j in units
        ]
        wide = []
        for (u, a, j), d_prob in zip(units, d_probs):
            p_wide, s_wide = [], []
            for s in range(2):
                p = probs[u, a, 2 * j + s]
                dp = fold(d_prob[:, s * PAIR : (s + 1) * PAIR], second)
                ds = p * (dp - jnp.sum(p * dp, axis=0, keepdims=True)) * factor
                p_wide.append(unfold(p, second))
                s_wide.append(unfold(ds, second))
            wide.append((p_wide, s_wide))
        for (u, a, j), (p_wide, s_wide) in zip(units, wide):
            lanes = slice(a * PAIR, (a + 1) * PAIR)
            dv = nt(part(dheads, u, 0, a, j), jnp.concatenate(p_wide, axis=0))
            dq = nn(part(packed, u, 1, a, j), jnp.concatenate(s_wide, axis=1))
            dk = nt(part(packed, u, 0, a, j), jnp.concatenate(s_wide, axis=0))
            dpacked[u, 64 * j : 64 * j + 64, lanes] = low(own_heads(dq))
            dpacked[u, CP + 64 * j : CP + 64 * j + 64, lanes] = low(own_heads(dk))
            dpacked[u, 2 * CP + 64 * j : 2 * CP + 64 * j + 64, lanes] = low(own_heads(dv))

    heads_back(0)
    go_first(1)
    heads_back(1)
    heads_back(2)
    go_third(0)
    heads_back(3)
    qkv = over_blocks(lambda b: nt(both(s_n1, b), both(dpacked, b)))
    for i in range(4):
        put_tile(22 + i, qkv[:, i * 128 : (i + 1) * 128])
    put_pair(26, qkv[:, 512:576], jnp.zeros((CP, 64), F32))
    put_tile(27, jnp.zeros((CP, 128), F32))
    go_first(2)
    go_second(1)

    ones_pair = eye(PAIR, PAIR)

    def inputs_back(*us):
        d_ins = [
            s_dmid[u] + norm_back(nn(wqkvp[...], dpacked[u]), s_norm1[u], s_inv1[u], gain1)
            for u in us
        ]
        for u, d_in in zip(us, d_ins):
            b, half = place_of(u)
            d_low = low(d_in)
            for a in range(PAIRS):
                natural = nt(ones_pair, d_low[:, a * PAIR : (a + 1) * PAIR])
                at = half * UT + a * PAIR
                d_ref[b, at : at + PAIR, :] = low(natural[:, :C])

    inputs_back(6, 7)
    edge = d_ref[NBLK - 1].astype(F32).reshape(ROWS, 2, 8, C)[:, 1]
    strip_out[...] = low(edge.reshape(ROWS * 8, C))
    leaving = [
        copy(strip_out.at[224:256], hc_ref, out_send.at[2], out_recv.at[2], (down, right)),
        copy(strip_out, hs_ref, out_send.at[1], out_recv.at[1], (row, right)),
    ]
    inputs_back(3, 4, 5)
    inputs_back(0, 1, 2)
    leaving.append(
        copy(d_ref.at[:, 448:512, :], hr_ref, out_send.at[0], out_recv.at[0], (down, col))
    )
    stores = [pltpu.make_async_copy(d_ref, d_hbm, store.at[0])]
    stores[0].start()

    def keep(g):
        for c in flying[g]["end"]:
            c.wait_recv()
        at = slice(BASE[g], BASE[g] + TILES[g] * CP)
        stores.append(pltpu.make_async_copy(sum_ref.at[at], sum_hbm.at[at], store.at[1 + g]))
        stores[-1].start()

    go_back(0)
    go_second(2)
    go_third(1)
    go_end(0)
    go_third(2)
    go_back(1)
    keep(0)
    go_back(2)
    go_end(1)
    keep(1)
    go_end(2)
    keep(2)
    for c in leaving:
        c.wait_recv()
    for c in started:
        c.wait_send()
    for c in stores:
        c.wait()


def call_layer(features, cotangent, w_qkv, w_proj, w_fc1, w_fc2_t, w_conv, g1, g2, table):
    reductions = [VMEM((3, n, 128), BF) for n in PARTS[:2] * 2]
    for slots in (2 * SIDE - 1, SIDE, SIDE):
        reductions += [VMEM((3, slots, n, 128), BF) for n in SHARES]
    inputs = (features, cotangent, w_qkv, w_proj, w_fc1, w_fc2_t, w_conv, g1, g2, table)
    scratch = [VMEM(v.shape, v.dtype) for v in inputs]
    scratch += [
        VMEM((NBLK, TOK, C), BF),
        VMEM((GROWS, 128), BF),
        VMEM((4, COLS, C), BF),
        VMEM((5, COLS, C), BF),
        VMEM((ROWS * 4, C), BF),
        VMEM((ROWS * 8, C), BF),
        VMEM((16, C), BF),
        VMEM((48, C), BF),
        VMEM((ROWS * 4, C), BF),
        VMEM((ROWS * 8, C), BF),
        VMEM((256, C), BF),
        VMEM((GROWS, 128), BF),
        *reductions,
        VMEM((NBLK, TOK, C), BF),
        VMEM((3, NBLK, (ROWS + 2) * BLK, C), BF),
        VMEM((3 * CP, CP), BF),
        VMEM((CP, 3 * CP), BF),
        VMEM((CP, CP), BF),
        VMEM((CP, CP), BF),
        VMEM((FF, CP), BF),
        VMEM((CP, FF), BF),
        VMEM((CP, FF), BF),
        VMEM((FF, CP), BF),
        VMEM((HEADS, WIN * WIN, PAIR), F32),
        VMEM((UNITS, CP, UT), F32),
        VMEM((UNITS, 1, UT), F32),
        VMEM((UNITS, CP, UT), BF),
        VMEM((UNITS, 3 * CP, UT), BF),
        VMEM((UNITS, CP, UT), BF),
        VMEM((UNITS, PAIRS, HEADS, WIN * WIN, PAIR), F32),
        VMEM((UNITS, CP, UT), F32),
        VMEM((UNITS, 1, UT), F32),
        VMEM((UNITS, CP, UT), BF),
        VMEM((UNITS, FF, UT), F32),
        VMEM((UNITS, FF, UT), BF),
        VMEM((3, UNITS, CP, UT), BF),
        VMEM((UNITS, CP, UT), BF),
        VMEM((UNITS, FF, UT), BF),
        VMEM((UNITS, CP, UT), BF),
        VMEM((UNITS, CP, UT), BF),
        VMEM((UNITS, 3 * CP, UT), BF),
        VMEM((UNITS, CP, UT), F32),
        pltpu.SemaphoreType.DMA((10,)),
        pltpu.SemaphoreType.DMA((4,)),
        pltpu.SemaphoreType.DMA((6,)),
        pltpu.SemaphoreType.DMA((6,)),
        pltpu.SemaphoreType.DMA((3,)),
        pltpu.SemaphoreType.DMA((3,)),
        pltpu.SemaphoreType.DMA((2, 6)),
        pltpu.SemaphoreType.DMA((2, 6)),
        pltpu.SemaphoreType.DMA((3, 4, 3, 2 * SIDE - 1)),
        pltpu.SemaphoreType.DMA((3, 4, 3, 2 * SIDE - 1)),
    ]
    return pl.pallas_call(
        layer,
        out_shape=(
            jax.ShapeDtypeStruct((NBLK, TOK, C), BF),
            jax.ShapeDtypeStruct((GROWS, 128), BF),
            jax.ShapeDtypeStruct((NBLK, 64, C), BF),
            jax.ShapeDtypeStruct((256, C), BF),
            jax.ShapeDtypeStruct((32, C), BF),
        ),
        in_specs=[pl.BlockSpec(memory_space=pl.ANY)] * 10,
        out_specs=[pl.BlockSpec(memory_space=pl.ANY)] * 2 + [pl.BlockSpec(memory_space=VMEM)] * 3,
        scratch_shapes=scratch,
        compiler_params=pltpu.CompilerParams(
            collective_id=0, has_side_effects=True, vmem_limit_bytes=60 * 2**20
        ),
        name="layer",
    )(*inputs)


def results(
    d_hbm, hr_hbm, hs_hbm, hc_hbm, sum_hbm,
    out_hbm, qkv_hbm, proj_hbm, fc1_hbm, fc2_hbm, conv_hbm,
    d_ref, hr_ref, hs_ref, hc_ref, sum_ref,
    out_ref, qkv_ref, proj_ref, fc1_ref, fc2_ref, conv_ref, load, store,
):
    hbm = (hr_hbm, hs_hbm, hc_hbm, d_hbm, sum_hbm)
    own = (hr_ref, hs_ref, hc_ref, d_ref, sum_ref)
    loads = [pltpu.make_async_copy(s, t, load.at[i]) for i, (s, t) in enumerate(zip(hbm, own))]
    for c in loads:
        c.start()
    stores = []

    def keep(source, target):
        stores.append(pltpu.make_async_copy(source, target, store.at[len(stores)]))
        stores[-1].start()

    for c in loads[:4]:
        c.wait()
    sub = iota((8, C), 0)
    extras = hs_ref[...].astype(F32).reshape(ROWS, 8, C)
    corners = hc_ref[...].astype(F32).reshape(4, 8, C)
    for i in range(ROWS):
        if i < 4:
            pieces = [hr_ref[b, i * BLK : (i + 1) * BLK, :] for b in range(NBLK)]
            extra = corners[i]
        else:
            pieces = [d_ref[b, (i - 4) * BLK : (i - 3) * BLK, :] for b in range(NBLK)]
            extra = extras[i - 4]
        v = pltpu.roll(jnp.concatenate(pieces, axis=0).astype(F32), 4, 0)
        head = jnp.where(sub < 4, pltpu.roll(extra, 4, 0), v[:8])
        out_ref[i] = low(jnp.concatenate([head, v[8:]], axis=0))

    keep(out_ref, out_hbm)
    loads[4].wait()
    scale = 1.0 / math.sqrt(ROWS * COLS * lax.axis_size("row") * lax.axis_size("col"))

    def full(i):
        return sum_ref[i * CP : (i + 1) * CP, :]

    def rest(i):
        return full(9 + i // 2)[:, 64 * (i % 2) : 64 * (i % 2) + 64]

    def square(i, r):
        return jnp.concatenate([full(i), rest(r)], axis=1)

    for t in range(9):
        conv_ref[t] = square(t, t).astype(F32)[:C, :C] * scale
    keep(conv_ref, conv_hbm)
    proj_ref[...] = nn(spread(CP, C, 1), jnp.concatenate([full(20), full(21)[:, :64]], axis=1))[:, :C] * scale
    keep(proj_ref, proj_hbm)
    fc2 = jnp.concatenate([full(14), full(15), full(16)], axis=1).astype(F32)
    fc2_ref[...] = fc2[:C, :FF] * scale
    keep(fc2_ref, fc2_hbm)
    fc1 = jnp.concatenate([full(17), full(18), full(19)], axis=1).astype(F32)
    fc1_ref[...] = fc1[:C, :FF] * scale
    keep(fc1_ref, fc1_hbm)
    qkv = jnp.concatenate([full(22), full(23), full(24), full(25), full(26)[:, :64]], axis=1)
    qkv_ref[...] = nn(qkv, spread(3 * CP, 3 * C, 0))[:C] * scale
    keep(qkv_ref, qkv_hbm)
    for c in stores:
        c.wait()


def call_results(d_shifted, halo, sums):
    operands = (d_shifted, *halo, sums)
    shapes = (
        jax.ShapeDtypeStruct((ROWS, COLS, C), BF),
        jax.ShapeDtypeStruct((C, 3 * C), F32),
        jax.ShapeDtypeStruct((C, C), F32),
        jax.ShapeDtypeStruct((C, FF), F32),
        jax.ShapeDtypeStruct((C, FF), F32),
        jax.ShapeDtypeStruct((9, C, C), F32),
    )
    return pl.pallas_call(
        results,
        out_shape=shapes,
        in_specs=[pl.BlockSpec(memory_space=pl.ANY)] * 5,
        out_specs=[pl.BlockSpec(memory_space=pl.ANY)] * 6,
        scratch_shapes=[
            *(VMEM(v.shape, v.dtype) for v in operands + shapes),
            pltpu.SemaphoreType.DMA((5,)),
            pltpu.SemaphoreType.DMA((6,)),
        ],
        compiler_params=pltpu.CompilerParams(vmem_limit_bytes=60 * 2**20),
        name="results",
    )(*operands)


def local(features, cotangent, w_qkv, w_proj, w_fc1, w_fc2, w_conv, gain_attn, gain_mlp, pos_table):
    d_shifted, sums, *halo = call_layer(
        features,
        cotangent,
        w_qkv,
        w_proj,
        w_fc1,
        w_fc2.T,
        w_conv,
        gain_attn.reshape(1, C),
        gain_mlp.reshape(1, C),
        pos_table.T,
    )
    d_features, qkv, proj, fc1, fc2, conv = call_results(d_shifted, halo, sums)
    return d_features, qkv, proj, fc1, fc2.T, conv


def solution(mesh):
    return jax.shard_map(
        local,
        mesh=mesh,
        in_specs=(P("row", "col", None), P("row", "col", None)) + (P(),) * 8,
        out_specs=(P("row", "col", None),) + (P(),) * 5,
        check_vma=False,
    )
```

```python
import math

import jax
import jax.numpy as jnp
from jax import lax
from jax.experimental import pallas as pl
from jax.experimental.pallas import tpu as pltpu
from jax.sharding import PartitionSpec as P

C = 180
CP = 192
HEADS = 6
HD = 30
HP = 32
FF = 360
WIN = 8
SHIFT = 4
ROWS = 32
COLS = 64
BLK = 16
NBLK = COLS // BLK
TOK = ROWS * BLK
PAIR = WIN * BLK
UT = TOK // 2
UNITS = 8
PAIRS = UT // PAIR
SIDE = 4
TILES = (14, 8, 6)
BASE = (0, TILES[0] * CP, (TILES[0] + TILES[1]) * CP)
GROWS = sum(TILES) * CP
HALVES = tuple(t * CP // 2 for t in TILES)
PARTS = tuple(h // 3 for h in HALVES)
SHARES = tuple(p // SIDE for p in PARTS)
BF = jnp.bfloat16
F32 = jnp.float32
MESH = pl.DeviceIdType.MESH
VMEM = pltpu.VMEM


def iota(shape, dim):
    return lax.broadcasted_iota(jnp.int32, shape, dim)


def nn(a, b):
    return lax.dot_general(a, b, (((1,), (0,)), ((), ())), preferred_element_type=F32)


def nt(a, b):
    return lax.dot_general(a, b, (((1,), (1,)), ((), ())), preferred_element_type=F32)


def low(a):
    return a.astype(BF)


def eye(rows, cols):
    return low(jnp.where(iota((rows, cols), 0) == iota((rows, cols), 1), 1.0, 0.0))


def spread(padded, plain, pad_dim):
    shape = (padded, plain) if pad_dim == 0 else (plain, padded)
    p = iota(shape, pad_dim)
    c = iota(shape, 1 - pad_dim)
    hit = ((p & (HP - 1)) < HD) & (c == (p >> 5) * HD + (p & (HP - 1)))
    return low(jnp.where(hit, 1.0, 0.0))


def column(gain_ref):
    wide = jnp.where(iota((CP, C), 0) == iota((CP, C), 1), gain_ref[...], 0.0)
    return jnp.sum(wide, axis=1, keepdims=True)


def moments(values):
    mean = jnp.sum(values[:C], axis=0, keepdims=True) * (1.0 / C)
    centred = values - mean
    inner = centred[:C]
    var = jnp.sum(inner * inner, axis=0, keepdims=True) * (1.0 / C)
    return centred, lax.rsqrt(var + 1e-05)


def norm_back(upstream, normed, inverse, gain):
    scaled = upstream * gain
    first = jnp.sum(scaled, axis=0, keepdims=True) * (1.0 / C)
    second = jnp.sum(scaled * normed, axis=0, keepdims=True) * (1.0 / C)
    return inverse * (scaled - first - normed * second)


def gelu_parts(x):
    u = jnp.abs(x) * math.sqrt(0.5)
    t = 1.0 / (1.0 + 0.3275911 * u)
    e = jnp.exp(-u * u)
    poly = t * (
        0.254829592
        + t * (-0.284496736 + t * (1.421413741 + t * (-1.453152027 + t * 1.061405429)))
    )
    tail = 0.5 * poly * e
    cdf = jnp.where(x >= 0.0, 1.0 - tail, tail)
    return cdf, e * (1.0 / math.sqrt(2.0 * math.pi))


def fold(scores, second):
    parts = scores.reshape(WIN, 2, WIN, PAIR)
    return jnp.where(second, parts[:, 1], parts[:, 0]).reshape(WIN * WIN, PAIR)


def unfold(probs, second):
    parts = probs.reshape(WIN, WIN, PAIR)
    zero = jnp.zeros_like(parts)
    both = jnp.stack([jnp.where(second, zero, parts), jnp.where(second, parts, zero)], axis=1)
    return low(both.reshape(PAIR, PAIR))


def two_heads(block):
    zero = jnp.zeros((HP, PAIR), BF)
    top = jnp.concatenate([block[:HP], zero], axis=1)
    return jnp.concatenate([top, jnp.concatenate([zero, block[HP:]], axis=1)], axis=0)


def own_heads(product):
    return jnp.concatenate([product[:HP, :PAIR], product[HP:, PAIR:]], axis=0)


def tn(a, b):
    return lax.dot_general(a, b, (((0,), (0,)), ((), ())), preferred_element_type=F32)


def layer(
    f_hbm, g_hbm, wqkv_hbm, wproj_hbm, w1_hbm, w2_hbm, wconv_hbm, g1_hbm, g2_hbm, pos_hbm,
    d_hbm, sum_hbm, hr_ref, hs_ref, hc_ref,
    f_ref, g_ref, wqkv_ref, wproj_ref, w1_ref, w2_ref, wconv_ref, g1_ref, g2_ref, pos_ref,
    d_ref, sum_ref,
    fr_ref, gr_ref, fstrip_ref, gstrip_ref, fcorner_ref, gcorner_ref,
    fstrip_in, gstrip_in, strip_out,
    grads_ref, core0, core1, held0, held1, first0, first1, first2, second0, second1, second2, third0, third1, third2,
    xs, gs, wqkvt, wqkvp, wprojt, wprojp, w1t, w1p, w2t, w2p, bias,
    s_norm1, s_inv1, s_n1, packed, attended, probs, s_norm2, s_inv2, s_n2, s_slope, s_hidden, s_z,
    dshift, s_dpre, s_dattn, dheads, dpacked, s_dmid,
    load, store, in_send, in_recv, out_send, out_recv, core_send, core_recv, send, recv,
):
    row, col = lax.axis_index("row"), lax.axis_index("col")
    n_row, n_col = lax.axis_size("row"), lax.axis_size("col")
    up, down = lax.rem(row + n_row - 1, n_row), lax.rem(row + 1, n_row)
    left, right = lax.rem(col + n_col - 1, n_col), lax.rem(col + 1, n_col)
    last_row, last_col = row == n_row - 1, col == n_col - 1
    factor = HD**-0.5
    core, z, y = lax.rem(row, 2), lax.rem(row // 2, SIDE), lax.rem(col, SIDE)
    x = (row // 8) * 2 + col // SIDE
    here = (x, y, z)

    def device(xyz, c):
        return ((xyz[0] // 2) * 8 + xyz[2] * 2 + c, lax.rem(xyz[0], 2) * SIDE + xyz[1])

    def along(axis, k, other):
        there = list(here)
        there[axis] = lax.rem(there[axis] + k, SIDE)
        return device(there, 1 - core if other else core)

    sibling = device(here, 1 - core)
    seven = [(k, other) for k in range(SIDE) for other in (0, 1) if k + other > 0]
    barrier = pltpu.get_barrier_semaphore()
    greeted = [sibling, (up, col), (row, left), (up, left), (down, col), (row, right)]
    greeted += [(down, right)]
    greeted += [along(axis, k, o) for axis in range(3) for k, o in seven if k > 0]
    for peer in greeted:
        pl.semaphore_signal(barrier, inc=1, device_id=peer, device_id_type=MESH)

    hbm = (f_hbm, g_hbm, wqkv_hbm, wproj_hbm, w1_hbm, w2_hbm, wconv_hbm, g1_hbm, g2_hbm, pos_hbm)
    own = (f_ref, g_ref, wqkv_ref, wproj_ref, w1_ref, w2_ref, wconv_ref, g1_ref, g2_ref, pos_ref)
    loads = [pltpu.make_async_copy(s, t, load.at[i]) for i, (s, t) in enumerate(zip(hbm, own))]
    for c in loads:
        c.start()
    started = []

    def copy(src, dst, s, r, peer):
        c = pltpu.make_async_remote_copy(
            src_ref=src, dst_ref=dst, send_sem=s, recv_sem=r, device_id=peer, device_id_type=MESH
        )
        c.start()
        started.append(c)
        return c

    loads[0].wait()
    fs = f_ref[:, 0:16, :].astype(F32)[:, 0:8, :].reshape(ROWS // 2, 2, 8, C)
    pairs = jnp.where(iota((ROWS // 2, 8, C), 1) < 4, fs[:, 0], pltpu.roll(fs[:, 1], 4, 1))
    fstrip_in[...] = low(pairs.reshape(ROWS * 4, C))
    pl.semaphore_wait(barrier, len(greeted))
    f_arriving = [
        copy(fstrip_in.at[0:16], fcorner_ref, in_send.at[0], in_recv.at[0], (up, left)),
        copy(fstrip_in, fstrip_ref, in_send.at[1], in_recv.at[1], (row, left)),
        copy(f_ref.at[0:4], fr_ref, in_send.at[2], in_recv.at[2], (up, col)),
    ]
    loads[1].wait()
    cs = g_ref[:, 0:16, :].astype(F32)[:, 0:8, :]
    gstrip_in[...] = low(cs.reshape(ROWS * 8, C))
    g_arriving = [
        copy(gstrip_in.at[0:48], gcorner_ref, in_send.at[3], in_recv.at[3], (up, left)),
        copy(gstrip_in, gstrip_ref, in_send.at[4], in_recv.at[4], (row, left)),
        copy(g_ref.at[0:5], gr_ref, in_send.at[5], in_recv.at[5], (up, col)),
    ]

    sub = iota((8, C), 0)
    keep0 = jnp.where((sub == 3) & last_col, 0.0, 1.0)
    keep2 = jnp.where((sub == 4) & last_col, 0.0, 1.0)
    LASTB = NBLK - 1

    def put(target, i, rolled):
        whole = low(rolled[: LASTB * BLK])
        for b in range(LASTB):
            target[b, i * BLK : (i + 1) * BLK, :] = whole[b * BLK : (b + 1) * BLK]

    def put_last(target, i, body, last):
        target[LASTB, i * BLK : (i + 1) * BLK, :] = low(jnp.concatenate([body, last], axis=0))

    def put_x(i, v):
        put(xs, i, pltpu.roll(v, 60, 0))

    def put_x_last(i, v, extra):
        r = pltpu.roll(v, 12, 0)
        put_last(xs, i, r[:8], jnp.where(sub < 4, r[8:], extra))

    def put_g(i, v):
        for k, turn in enumerate((59, 60, 61)):
            put(gs.at[k], i, pltpu.roll(v, turn, 0))

    def put_g_last(i, v, extra):
        for k, n in enumerate((5, 4, 3)):
            r = pltpu.roll(v, 16 - n, 0)
            last = jnp.where(sub < 8 - n, r[8:], pltpu.roll(extra, 8 - n, 0))
            if k != 1:
                last = last * (keep0, keep2)[k // 2]
            put_last(gs.at[k], i, r[:8], last)

    for i in range(ROWS - 4):
        put_x(i, f_ref[i + 4].astype(F32))
    for i in range(ROWS - 3):
        put_g(i, g_ref[i + 3].astype(F32))

    for c in loads[2:]:
        c.wait()
    pad = eye(CP, C)
    sel, sel_one = spread(3 * CP, 3 * C, 0), spread(CP, C, 0)
    wq = low(nn(pad, wqkv_ref[...]))
    wqkvt[...] = low(nt(sel, wq))
    wqkvp[...] = low(nt(wq, sel))
    turned = low(nt(pad, wproj_ref[...]))
    wprojt[...] = low(nt(turned, sel_one))
    wprojp[...] = low(nt(sel_one, turned))
    w1p[...] = low(nn(pad, w1_ref[...]))
    w1t[...] = low(nt(eye(FF, FF), w1p[...]))
    w2t[...] = low(nn(pad, w2_ref[...]))
    w2p[...] = low(nt(eye(FF, FF), w2t[...]))
    gain1, gain2 = column(g1_ref), column(g2_ref)

    table = pos_ref[...]
    high = low(table)
    mid = low(table - high.astype(F32))
    rest_piece = low(table - high.astype(F32) - mid.astype(F32))
    entry, place = iota((225, 15 * BLK), 0), iota((225, 15 * BLK), 1)
    for kc in range(WIN):
        hit = entry == (place >> 4) * 15 + (place & 7) - kc + 7
        pick = low(jnp.where(hit, 1.0, 0.0))
        line = nn(high, pick) + nn(mid, pick) + nn(rest_piece, pick)
        for h in range(HEADS):
            for kr in range(WIN):
                start = (WIN - 1 - kr) * BLK
                at = kr * WIN + kc
                bias[h, at : at + 1, :] = line[h : h + 1, start : start + PAIR]
    dshift[...] = jnp.zeros_like(dshift)

    def last_rows():
        f_arriving[2].wait_recv()
        for i in range(ROWS - 4, ROWS):
            put_x(i, fr_ref[i - 28].astype(F32))

    def last_block():
        f_arriving[1].wait_recv()
        f_arriving[0].wait_recv()
        quads = fstrip_ref[...].astype(F32).reshape(ROWS // 2, 8, C)
        corner = fcorner_ref[...].astype(F32).reshape(2, 8, C)

        def quad(source, i):
            return pltpu.roll(source[i // 2], 4, 0) if i % 2 == 0 else source[i // 2]

        for i in range(ROWS):
            if i < ROWS - 4:
                put_x_last(i, f_ref[i + 4, COLS - 16 :, :].astype(F32), quad(quads, i + 4))
            else:
                put_x_last(i, fr_ref[i - 28, COLS - 16 :, :].astype(F32), quad(corner, i - 28))

    lane = iota((1, PAIR), 1)
    second = ((lane >> 3) & 1) == 1
    k_sub, q_lane = iota((WIN * WIN, PAIR), 0), iota((WIN * WIN, PAIR), 1)
    rows_differ = ((k_sub >> 5) & 1) != ((q_lane >> 6) & 1)
    cols_differ = (((k_sub >> 2) & 1) != ((q_lane >> 2) & 1)) & (((q_lane >> 3) & 1) == 1)
    tok = iota((1, UT), 1) >> 4

    def place_of(u):
        t = u // 6
        return (1 - t) * (u % 3) + 3 * t, (1 - t) * (u // 3) + t * (u - 6)

    def lines(start, size):
        return pl.ds(start if isinstance(start, int) else pl.multiple_of(start, 16), size)

    def drops(half):
        return (tok == 27 - 16 * half) & last_row, (tok == 28 - 16 * half) & last_row

    def forward(*bs):
        at = [place_of(u) for u in bs]
        xv = [nt(pad, xs[b, lines(half * UT, UT), :]) for b, half in at]
        for b, x in zip(bs, xv):
            centred, inv1 = moments(x)
            normed1 = centred * inv1
            s_norm1[b] = normed1
            s_inv1[b] = inv1
            s_n1[b] = low(normed1 * gain1)
        for b in bs:
            packed[b] = low(nn(wqkvt[...], s_n1[b]))
        units = [(b, a, j) for b in bs for a in range(PAIRS) for j in range(HEADS // 2)]

        def part(b, third, a, j):
            top = third * CP + 64 * j
            return packed[b, top : top + 64, a * PAIR : (a + 1) * PAIR]

        scores = [tn(part(b, 1, a, j), two_heads(part(b, 0, a, j))) for b, a, j in units]
        soft = []
        for (b, a, j), score in zip(units, scores):
            block, half = place_of(b)
            row_flag = last_row & (half * PAIRS + a == ROWS // WIN - 1)
            col_flag = last_col & (block == NBLK - 1)
            mask = jnp.where((rows_differ & row_flag) | (cols_differ & col_flag), -100.0, 0.0)
            wide = []
            for s in range(2):
                sc = fold(score[:, s * PAIR : (s + 1) * PAIR], second)
                sc = sc * factor + bias[2 * j + s] + mask
                e = jnp.exp(sc - jnp.max(sc, axis=0, keepdims=True))
                p = e * (1.0 / jnp.sum(e, axis=0, keepdims=True))
                probs[b, a, 2 * j + s] = p
                wide.append(unfold(p, second))
            soft.append(jnp.concatenate(wide, axis=1))
        for (b, a, j), wide in zip(units, soft):
            o = nn(part(b, 2, a, j), wide)
            attended[b, 64 * j : 64 * j + 64, a * PAIR : (a + 1) * PAIR] = low(own_heads(o))

        middles = [x + nn(wprojt[...], attended[b]) for b, x in zip(bs, xv)]
        for b, middle in zip(bs, middles):
            centred2, inv2 = moments(middle)
            normed2 = centred2 * inv2
            s_norm2[b] = normed2
            s_inv2[b] = inv2
            s_n2[b] = low(normed2 * gain2)
        pres = [nn(w1t[...], s_n2[b]) for b in bs]
        for b, pre in zip(bs, pres):
            cdf, pdf = gelu_parts(pre)
            s_hidden[b] = low(pre * cdf)
            s_slope[b] = cdf + pre * pdf
        for b, (_, half), middle in zip(bs, at, middles):
            drop0, drop2 = drops(half)
            z = middle + nn(w2t[...], s_hidden[b])
            s_z[1, b] = low(z)
            s_z[0, b] = low(jnp.where(drop0, 0.0, z))
            s_z[2, b] = low(jnp.where(drop2, 0.0, z))

    forward(0, 1, 2)
    last_rows()
    last_block()
    forward(3, 4, 5, 6, 7)

    for c in g_arriving:
        c.wait_recv()
    for i in range(ROWS + 2):
        if i < ROWS - 3:
            extra = gstrip_ref[(i + 3) * 8 : (i + 4) * 8, :]
            put_g_last(i, g_ref[i + 3, COLS - 16 :, :].astype(F32), extra.astype(F32))
        else:
            k = i - ROWS + 3
            put_g(i, gr_ref[k].astype(F32))
            extra = gcorner_ref[k * 8 : (k + 1) * 8, :]
            put_g_last(i, gr_ref[k, COLS - 16 :, :].astype(F32), extra.astype(F32))

    def tap(b, dy, dx):
        return gs[dx, b, (2 - dy) * BLK : (2 - dy) * BLK + TOK, :]

    def halves(b):
        return (b, b + 3) if b < NBLK - 1 else (6, 7)

    def both(ref, b):
        return jnp.concatenate([ref[u] for u in halves(b)], axis=1)

    def over_blocks(term):
        total = term(0)
        for b in range(1, NBLK):
            total = total + term(b)
        return total

    def put_tile(place, tile):
        grads_ref[place * CP : (place + 1) * CP, :] = low(tile)

    def put_pair(place, left, right):
        put_tile(place, jnp.concatenate([left, right], axis=1))

    held_back = None
    for t in range(9):
        total = over_blocks(lambda b: nn(both(s_z.at[t // 3], b), tap(b, t // 3, t % 3)))
        put_tile(t, total[:, :128])
        narrow = jnp.concatenate([total[:, 128:], jnp.zeros((CP, 256 - 12 - C), F32)], axis=1)
        narrow = narrow[:, :64]
        if t % 2 == 0:
            held_back = narrow
        else:
            put_pair(9 + t // 2, held_back, narrow)
    put_pair(13, held_back, jnp.zeros((CP, 64), F32))
    steps = ((first0, second0, third0), (first1, second1, third1), (first2, second2, third2))
    staged = ((core0, held0), (core1, held1))
    flying = [{}, {}, {}]

    def rows(start, size):
        return pl.ds(pl.multiple_of(start, 16), size)

    def share_rows(g, c, p, share):
        at = BASE[g] + c * HALVES[g] + p * PARTS[g] + share * SHARES[g]
        return rows(at, SHARES[g])

    def part_rows(g, c, p):
        return rows(BASE[g] + c * HALVES[g] + p * PARTS[g], PARTS[g])

    def go_core(g):
        flying[g]["core"] = [
            copy(
                grads_ref.at[part_rows(g, 1 - core, p)],
                staged[g][0].at[p],
                core_send.at[g, p],
                core_recv.at[g, p],
                sibling,
            )
            for p in range(3)
        ]

    def go_first(g):
        if g < 2:
            flying[g]["first"] = []
            for p in range(3):
                flying[g]["core"][p].wait_recv()
                total = grads_ref[part_rows(g, core, p), :].astype(F32)
                staged[g][1][p] = low(total + staged[g][0][p].astype(F32))
                group = []
                for k in range(1, SIDE):
                    share = lax.rem(here[p] + k, SIDE)
                    group.append(
                        copy(
                            staged[g][1].at[p, rows(share * SHARES[g], SHARES[g])],
                            steps[g][0].at[p, k - 1],
                            send.at[g, 0, p, k - 1],
                            recv.at[g, 0, p, k - 1],
                            along(p, k, 0),
                        )
                    )
                flying[g]["first"].append(group)
            return
        flying[g]["first"] = [
            [
                copy(
                    grads_ref.at[
                        share_rows(g, 1 - core if o else core, p, lax.rem(here[p] + k, SIDE))
                    ],
                    steps[g][0].at[p, i],
                    send.at[g, 0, p, i],
                    recv.at[g, 0, p, i],
                    along(p, k, o),
                )
                for i, (k, o) in enumerate(seven)
            ]
            for p in range(3)
        ]

    def spread_out(g, p, step, source, axis):
        target = steps[g][step]
        target[p, here[axis]] = source
        return [
            copy(
                target.at[p, here[axis]],
                target.at[p, here[axis]],
                send.at[g, step, p, k - 1],
                recv.at[g, step, p, k - 1],
                along(axis, k, 0),
            )
            for k in range(1, SIDE)
        ]

    def gathered(copies, target, p):
        for c in copies:
            c.wait_recv()
        total = target[p, 0].astype(F32)
        for k in range(1, SIDE):
            total = total + target[p, k].astype(F32)
        return low(total)

    def go_second(g):
        flying[g]["second"] = []
        for p in range(3):
            if g < 2:
                total = staged[g][1][p, rows(here[p] * SHARES[g], SHARES[g]), :].astype(F32)
            else:
                total = grads_ref[share_rows(g, core, p, here[p]), :].astype(F32)
            for i in range(len(flying[g]["first"][p])):
                flying[g]["first"][p][i].wait_recv()
                total = total + steps[g][0][p, i].astype(F32)
            flying[g]["second"].append(spread_out(g, p, 1, low(total), (p + 1) % 3))

    def go_third(g):
        flying[g]["third"] = []
        for p in range(3):
            total = gathered(flying[g]["second"][p], steps[g][1], p)
            flying[g]["third"].append(spread_out(g, p, 2, total, (p + 2) % 3))

    def go_back(g):
        flying[g]["back"] = []
        partners = [(k, 0) for k in range(1, SIDE)] if g < 2 else seven
        for p in range(3):
            at = share_rows(g, core, p, here[p])
            sum_ref[at, :] = gathered(flying[g]["third"][p], steps[g][2], p)
            flying[g]["back"].append(
                [
                    copy(
                        sum_ref.at[at],
                        sum_ref.at[at],
                        send.at[g, 3, p, i],
                        recv.at[g, 3, p, i],
                        along(p, k, o),
                    )
                    for i, (k, o) in enumerate(partners)
                ]
            )

    def go_end(g):
        flying[g]["end"] = []
        for p in range(3):
            for c in flying[g]["back"][p]:
                c.wait_recv()
            if g < 2:
                at = part_rows(g, core, p)
                flying[g]["end"].append(
                    copy(
                        sum_ref.at[at],
                        sum_ref.at[at],
                        core_send.at[g, 3 + p],
                        core_recv.at[g, 3 + p],
                        sibling,
                    )
                )

    go_core(0)

    line = iota((1, TOK), 1) >> 4

    def conv_back(b):
        total = None
        for dy in range(3):
            part = None
            for dx in range(3):
                product = nt(wconv_ref[3 * dy + dx], tap(b, dy, dx))
                part = product if part is None else part + product
            if dy != 1:
                part = jnp.where((line == (27, 28)[dy // 2]) & last_row, 0.0, part)
            total = part if total is None else total + part
        for i, u in enumerate(halves(b)):
            dshift[u, :C, :] = low(total[:, i * UT : (i + 1) * UT])

    def back_to_heads(step, carry):
        bs = [4 * step + i for i in range(4)]
        d_pres = [low(nn(w2p[...], dshift[b]) * s_slope[b]) for b in bs]
        d_middles = []
        for b, d_pre in zip(bs, d_pres):
            s_dpre[b] = d_pre
            d_middle = dshift[b].astype(F32) + norm_back(
                nn(w1p[...], d_pre), s_norm2[b], s_inv2[b], gain2
            )
            s_dmid[b] = d_middle
            d_middles.append(low(d_middle))
        for b, d_attn in zip(bs, d_middles):
            s_dattn[b] = d_attn
            dheads[b] = low(nn(wprojp[...], d_attn))
        return carry

    for b in range(NBLK):
        conv_back(b)
    go_first(0)
    lax.fori_loop(0, 2, back_to_heads, 0)

    fc2 = over_blocks(lambda b: nt(both(dshift, b), both(s_hidden, b)))
    fc1 = over_blocks(lambda b: nt(both(s_n2, b), both(s_dpre, b)))
    for place, total in ((14, fc2), (17, fc1)):
        put_tile(place, total[:, :128])
        put_tile(place + 1, total[:, 128:256])
        put_pair(place + 2, total[:, 256:], jnp.zeros((CP, 384 - FF), F32))
    proj = over_blocks(lambda b: nt(both(attended, b), both(s_dattn, b)))
    put_tile(20, proj[:, :128])
    put_pair(21, proj[:, 128:192], jnp.zeros((CP, 64), F32))
    go_core(1)

    def heads_back(step):
        units = [
            (u, a, j)
            for u in (2 * step, 2 * step + 1)
            for a in range(PAIRS)
            for j in range(HEADS // 2)
        ]

        def part(ref, u, third, a, j):
            top = third * CP + 64 * j
            return ref[u, top : top + 64, a * PAIR : (a + 1) * PAIR]

        d_probs = [
            tn(part(packed, u, 2, a, j), two_heads(part(dheads, u, 0, a, j))) for u, a, j in units
        ]
        wide = []
        for (u, a, j), d_prob in zip(units, d_probs):
            p_wide, s_wide = [], []
            for s in range(2):
                p = probs[u, a, 2 * j + s]
                dp = fold(d_prob[:, s * PAIR : (s + 1) * PAIR], second)
                ds = p * (dp - jnp.sum(p * dp, axis=0, keepdims=True)) * factor
                p_wide.append(unfold(p, second))
                s_wide.append(unfold(ds, second))
            wide.append((p_wide, s_wide))
        for (u, a, j), (p_wide, s_wide) in zip(units, wide):
            lanes = slice(a * PAIR, (a + 1) * PAIR)
            dv = nt(part(dheads, u, 0, a, j), jnp.concatenate(p_wide, axis=0))
            dq = nn(part(packed, u, 1, a, j), jnp.concatenate(s_wide, axis=1))
            dk = nt(part(packed, u, 0, a, j), jnp.concatenate(s_wide, axis=0))
            dpacked[u, 64 * j : 64 * j + 64, lanes] = low(own_heads(dq))
            dpacked[u, CP + 64 * j : CP + 64 * j + 64, lanes] = low(own_heads(dk))
            dpacked[u, 2 * CP + 64 * j : 2 * CP + 64 * j + 64, lanes] = low(own_heads(dv))

    heads_back(0)
    go_second(0)
    heads_back(1)
    go_first(1)
    heads_back(2)
    heads_back(3)
    qkv = over_blocks(lambda b: nt(both(s_n1, b), both(dpacked, b)))
    for i in range(4):
        put_tile(22 + i, qkv[:, i * 128 : (i + 1) * 128])
    put_pair(26, qkv[:, 512:576], jnp.zeros((CP, 64), F32))
    put_tile(27, jnp.zeros((CP, 128), F32))
    go_first(2)
    go_third(0)

    ones_pair = eye(PAIR, PAIR)

    def inputs_back(*us):
        d_ins = [
            s_dmid[u] + norm_back(nn(wqkvp[...], dpacked[u]), s_norm1[u], s_inv1[u], gain1)
            for u in us
        ]
        for u, d_in in zip(us, d_ins):
            b, half = place_of(u)
            d_low = low(d_in)
            for a in range(PAIRS):
                natural = nt(ones_pair, d_low[:, a * PAIR : (a + 1) * PAIR])
                at = half * UT + a * PAIR
                d_ref[b, at : at + PAIR, :] = low(natural[:, :C])

    inputs_back(6, 7)
    edge = d_ref[NBLK - 1].astype(F32).reshape(ROWS // 2, 2, 2, 8, C)[:, :, 1]
    pairs = jnp.where(
        iota((ROWS // 2, 8, C), 1) < 4, pltpu.roll(edge[:, 0], 4, 1), edge[:, 1]
    )
    strip_out[...] = low(pairs.reshape(ROWS * 4, C))
    leaving = [
        copy(strip_out.at[112:128], hc_ref, out_send.at[2], out_recv.at[2], (down, right)),
        copy(strip_out, hs_ref, out_send.at[1], out_recv.at[1], (row, right)),
    ]
    go_second(1)
    inputs_back(3, 4, 5)
    inputs_back(0, 1, 2)
    leaving.append(
        copy(d_ref.at[:, 448:512, :], hr_ref, out_send.at[0], out_recv.at[0], (down, col))
    )
    stores = [pltpu.make_async_copy(d_ref, d_hbm, store.at[0])]
    stores[0].start()

    def keep(g):
        for c in flying[g]["end"]:
            c.wait_recv()
        at = slice(BASE[g], BASE[g] + TILES[g] * CP)
        stores.append(pltpu.make_async_copy(sum_ref.at[at], sum_hbm.at[at], store.at[1 + g]))
        stores[-1].start()

    go_second(2)
    go_back(0)
    go_third(1)
    go_third(2)
    go_end(0)
    go_back(1)
    go_back(2)
    keep(0)
    go_end(1)
    go_end(2)
    keep(1)
    keep(2)
    for c in leaving:
        c.wait_recv()
    for c in started:
        c.wait_send()
    for c in stores:
        c.wait()


def call_layer(features, cotangent, w_qkv, w_proj, w_fc1, w_fc2_t, w_conv, g1, g2, table):
    reductions = [VMEM((3, n, 128), BF) for n in PARTS[:2] * 2]
    for slots in (2 * SIDE - 1, SIDE, SIDE):
        reductions += [VMEM((3, slots, n, 128), BF) for n in SHARES]
    inputs = (features, cotangent, w_qkv, w_proj, w_fc1, w_fc2_t, w_conv, g1, g2, table)
    scratch = [VMEM(v.shape, v.dtype) for v in inputs]
    scratch += [
        VMEM((NBLK, TOK, C), BF),
        VMEM((GROWS, 128), BF),
        VMEM((4, COLS, C), BF),
        VMEM((5, COLS, C), BF),
        VMEM((ROWS * 4, C), BF),
        VMEM((ROWS * 8, C), BF),
        VMEM((16, C), BF),
        VMEM((48, C), BF),
        VMEM((ROWS * 4, C), BF),
        VMEM((ROWS * 8, C), BF),
        VMEM((ROWS * 4, C), BF),
        VMEM((GROWS, 128), BF),
        *reductions,
        VMEM((NBLK, TOK, C), BF),
        VMEM((3, NBLK, (ROWS + 2) * BLK, C), BF),
        VMEM((3 * CP, CP), BF),
        VMEM((CP, 3 * CP), BF),
        VMEM((CP, CP), BF),
        VMEM((CP, CP), BF),
        VMEM((FF, CP), BF),
        VMEM((CP, FF), BF),
        VMEM((CP, FF), BF),
        VMEM((FF, CP), BF),
        VMEM((HEADS, WIN * WIN, PAIR), F32),
        VMEM((UNITS, CP, UT), F32),
        VMEM((UNITS, 1, UT), F32),
        VMEM((UNITS, CP, UT), BF),
        VMEM((UNITS, 3 * CP, UT), BF),
        VMEM((UNITS, CP, UT), BF),
        VMEM((UNITS, PAIRS, HEADS, WIN * WIN, PAIR), F32),
        VMEM((UNITS, CP, UT), F32),
        VMEM((UNITS, 1, UT), F32),
        VMEM((UNITS, CP, UT), BF),
        VMEM((UNITS, FF, UT), F32),
        VMEM((UNITS, FF, UT), BF),
        VMEM((3, UNITS, CP, UT), BF),
        VMEM((UNITS, CP, UT), BF),
        VMEM((UNITS, FF, UT), BF),
        VMEM((UNITS, CP, UT), BF),
        VMEM((UNITS, CP, UT), BF),
        VMEM((UNITS, 3 * CP, UT), BF),
        VMEM((UNITS, CP, UT), F32),
        pltpu.SemaphoreType.DMA((10,)),
        pltpu.SemaphoreType.DMA((4,)),
        pltpu.SemaphoreType.DMA((6,)),
        pltpu.SemaphoreType.DMA((6,)),
        pltpu.SemaphoreType.DMA((3,)),
        pltpu.SemaphoreType.DMA((3,)),
        pltpu.SemaphoreType.DMA((2, 6)),
        pltpu.SemaphoreType.DMA((2, 6)),
        pltpu.SemaphoreType.DMA((3, 4, 3, 2 * SIDE - 1)),
        pltpu.SemaphoreType.DMA((3, 4, 3, 2 * SIDE - 1)),
    ]
    return pl.pallas_call(
        layer,
        out_shape=(
            jax.ShapeDtypeStruct((NBLK, TOK, C), BF),
            jax.ShapeDtypeStruct((GROWS, 128), BF),
            jax.ShapeDtypeStruct((NBLK, 64, C), BF),
            jax.ShapeDtypeStruct((ROWS * 4, C), BF),
            jax.ShapeDtypeStruct((16, C), BF),
        ),
        in_specs=[pl.BlockSpec(memory_space=pl.ANY)] * 10,
        out_specs=[pl.BlockSpec(memory_space=pl.ANY)] * 2 + [pl.BlockSpec(memory_space=VMEM)] * 3,
        scratch_shapes=scratch,
        compiler_params=pltpu.CompilerParams(
            collective_id=0, has_side_effects=True, vmem_limit_bytes=60 * 2**20
        ),
        name="layer",
    )(*inputs)


def results(
    d_hbm, hr_hbm, hs_hbm, hc_hbm, sum_hbm,
    out_hbm, qkv_hbm, proj_hbm, fc1_hbm, fc2_hbm, conv_hbm,
    d_ref, hr_ref, hs_ref, hc_ref, sum_ref,
    out_ref, qkv_ref, proj_ref, fc1_ref, fc2_ref, conv_ref, load, store,
):
    hbm = (hr_hbm, hs_hbm, hc_hbm, d_hbm, sum_hbm)
    own = (hr_ref, hs_ref, hc_ref, d_ref, sum_ref)
    loads = [pltpu.make_async_copy(s, t, load.at[i]) for i, (s, t) in enumerate(zip(hbm, own))]
    for c in loads:
        c.start()
    stores = []

    def keep(source, target):
        stores.append(pltpu.make_async_copy(source, target, store.at[len(stores)]))
        stores[-1].start()

    for c in loads[:4]:
        c.wait()
    sub = iota((8, C), 0)
    extras = hs_ref[...].astype(F32).reshape(ROWS // 2, 8, C)
    corners = hc_ref[...].astype(F32).reshape(2, 8, C)
    for i in range(ROWS):
        if i < 4:
            pieces = [hr_ref[b, i * BLK : (i + 1) * BLK, :] for b in range(NBLK)]
            extra = corners[i // 2]
        else:
            pieces = [d_ref[b, (i - 4) * BLK : (i - 3) * BLK, :] for b in range(NBLK)]
            extra = extras[(i - 4) // 2]
        v = pltpu.roll(jnp.concatenate(pieces, axis=0).astype(F32), 4, 0)
        head = jnp.where(sub < 4, pltpu.roll(extra, 4, 0) if i % 2 else extra, v[:8])
        out_ref[i] = low(jnp.concatenate([head, v[8:]], axis=0))

    keep(out_ref, out_hbm)
    loads[4].wait()
    scale = 1.0 / math.sqrt(ROWS * COLS * lax.axis_size("row") * lax.axis_size("col"))

    def full(i):
        return sum_ref[i * CP : (i + 1) * CP, :]

    def rest(i):
        return full(9 + i // 2)[:, 64 * (i % 2) : 64 * (i % 2) + 64]

    def square(i, r):
        return jnp.concatenate([full(i), rest(r)], axis=1)

    for t in range(9):
        conv_ref[t] = square(t, t).astype(F32)[:C, :C] * scale
    keep(conv_ref, conv_hbm)
    proj_ref[...] = nn(spread(CP, C, 1), jnp.concatenate([full(20), full(21)[:, :64]], axis=1))[:, :C] * scale
    keep(proj_ref, proj_hbm)
    fc2 = jnp.concatenate([full(14), full(15), full(16)], axis=1).astype(F32)
    fc2_ref[...] = fc2[:C, :FF] * scale
    keep(fc2_ref, fc2_hbm)
    fc1 = jnp.concatenate([full(17), full(18), full(19)], axis=1).astype(F32)
    fc1_ref[...] = fc1[:C, :FF] * scale
    keep(fc1_ref, fc1_hbm)
    qkv = jnp.concatenate([full(22), full(23), full(24), full(25), full(26)[:, :64]], axis=1)
    qkv_ref[...] = nn(qkv, spread(3 * CP, 3 * C, 0))[:C] * scale
    keep(qkv_ref, qkv_hbm)
    for c in stores:
        c.wait()


def call_results(d_shifted, halo, sums):
    operands = (d_shifted, *halo, sums)
    shapes = (
        jax.ShapeDtypeStruct((ROWS, COLS, C), BF),
        jax.ShapeDtypeStruct((C, 3 * C), F32),
        jax.ShapeDtypeStruct((C, C), F32),
        jax.ShapeDtypeStruct((C, FF), F32),
        jax.ShapeDtypeStruct((C, FF), F32),
        jax.ShapeDtypeStruct((9, C, C), F32),
    )
    return pl.pallas_call(
        results,
        out_shape=shapes,
        in_specs=[pl.BlockSpec(memory_space=pl.ANY)] * 5,
        out_specs=[pl.BlockSpec(memory_space=pl.ANY)] * 6,
        scratch_shapes=[
            *(VMEM(v.shape, v.dtype) for v in operands + shapes),
            pltpu.SemaphoreType.DMA((5,)),
            pltpu.SemaphoreType.DMA((6,)),
        ],
        compiler_params=pltpu.CompilerParams(vmem_limit_bytes=60 * 2**20),
        name="results",
    )(*operands)


def local(features, cotangent, w_qkv, w_proj, w_fc1, w_fc2, w_conv, gain_attn, gain_mlp, pos_table):
    d_shifted, sums, *halo = call_layer(
        features,
        cotangent,
        w_qkv,
        w_proj,
        w_fc1,
        w_fc2.T,
        w_conv,
        gain_attn.reshape(1, C),
        gain_mlp.reshape(1, C),
        pos_table.T,
    )
    d_features, qkv, proj, fc1, fc2, conv = call_results(d_shifted, halo, sums)
    return d_features, qkv, proj, fc1, fc2.T, conv


def solution(mesh):
    return jax.shard_map(
        local,
        mesh=mesh,
        in_specs=(P("row", "col", None), P("row", "col", None)) + (P(),) * 8,
        out_specs=(P("row", "col", None),) + (P(),) * 5,
        check_vma=False,
    )
```

```python
import math

import jax
import jax.numpy as jnp
from jax import lax
from jax.experimental import pallas as pl
from jax.experimental.pallas import tpu as pltpu
from jax.sharding import PartitionSpec as P

C = 180
CP = 192
HEADS = 6
HD = 30
HP = 32
FF = 360
WIN = 8
SHIFT = 4
ROWS = 32
COLS = 64
BLK = 16
NBLK = COLS // BLK
TOK = ROWS * BLK
PAIR = WIN * BLK
UT = TOK // 2
UNITS = 8
PAIRS = UT // PAIR
SIDE = 4
TILES = (14, 8, 6)
BASE = (0, TILES[0] * CP, (TILES[0] + TILES[1]) * CP)
GROWS = sum(TILES) * CP
HALVES = tuple(t * CP // 2 for t in TILES)
PARTS = tuple(h // 3 for h in HALVES)
SHARES = tuple(p // SIDE for p in PARTS)
BF = jnp.bfloat16
F32 = jnp.float32
MESH = pl.DeviceIdType.MESH
VMEM = pltpu.VMEM


def iota(shape, dim):
    return lax.broadcasted_iota(jnp.int32, shape, dim)


def nn(a, b):
    return lax.dot_general(a, b, (((1,), (0,)), ((), ())), preferred_element_type=F32)


def nt(a, b):
    return lax.dot_general(a, b, (((1,), (1,)), ((), ())), preferred_element_type=F32)


def low(a):
    return a.astype(BF)


def eye(rows, cols):
    return low(jnp.where(iota((rows, cols), 0) == iota((rows, cols), 1), 1.0, 0.0))


def spread(padded, plain, pad_dim):
    shape = (padded, plain) if pad_dim == 0 else (plain, padded)
    p = iota(shape, pad_dim)
    c = iota(shape, 1 - pad_dim)
    hit = ((p & (HP - 1)) < HD) & (c == (p >> 5) * HD + (p & (HP - 1)))
    return low(jnp.where(hit, 1.0, 0.0))


def column(gain_ref):
    wide = jnp.where(iota((CP, C), 0) == iota((CP, C), 1), gain_ref[...], 0.0)
    return jnp.sum(wide, axis=1, keepdims=True)


def moments(values):
    mean = jnp.sum(values[:C], axis=0, keepdims=True) * (1.0 / C)
    centred = values - mean
    inner = centred[:C]
    var = jnp.sum(inner * inner, axis=0, keepdims=True) * (1.0 / C)
    return centred, lax.rsqrt(var + 1e-05)


def norm_back(upstream, normed, inverse, gain):
    scaled = upstream * gain
    first = jnp.sum(scaled, axis=0, keepdims=True) * (1.0 / C)
    second = jnp.sum(scaled * normed, axis=0, keepdims=True) * (1.0 / C)
    return inverse * (scaled - first - normed * second)


def gelu_parts(x):
    u = jnp.abs(x) * math.sqrt(0.5)
    t = 1.0 / (1.0 + 0.3275911 * u)
    e = jnp.exp(-u * u)
    poly = t * (
        0.254829592
        + t * (-0.284496736 + t * (1.421413741 + t * (-1.453152027 + t * 1.061405429)))
    )
    tail = 0.5 * poly * e
    cdf = jnp.where(x >= 0.0, 1.0 - tail, tail)
    return cdf, e * (1.0 / math.sqrt(2.0 * math.pi))


def fold(scores, second):
    parts = scores.reshape(WIN, 2, WIN, PAIR)
    return jnp.where(second, parts[:, 1], parts[:, 0]).reshape(WIN * WIN, PAIR)


def unfold(probs, second):
    parts = probs.reshape(WIN, WIN, PAIR)
    zero = jnp.zeros_like(parts)
    both = jnp.stack([jnp.where(second, zero, parts), jnp.where(second, parts, zero)], axis=1)
    return low(both.reshape(PAIR, PAIR))


def two_heads(block):
    zero = jnp.zeros((HP, PAIR), BF)
    top = jnp.concatenate([block[:HP], zero], axis=1)
    return jnp.concatenate([top, jnp.concatenate([zero, block[HP:]], axis=1)], axis=0)


def own_heads(product):
    return jnp.concatenate([product[:HP, :PAIR], product[HP:, PAIR:]], axis=0)


def tn(a, b):
    return lax.dot_general(a, b, (((0,), (0,)), ((), ())), preferred_element_type=F32)


def layer(
    f_hbm, g_hbm, wqkv_hbm, wproj_hbm, w1_hbm, w2_hbm, wconv_hbm, g1_hbm, g2_hbm, pos_hbm,
    d_hbm, sum_hbm, hr_ref, hs_ref, hc_ref,
    f_ref, g_ref, wqkv_ref, wproj_ref, w1_ref, w2_ref, wconv_ref, g1_ref, g2_ref, pos_ref,
    d_ref, sum_ref,
    fr_ref, gr_ref, fstrip_ref, gstrip_ref, fcorner_ref, gcorner_ref,
    fstrip_in, gstrip_in, strip_out,
    grads_ref, core0, core1, held0, held1, first0, first1, first2, second0, second1, second2, third0, third1, third2,
    xs, gs, wqkvt, wqkvp, wprojt, wprojp, w1t, w1p, w2t, w2p, offsets, bias,
    s_norm1, s_inv1, s_n1, packed, attended, probs, s_norm2, s_inv2, s_n2, s_slope, s_hidden, s_z,
    dshift, s_dpre, s_dattn, dheads, dpacked, s_dmid,
    load, store, in_send, in_recv, out_send, out_recv, core_send, core_recv, send, recv,
):
    row, col = lax.axis_index("row"), lax.axis_index("col")
    n_row, n_col = lax.axis_size("row"), lax.axis_size("col")
    up, down = lax.rem(row + n_row - 1, n_row), lax.rem(row + 1, n_row)
    left, right = lax.rem(col + n_col - 1, n_col), lax.rem(col + 1, n_col)
    last_row, last_col = row == n_row - 1, col == n_col - 1
    factor = HD**-0.5
    core, z, y = lax.rem(row, 2), lax.rem(row // 2, SIDE), lax.rem(col, SIDE)
    x = (row // 8) * 2 + col // SIDE
    here = (x, y, z)

    def device(xyz, c):
        return ((xyz[0] // 2) * 8 + xyz[2] * 2 + c, lax.rem(xyz[0], 2) * SIDE + xyz[1])

    def along(axis, k, other):
        there = list(here)
        there[axis] = lax.rem(there[axis] + k, SIDE)
        return device(there, 1 - core if other else core)

    sibling = device(here, 1 - core)
    seven = [(k, other) for k in range(SIDE) for other in (0, 1) if k + other > 0]
    barrier = pltpu.get_barrier_semaphore()
    greeted = [sibling, (up, col), (row, left), (up, left), (down, col), (row, right)]
    greeted += [(down, right)]
    greeted += [along(axis, k, o) for axis in range(3) for k, o in seven if k > 0]
    for peer in greeted:
        pl.semaphore_signal(barrier, inc=1, device_id=peer, device_id_type=MESH)

    hbm = (f_hbm, g_hbm, wqkv_hbm, wproj_hbm, w1_hbm, w2_hbm, wconv_hbm, g1_hbm, g2_hbm, pos_hbm)
    own = (f_ref, g_ref, wqkv_ref, wproj_ref, w1_ref, w2_ref, wconv_ref, g1_ref, g2_ref, pos_ref)
    loads = [pltpu.make_async_copy(s, t, load.at[i]) for i, (s, t) in enumerate(zip(hbm, own))]
    for c in loads:
        c.start()
    started = []

    def copy(src, dst, s, r, peer):
        c = pltpu.make_async_remote_copy(
            src_ref=src, dst_ref=dst, send_sem=s, recv_sem=r, device_id=peer, device_id_type=MESH
        )
        c.start()
        started.append(c)
        return c

    loads[0].wait()
    fs = f_ref[:, 0:16, :].astype(F32)[:, 0:8, :].reshape(ROWS // 2, 2, 8, C)
    pairs = jnp.where(iota((ROWS // 2, 8, C), 1) < 4, fs[:, 0], pltpu.roll(fs[:, 1], 4, 1))
    fstrip_in[...] = low(pairs.reshape(ROWS * 4, C))
    pl.semaphore_wait(barrier, len(greeted))
    f_arriving = [
        copy(fstrip_in.at[0:16], fcorner_ref, in_send.at[0], in_recv.at[0], (up, left)),
        copy(fstrip_in, fstrip_ref, in_send.at[1], in_recv.at[1], (row, left)),
        copy(f_ref.at[0:4], fr_ref, in_send.at[2], in_recv.at[2], (up, col)),
    ]
    loads[1].wait()
    cs = g_ref[:, 0:16, :].astype(F32)[:, 0:8, :]
    gstrip_in[...] = low(cs.reshape(ROWS * 8, C))
    g_arriving = [
        copy(gstrip_in.at[0:48], gcorner_ref, in_send.at[3], in_recv.at[3], (up, left)),
        copy(gstrip_in, gstrip_ref, in_send.at[4], in_recv.at[4], (row, left)),
        copy(g_ref.at[0:5], gr_ref, in_send.at[5], in_recv.at[5], (up, col)),
    ]

    sub = iota((8, C), 0)
    keep0 = jnp.where((sub == 3) & last_col, 0.0, 1.0)
    keep2 = jnp.where((sub == 4) & last_col, 0.0, 1.0)
    LASTB = NBLK - 1

    def put(target, i, rolled):
        whole = low(rolled[: LASTB * BLK])
        for b in range(LASTB):
            target[b, i * BLK : (i + 1) * BLK, :] = whole[b * BLK : (b + 1) * BLK]

    def put_last(target, i, body, last):
        target[LASTB, i * BLK : (i + 1) * BLK, :] = low(jnp.concatenate([body, last], axis=0))

    def put_x(i, v):
        put(xs, i, pltpu.roll(v, 60, 0))

    def put_x_last(i, v, extra):
        r = pltpu.roll(v, 12, 0)
        put_last(xs, i, r[:8], jnp.where(sub < 4, r[8:], extra))

    def put_g(i, v):
        for k, turn in enumerate((59, 60, 61)):
            put(gs.at[k], i, pltpu.roll(v, turn, 0))

    def put_g_last(i, v, extra):
        for k, n in enumerate((5, 4, 3)):
            r = pltpu.roll(v, 16 - n, 0)
            last = jnp.where(sub < 8 - n, r[8:], pltpu.roll(extra, 8 - n, 0))
            if k != 1:
                last = last * (keep0, keep2)[k // 2]
            put_last(gs.at[k], i, r[:8], last)

    for i in range(ROWS - 4):
        put_x(i, f_ref[i + 4].astype(F32))
    for i in range(ROWS - 3):
        put_g(i, g_ref[i + 3].astype(F32))

    for c in loads[2:]:
        c.wait()
    pad = eye(CP, C)
    sel, sel_one = spread(3 * CP, 3 * C, 0), spread(CP, C, 0)
    wq = low(nn(pad, wqkv_ref[...]))
    wqkvt[...] = low(nt(sel, wq))
    wqkvp[...] = low(nt(wq, sel))
    turned = low(nt(pad, wproj_ref[...]))
    wprojt[...] = low(nt(turned, sel_one))
    wprojp[...] = low(nt(sel_one, turned))
    w1p[...] = low(nn(pad, w1_ref[...]))
    w1t[...] = low(nt(eye(FF, FF), w1p[...]))
    w2t[...] = low(nn(pad, w2_ref[...]))
    w2p[...] = low(nt(eye(FF, FF), w2t[...]))
    gain1, gain2 = column(g1_ref), column(g2_ref)

    table = pos_ref[...]
    high = low(table)
    mid = low(table - high.astype(F32))
    rest_piece = low(table - high.astype(F32) - mid.astype(F32))
    entry, place = iota((225, 15 * BLK), 0), iota((225, 15 * BLK), 1)
    for kc in range(WIN):
        hit = entry == (place >> 4) * 15 + (place & 7) - kc + 7
        pick = low(jnp.where(hit, 1.0, 0.0))
        line = nn(high, pick) + nn(mid, pick) + nn(rest_piece, pick)
        for h in range(HEADS):
            offsets[h, kc : kc + 1, :] = line[h : h + 1]
    for h in range(HEADS):
        by_key = offsets[h]
        for kr in range(WIN):
            start = (WIN - 1 - kr) * BLK
            bias[h, kr * WIN : (kr + 1) * WIN, :] = by_key[:, start : start + PAIR]
    dshift[...] = jnp.zeros_like(dshift)

    def last_rows():
        f_arriving[2].wait_recv()
        for i in range(ROWS - 4, ROWS):
            put_x(i, fr_ref[i - 28].astype(F32))

    def last_block():
        f_arriving[1].wait_recv()
        f_arriving[0].wait_recv()
        quads = fstrip_ref[...].astype(F32).reshape(ROWS // 2, 8, C)
        corner = fcorner_ref[...].astype(F32).reshape(2, 8, C)

        def quad(source, i):
            return pltpu.roll(source[i // 2], 4, 0) if i % 2 == 0 else source[i // 2]

        for i in range(ROWS):
            if i < ROWS - 4:
                put_x_last(i, f_ref[i + 4, COLS - 16 :, :].astype(F32), quad(quads, i + 4))
            else:
                put_x_last(i, fr_ref[i - 28, COLS - 16 :, :].astype(F32), quad(corner, i - 28))

    lane = iota((1, PAIR), 1)
    second = ((lane >> 3) & 1) == 1
    k_sub, q_lane = iota((WIN * WIN, PAIR), 0), iota((WIN * WIN, PAIR), 1)
    rows_differ = ((k_sub >> 5) & 1) != ((q_lane >> 6) & 1)
    cols_differ = (((k_sub >> 2) & 1) != ((q_lane >> 2) & 1)) & (((q_lane >> 3) & 1) == 1)
    tok = iota((1, UT), 1) >> 4

    def place_of(u):
        t = u // 6
        return (1 - t) * (u % 3) + 3 * t, (1 - t) * (u // 3) + t * (u - 6)

    def lines(start, size):
        return pl.ds(start if isinstance(start, int) else pl.multiple_of(start, 16), size)

    def drops(half):
        return (tok == 27 - 16 * half) & last_row, (tok == 28 - 16 * half) & last_row

    def forward(*bs):
        at = [place_of(u) for u in bs]
        xv = [nt(pad, xs[b, lines(half * UT, UT), :]) for b, half in at]
        for b, x in zip(bs, xv):
            centred, inv1 = moments(x)
            normed1 = centred * inv1
            s_norm1[b] = normed1
            s_inv1[b] = inv1
            s_n1[b] = low(normed1 * gain1)
        for b in bs:
            packed[b] = low(nn(wqkvt[...], s_n1[b]))
        units = [(b, a, j) for b in bs for a in range(PAIRS) for j in range(HEADS // 2)]

        def part(b, third, a, j):
            top = third * CP + 64 * j
            return packed[b, top : top + 64, a * PAIR : (a + 1) * PAIR]

        scores = [tn(part(b, 1, a, j), two_heads(part(b, 0, a, j))) for b, a, j in units]
        soft = []
        for (b, a, j), score in zip(units, scores):
            block, half = place_of(b)
            row_flag = last_row & (half * PAIRS + a == ROWS // WIN - 1)
            col_flag = last_col & (block == NBLK - 1)
            mask = jnp.where((rows_differ & row_flag) | (cols_differ & col_flag), -100.0, 0.0)
            wide = []
            for s in range(2):
                sc = fold(score[:, s * PAIR : (s + 1) * PAIR], second)
                sc = sc * factor + bias[2 * j + s] + mask
                e = jnp.exp(sc - jnp.max(sc, axis=0, keepdims=True))
                p = e * (1.0 / jnp.sum(e, axis=0, keepdims=True))
                probs[b, a, 2 * j + s] = p
                wide.append(unfold(p, second))
            soft.append(jnp.concatenate(wide, axis=1))
        for (b, a, j), wide in zip(units, soft):
            o = nn(part(b, 2, a, j), wide)
            attended[b, 64 * j : 64 * j + 64, a * PAIR : (a + 1) * PAIR] = low(own_heads(o))

        middles = [x + nn(wprojt[...], attended[b]) for b, x in zip(bs, xv)]
        for b, middle in zip(bs, middles):
            centred2, inv2 = moments(middle)
            normed2 = centred2 * inv2
            s_norm2[b] = normed2
            s_inv2[b] = inv2
            s_n2[b] = low(normed2 * gain2)
        pres = [nn(w1t[...], s_n2[b]) for b in bs]
        for b, pre in zip(bs, pres):
            cdf, pdf = gelu_parts(pre)
            s_hidden[b] = low(pre * cdf)
            s_slope[b] = cdf + pre * pdf
        for b, (_, half), middle in zip(bs, at, middles):
            drop0, drop2 = drops(half)
            z = middle + nn(w2t[...], s_hidden[b])
            s_z[1, b] = low(z)
            s_z[0, b] = low(jnp.where(drop0, 0.0, z))
            s_z[2, b] = low(jnp.where(drop2, 0.0, z))

    forward(0, 1, 2)
    last_rows()
    last_block()
    forward(3, 4, 5, 6, 7)

    for c in g_arriving:
        c.wait_recv()
    for i in range(ROWS + 2):
        if i < ROWS - 3:
            extra = gstrip_ref[(i + 3) * 8 : (i + 4) * 8, :]
            put_g_last(i, g_ref[i + 3, COLS - 16 :, :].astype(F32), extra.astype(F32))
        else:
            k = i - ROWS + 3
            put_g(i, gr_ref[k].astype(F32))
            extra = gcorner_ref[k * 8 : (k + 1) * 8, :]
            put_g_last(i, gr_ref[k, COLS - 16 :, :].astype(F32), extra.astype(F32))

    def tap(b, dy, dx):
        return gs[dx, b, (2 - dy) * BLK : (2 - dy) * BLK + TOK, :]

    def halves(b):
        return (b, b + 3) if b < NBLK - 1 else (6, 7)

    def both(ref, b):
        return jnp.concatenate([ref[u] for u in halves(b)], axis=1)

    def over_blocks(term):
        total = term(0)
        for b in range(1, NBLK):
            total = total + term(b)
        return total

    def put_tile(place, tile):
        grads_ref[place * CP : (place + 1) * CP, :] = low(tile)

    def put_pair(place, left, right):
        put_tile(place, jnp.concatenate([left, right], axis=1))

    held_back = None
    for t in range(9):
        total = over_blocks(lambda b: nn(both(s_z.at[t // 3], b), tap(b, t // 3, t % 3)))
        put_tile(t, total[:, :128])
        narrow = jnp.concatenate([total[:, 128:], jnp.zeros((CP, 256 - 12 - C), F32)], axis=1)
        narrow = narrow[:, :64]
        if t % 2 == 0:
            held_back = narrow
        else:
            put_pair(9 + t // 2, held_back, narrow)
    put_pair(13, held_back, jnp.zeros((CP, 64), F32))
    steps = ((first0, second0, third0), (first1, second1, third1), (first2, second2, third2))
    staged = ((core0, held0), (core1, held1))
    flying = [{}, {}, {}]

    def rows(start, size):
        return pl.ds(pl.multiple_of(start, 16), size)

    def share_rows(g, c, p, share):
        at = BASE[g] + c * HALVES[g] + p * PARTS[g] + share * SHARES[g]
        return rows(at, SHARES[g])

    def part_rows(g, c, p):
        return rows(BASE[g] + c * HALVES[g] + p * PARTS[g], PARTS[g])

    def go_core(g):
        flying[g]["core"] = [
            copy(
                grads_ref.at[part_rows(g, 1 - core, p)],
                staged[g][0].at[p],
                core_send.at[g, p],
                core_recv.at[g, p],
                sibling,
            )
            for p in range(3)
        ]

    def go_first(g):
        if g < 2:
            flying[g]["first"] = []
            for p in range(3):
                flying[g]["core"][p].wait_recv()
                total = grads_ref[part_rows(g, core, p), :].astype(F32)
                staged[g][1][p] = low(total + staged[g][0][p].astype(F32))
                group = []
                for k in range(1, SIDE):
                    share = lax.rem(here[p] + k, SIDE)
                    group.append(
                        copy(
                            staged[g][1].at[p, rows(share * SHARES[g], SHARES[g])],
                            steps[g][0].at[p, k - 1],
                            send.at[g, 0, p, k - 1],
                            recv.at[g, 0, p, k - 1],
                            along(p, k, 0),
                        )
                    )
                flying[g]["first"].append(group)
            return
        flying[g]["first"] = [
            [
                copy(
                    grads_ref.at[
                        share_rows(g, 1 - core if o else core, p, lax.rem(here[p] + k, SIDE))
                    ],
                    steps[g][0].at[p, i],
                    send.at[g, 0, p, i],
                    recv.at[g, 0, p, i],
                    along(p, k, o),
                )
                for i, (k, o) in enumerate(seven)
            ]
            for p in range(3)
        ]

    def spread_out(g, p, step, source, axis):
        target = steps[g][step]
        target[p, here[axis]] = source
        return [
            copy(
                target.at[p, here[axis]],
                target.at[p, here[axis]],
                send.at[g, step, p, k - 1],
                recv.at[g, step, p, k - 1],
                along(axis, k, 0),
            )
            for k in range(1, SIDE)
        ]

    def gathered(copies, target, p):
        for c in copies:
            c.wait_recv()
        total = target[p, 0].astype(F32)
        for k in range(1, SIDE):
            total = total + target[p, k].astype(F32)
        return low(total)

    def go_second(g):
        flying[g]["second"] = []
        for p in range(3):
            if g < 2:
                total = staged[g][1][p, rows(here[p] * SHARES[g], SHARES[g]), :].astype(F32)
            else:
                total = grads_ref[share_rows(g, core, p, here[p]), :].astype(F32)
            for i in range(len(flying[g]["first"][p])):
                flying[g]["first"][p][i].wait_recv()
                total = total + steps[g][0][p, i].astype(F32)
            flying[g]["second"].append(spread_out(g, p, 1, low(total), (p + 1) % 3))

    def go_third(g):
        flying[g]["third"] = []
        for p in range(3):
            total = gathered(flying[g]["second"][p], steps[g][1], p)
            flying[g]["third"].append(spread_out(g, p, 2, total, (p + 2) % 3))

    def go_back(g):
        flying[g]["back"] = []
        partners = [(k, 0) for k in range(1, SIDE)] if g < 2 else seven
        for p in range(3):
            at = share_rows(g, core, p, here[p])
            sum_ref[at, :] = gathered(flying[g]["third"][p], steps[g][2], p)
            flying[g]["back"].append(
                [
                    copy(
                        sum_ref.at[at],
                        sum_ref.at[at],
                        send.at[g, 3, p, i],
                        recv.at[g, 3, p, i],
                        along(p, k, o),
                    )
                    for i, (k, o) in enumerate(partners)
                ]
            )

    def go_end(g):
        flying[g]["end"] = []
        for p in range(3):
            for c in flying[g]["back"][p]:
                c.wait_recv()
            if g < 2:
                at = part_rows(g, core, p)
                flying[g]["end"].append(
                    copy(
                        sum_ref.at[at],
                        sum_ref.at[at],
                        core_send.at[g, 3 + p],
                        core_recv.at[g, 3 + p],
                        sibling,
                    )
                )

    go_core(0)

    line = iota((1, TOK), 1) >> 4

    def conv_back(b):
        total = None
        for dy in range(3):
            part = None
            for dx in range(3):
                product = nt(wconv_ref[3 * dy + dx], tap(b, dy, dx))
                part = product if part is None else part + product
            if dy != 1:
                part = jnp.where((line == (27, 28)[dy // 2]) & last_row, 0.0, part)
            total = part if total is None else total + part
        for i, u in enumerate(halves(b)):
            dshift[u, :C, :] = low(total[:, i * UT : (i + 1) * UT])

    def back_to_heads():
        bs = range(UNITS)
        d_pres = [low(nn(w2p[...], dshift[b]) * s_slope[b]) for b in bs]
        d_middles = []
        for b, d_pre in zip(bs, d_pres):
            s_dpre[b] = d_pre
            d_middle = dshift[b].astype(F32) + norm_back(
                nn(w1p[...], d_pre), s_norm2[b], s_inv2[b], gain2
            )
            s_dmid[b] = d_middle
            d_middles.append(low(d_middle))
        for b, d_attn in zip(bs, d_middles):
            s_dattn[b] = d_attn
            dheads[b] = low(nn(wprojp[...], d_attn))

    conv_back(0)
    conv_back(1)
    go_first(0)
    conv_back(2)
    conv_back(3)
    back_to_heads()

    fc2 = over_blocks(lambda b: nt(both(dshift, b), both(s_hidden, b)))
    fc1 = over_blocks(lambda b: nt(both(s_n2, b), both(s_dpre, b)))
    for place, total in ((14, fc2), (17, fc1)):
        put_tile(place, total[:, :128])
        put_tile(place + 1, total[:, 128:256])
        put_pair(place + 2, total[:, 256:], jnp.zeros((CP, 384 - FF), F32))
    proj = over_blocks(lambda b: nt(both(attended, b), both(s_dattn, b)))
    put_tile(20, proj[:, :128])
    put_pair(21, proj[:, 128:192], jnp.zeros((CP, 64), F32))
    go_core(1)
    go_second(0)

    def heads_back(step):
        units = [
            (u, a, j)
            for u in (2 * step, 2 * step + 1)
            for a in range(PAIRS)
            for j in range(HEADS // 2)
        ]

        def part(ref, u, third, a, j):
            top = third * CP + 64 * j
            return ref[u, top : top + 64, a * PAIR : (a + 1) * PAIR]

        d_probs = [
            tn(part(packed, u, 2, a, j), two_heads(part(dheads, u, 0, a, j))) for u, a, j in units
        ]
        wide = []
        for (u, a, j), d_prob in zip(units, d_probs):
            p_wide, s_wide = [], []
            for s in range(2):
                p = probs[u, a, 2 * j + s]
                dp = fold(d_prob[:, s * PAIR : (s + 1) * PAIR], second)
                ds = p * (dp - jnp.sum(p * dp, axis=0, keepdims=True)) * factor
                p_wide.append(unfold(p, second))
                s_wide.append(unfold(ds, second))
            wide.append((p_wide, s_wide))
        for (u, a, j), (p_wide, s_wide) in zip(units, wide):
            lanes = slice(a * PAIR, (a + 1) * PAIR)
            dv = nt(part(dheads, u, 0, a, j), jnp.concatenate(p_wide, axis=0))
            dq = nn(part(packed, u, 1, a, j), jnp.concatenate(s_wide, axis=1))
            dk = nt(part(packed, u, 0, a, j), jnp.concatenate(s_wide, axis=0))
            dpacked[u, 64 * j : 64 * j + 64, lanes] = low(own_heads(dq))
            dpacked[u, CP + 64 * j : CP + 64 * j + 64, lanes] = low(own_heads(dk))
            dpacked[u, 2 * CP + 64 * j : 2 * CP + 64 * j + 64, lanes] = low(own_heads(dv))

    heads_back(0)
    heads_back(1)
    go_first(1)
    heads_back(2)
    heads_back(3)
    go_third(0)
    qkv = over_blocks(lambda b: nt(both(s_n1, b), both(dpacked, b)))
    for i in range(4):
        put_tile(22 + i, qkv[:, i * 128 : (i + 1) * 128])
    put_pair(26, qkv[:, 512:576], jnp.zeros((CP, 64), F32))
    put_tile(27, jnp.zeros((CP, 128), F32))
    go_first(2)

    ones_pair = eye(PAIR, PAIR)

    def inputs_back(*us):
        d_ins = [
            s_dmid[u] + norm_back(nn(wqkvp[...], dpacked[u]), s_norm1[u], s_inv1[u], gain1)
            for u in us
        ]
        for u, d_in in zip(us, d_ins):
            b, half = place_of(u)
            d_low = low(d_in)
            for a in range(PAIRS):
                natural = nt(ones_pair, d_low[:, a * PAIR : (a + 1) * PAIR])
                at = half * UT + a * PAIR
                d_ref[b, at : at + PAIR, :] = low(natural[:, :C])

    inputs_back(6, 7)
    edge = d_ref[NBLK - 1].astype(F32).reshape(ROWS // 2, 2, 2, 8, C)[:, :, 1]
    pairs = jnp.where(
        iota((ROWS // 2, 8, C), 1) < 4, pltpu.roll(edge[:, 0], 4, 1), edge[:, 1]
    )
    strip_out[...] = low(pairs.reshape(ROWS * 4, C))
    leaving = [
        copy(strip_out.at[112:128], hc_ref, out_send.at[2], out_recv.at[2], (down, right)),
        copy(strip_out, hs_ref, out_send.at[1], out_recv.at[1], (row, right)),
    ]
    go_second(1)
    inputs_back(3, 4, 5)
    inputs_back(0, 1, 2)
    leaving.append(
        copy(d_ref.at[:, 448:512, :], hr_ref, out_send.at[0], out_recv.at[0], (down, col))
    )
    stores = [pltpu.make_async_copy(d_ref, d_hbm, store.at[0])]
    stores[0].start()

    def keep(g):
        for c in flying[g]["end"]:
            c.wait_recv()
        at = slice(BASE[g], BASE[g] + TILES[g] * CP)
        stores.append(pltpu.make_async_copy(sum_ref.at[at], sum_hbm.at[at], store.at[1 + g]))
        stores[-1].start()

    go_back(0)
    go_second(2)
    go_third(1)
    go_third(2)
    go_end(0)
    go_back(1)
    go_back(2)
    keep(0)
    go_end(1)
    go_end(2)
    keep(1)
    keep(2)
    for c in leaving:
        c.wait_recv()
    for c in started:
        c.wait_send()
    for c in stores:
        c.wait()


def call_layer(features, cotangent, w_qkv, w_proj, w_fc1, w_fc2_t, w_conv, g1, g2, table):
    reductions = [VMEM((3, n, 128), BF) for n in PARTS[:2] * 2]
    for slots in (2 * SIDE - 1, SIDE, SIDE):
        reductions += [VMEM((3, slots, n, 128), BF) for n in SHARES]
    inputs = (features, cotangent, w_qkv, w_proj, w_fc1, w_fc2_t, w_conv, g1, g2, table)
    scratch = [VMEM(v.shape, v.dtype) for v in inputs]
    scratch += [
        VMEM((NBLK, TOK, C), BF),
        VMEM((GROWS, 128), BF),
        VMEM((4, COLS, C), BF),
        VMEM((5, COLS, C), BF),
        VMEM((ROWS * 4, C), BF),
        VMEM((ROWS * 8, C), BF),
        VMEM((16, C), BF),
        VMEM((48, C), BF),
        VMEM((ROWS * 4, C), BF),
        VMEM((ROWS * 8, C), BF),
        VMEM((ROWS * 4, C), BF),
        VMEM((GROWS, 128), BF),
        *reductions,
        VMEM((NBLK, TOK, C), BF),
        VMEM((3, NBLK, (ROWS + 2) * BLK, C), BF),
        VMEM((3 * CP, CP), BF),
        VMEM((CP, 3 * CP), BF),
        VMEM((CP, CP), BF),
        VMEM((CP, CP), BF),
        VMEM((FF, CP), BF),
        VMEM((CP, FF), BF),
        VMEM((CP, FF), BF),
        VMEM((FF, CP), BF),
        VMEM((HEADS, WIN, 15 * BLK), F32),
        VMEM((HEADS, WIN * WIN, PAIR), F32),
        VMEM((UNITS, CP, UT), F32),
        VMEM((UNITS, 1, UT), F32),
        VMEM((UNITS, CP, UT), BF),
        VMEM((UNITS, 3 * CP, UT), BF),
        VMEM((UNITS, CP, UT), BF),
        VMEM((UNITS, PAIRS, HEADS, WIN * WIN, PAIR), F32),
        VMEM((UNITS, CP, UT), F32),
        VMEM((UNITS, 1, UT), F32),
        VMEM((UNITS, CP, UT), BF),
        VMEM((UNITS, FF, UT), F32),
        VMEM((UNITS, FF, UT), BF),
        VMEM((3, UNITS, CP, UT), BF),
        VMEM((UNITS, CP, UT), BF),
        VMEM((UNITS, FF, UT), BF),
        VMEM((UNITS, CP, UT), BF),
        VMEM((UNITS, CP, UT), BF),
        VMEM((UNITS, 3 * CP, UT), BF),
        VMEM((UNITS, CP, UT), F32),
        pltpu.SemaphoreType.DMA((10,)),
        pltpu.SemaphoreType.DMA((4,)),
        pltpu.SemaphoreType.DMA((6,)),
        pltpu.SemaphoreType.DMA((6,)),
        pltpu.SemaphoreType.DMA((3,)),
        pltpu.SemaphoreType.DMA((3,)),
        pltpu.SemaphoreType.DMA((2, 6)),
        pltpu.SemaphoreType.DMA((2, 6)),
        pltpu.SemaphoreType.DMA((3, 4, 3, 2 * SIDE - 1)),
        pltpu.SemaphoreType.DMA((3, 4, 3, 2 * SIDE - 1)),
    ]
    return pl.pallas_call(
        layer,
        out_shape=(
            jax.ShapeDtypeStruct((NBLK, TOK, C), BF),
            jax.ShapeDtypeStruct((GROWS, 128), BF),
            jax.ShapeDtypeStruct((NBLK, 64, C), BF),
            jax.ShapeDtypeStruct((ROWS * 4, C), BF),
            jax.ShapeDtypeStruct((16, C), BF),
        ),
        in_specs=[pl.BlockSpec(memory_space=pl.ANY)] * 10,
        out_specs=[pl.BlockSpec(memory_space=pl.ANY)] * 2 + [pl.BlockSpec(memory_space=VMEM)] * 3,
        scratch_shapes=scratch,
        compiler_params=pltpu.CompilerParams(
            collective_id=0, has_side_effects=True, vmem_limit_bytes=60 * 2**20
        ),
        name="layer",
    )(*inputs)


def results(
    d_hbm, hr_hbm, hs_hbm, hc_hbm, sum_hbm,
    out_hbm, qkv_hbm, proj_hbm, fc1_hbm, fc2_hbm, conv_hbm,
    d_ref, hr_ref, hs_ref, hc_ref, sum_ref,
    out_ref, qkv_ref, proj_ref, fc1_ref, fc2_ref, conv_ref, sel_ref, load, store,
):
    hbm = (hr_hbm, hs_hbm, hc_hbm, d_hbm, sum_hbm)
    own = (hr_ref, hs_ref, hc_ref, d_ref, sum_ref)
    loads = [pltpu.make_async_copy(s, t, load.at[i]) for i, (s, t) in enumerate(zip(hbm, own))]
    for c in (loads[4], *loads[:4]):
        c.start()
    stores = []

    def keep(source, target):
        stores.append(pltpu.make_async_copy(source, target, store.at[len(stores)]))
        stores[-1].start()

    sel_ref[...] = spread(3 * CP, 3 * C, 0)
    loads[4].wait()
    scale = 1.0 / math.sqrt(ROWS * COLS * lax.axis_size("row") * lax.axis_size("col"))

    def full(i):
        return sum_ref[i * CP : (i + 1) * CP, :]

    def rest(i):
        return full(9 + i // 2)[:, 64 * (i % 2) : 64 * (i % 2) + 64]

    def square(i, r):
        return jnp.concatenate([full(i), rest(r)], axis=1)

    for t in range(9):
        conv_ref[t] = square(t, t).astype(F32)[:C, :C] * scale
    keep(conv_ref, conv_hbm)
    for c in loads[:4]:
        c.wait()
    sub = iota((8, C), 0)
    extras = hs_ref[...].astype(F32).reshape(ROWS // 2, 8, C)
    corners = hc_ref[...].astype(F32).reshape(2, 8, C)
    for i in range(ROWS):
        if i < 4:
            pieces = [hr_ref[b, i * BLK : (i + 1) * BLK, :] for b in range(NBLK)]
            extra = corners[i // 2]
        else:
            pieces = [d_ref[b, (i - 4) * BLK : (i - 3) * BLK, :] for b in range(NBLK)]
            extra = extras[(i - 4) // 2]
        v = pltpu.roll(jnp.concatenate(pieces, axis=0).astype(F32), 4, 0)
        head = jnp.where(sub < 4, pltpu.roll(extra, 4, 0) if i % 2 else extra, v[:8])
        out_ref[i] = low(jnp.concatenate([head, v[8:]], axis=0))

    keep(out_ref, out_hbm)
    proj_ref[...] = nn(spread(CP, C, 1), jnp.concatenate([full(20), full(21)[:, :64]], axis=1))[:, :C] * scale
    keep(proj_ref, proj_hbm)
    fc2 = jnp.concatenate([full(14), full(15), full(16)], axis=1).astype(F32)
    fc2_ref[...] = fc2[:C, :FF] * scale
    keep(fc2_ref, fc2_hbm)
    fc1 = jnp.concatenate([full(17), full(18), full(19)], axis=1).astype(F32)
    fc1_ref[...] = fc1[:C, :FF] * scale
    keep(fc1_ref, fc1_hbm)
    qkv = jnp.concatenate([full(22), full(23), full(24), full(25), full(26)[:, :64]], axis=1)
    qkv_ref[...] = nn(qkv, sel_ref[...])[:C] * scale
    keep(qkv_ref, qkv_hbm)
    for c in stores:
        c.wait()


def call_results(d_shifted, halo, sums):
    operands = (d_shifted, *halo, sums)
    shapes = (
        jax.ShapeDtypeStruct((ROWS, COLS, C), BF),
        jax.ShapeDtypeStruct((C, 3 * C), F32),
        jax.ShapeDtypeStruct((C, C), F32),
        jax.ShapeDtypeStruct((C, FF), F32),
        jax.ShapeDtypeStruct((C, FF), F32),
        jax.ShapeDtypeStruct((9, C, C), F32),
    )
    return pl.pallas_call(
        results,
        out_shape=shapes,
        in_specs=[pl.BlockSpec(memory_space=pl.ANY)] * 5,
        out_specs=[pl.BlockSpec(memory_space=pl.ANY)] * 6,
        scratch_shapes=[
            *(VMEM(v.shape, v.dtype) for v in operands + shapes),
            VMEM((3 * CP, 3 * C), BF),
            pltpu.SemaphoreType.DMA((5,)),
            pltpu.SemaphoreType.DMA((6,)),
        ],
        compiler_params=pltpu.CompilerParams(vmem_limit_bytes=60 * 2**20),
        name="results",
    )(*operands)


def local(features, cotangent, w_qkv, w_proj, w_fc1, w_fc2, w_conv, gain_attn, gain_mlp, pos_table):
    d_shifted, sums, *halo = call_layer(
        features,
        cotangent,
        w_qkv,
        w_proj,
        w_fc1,
        w_fc2.T,
        w_conv,
        gain_attn.reshape(1, C),
        gain_mlp.reshape(1, C),
        pos_table.T,
    )
    d_features, qkv, proj, fc1, fc2, conv = call_results(d_shifted, halo, sums)
    return d_features, qkv, proj, fc1, fc2.T, conv


def solution(mesh):
    return jax.shard_map(
        local,
        mesh=mesh,
        in_specs=(P("row", "col", None), P("row", "col", None)) + (P(),) * 8,
        out_specs=(P("row", "col", None),) + (P(),) * 5,
        check_vma=False,
    )
```

```python
import math

import jax
import jax.numpy as jnp
from jax import lax
from jax.experimental import pallas as pl
from jax.experimental.pallas import tpu as pltpu
from jax.sharding import PartitionSpec as P

C = 180
CP = 192
HEADS = 6
HD = 30
HP = 32
FF = 360
WIN = 8
SHIFT = 4
ROWS = 32
COLS = 64
BLK = 16
NBLK = COLS // BLK
TOK = ROWS * BLK
PAIR = WIN * BLK
UT = TOK // 2
UNITS = 8
PAIRS = UT // PAIR
SIDE = 4
TILES = (14, 8, 6)
BASE = (0, TILES[0] * CP, (TILES[0] + TILES[1]) * CP)
GROWS = sum(TILES) * CP
HALVES = tuple(t * CP // 2 for t in TILES)
PARTS = tuple(h // 3 for h in HALVES)
SHARES = tuple(p // SIDE for p in PARTS)
BF = jnp.bfloat16
F32 = jnp.float32
MESH = pl.DeviceIdType.MESH
VMEM = pltpu.VMEM


def iota(shape, dim):
    return lax.broadcasted_iota(jnp.int32, shape, dim)


def nn(a, b):
    return lax.dot_general(a, b, (((1,), (0,)), ((), ())), preferred_element_type=F32)


def nt(a, b):
    return lax.dot_general(a, b, (((1,), (1,)), ((), ())), preferred_element_type=F32)


def low(a):
    return a.astype(BF)


def eye(rows, cols):
    return low(jnp.where(iota((rows, cols), 0) == iota((rows, cols), 1), 1.0, 0.0))


def spread(padded, plain, pad_dim):
    shape = (padded, plain) if pad_dim == 0 else (plain, padded)
    p = iota(shape, pad_dim)
    c = iota(shape, 1 - pad_dim)
    hit = ((p & (HP - 1)) < HD) & (c == (p >> 5) * HD + (p & (HP - 1)))
    return low(jnp.where(hit, 1.0, 0.0))


def column(gain_ref):
    wide = jnp.where(iota((CP, C), 0) == iota((CP, C), 1), gain_ref[...], 0.0)
    return jnp.sum(wide, axis=1, keepdims=True)


def moments(values):
    mean = jnp.sum(values[:C], axis=0, keepdims=True) * (1.0 / C)
    centred = values - mean
    inner = centred[:C]
    var = jnp.sum(inner * inner, axis=0, keepdims=True) * (1.0 / C)
    return centred, lax.rsqrt(var + 1e-05)


def norm_back(upstream, normed, inverse, gain):
    scaled = upstream * gain
    first = jnp.sum(scaled, axis=0, keepdims=True) * (1.0 / C)
    second = jnp.sum(scaled * normed, axis=0, keepdims=True) * (1.0 / C)
    return inverse * (scaled - first - normed * second)


def gelu_parts(x):
    u = jnp.abs(x) * math.sqrt(0.5)
    t = 1.0 / (1.0 + 0.3275911 * u)
    e = jnp.exp(-u * u)
    poly = t * (
        0.254829592
        + t * (-0.284496736 + t * (1.421413741 + t * (-1.453152027 + t * 1.061405429)))
    )
    tail = 0.5 * poly * e
    cdf = jnp.where(x >= 0.0, 1.0 - tail, tail)
    return cdf, e * (1.0 / math.sqrt(2.0 * math.pi))


def fold(scores, second):
    parts = scores.reshape(WIN, 2, WIN, PAIR)
    return jnp.where(second, parts[:, 1], parts[:, 0]).reshape(WIN * WIN, PAIR)


def unfold(probs, second):
    parts = probs.reshape(WIN, WIN, PAIR)
    zero = jnp.zeros_like(parts)
    both = jnp.stack([jnp.where(second, zero, parts), jnp.where(second, parts, zero)], axis=1)
    return low(both.reshape(PAIR, PAIR))


def two_heads(block):
    zero = jnp.zeros((HP, PAIR), BF)
    top = jnp.concatenate([block[:HP], zero], axis=1)
    return jnp.concatenate([top, jnp.concatenate([zero, block[HP:]], axis=1)], axis=0)


def own_heads(product):
    return jnp.concatenate([product[:HP, :PAIR], product[HP:, PAIR:]], axis=0)


def tn(a, b):
    return lax.dot_general(a, b, (((0,), (0,)), ((), ())), preferred_element_type=F32)


def layer(
    f_hbm, g_hbm, wqkv_hbm, wproj_hbm, w1_hbm, w2_hbm, wconv_hbm, g1_hbm, g2_hbm, pos_hbm,
    d_hbm, sum_hbm, hr_ref, hs_ref, hc_ref,
    f_ref, g_ref, wqkv_ref, wproj_ref, w1_ref, w2_ref, wconv_ref, g1_ref, g2_ref, pos_ref,
    d_ref, sum_ref,
    fr_ref, gr_ref, fstrip_ref, gstrip_ref, fcorner_ref, gcorner_ref,
    fstrip_in, gstrip_in, strip_out,
    grads_ref, core0, core1, held0, held1, first0, first1, first2, second0, second1, second2, third0, third1, third2,
    xs, gs, wqkvt, wqkvp, wprojt, wprojp, w1t, w1p, w2t, w2p, offsets, bias,
    s_norm1, s_inv1, s_n1, packed, attended, probs, s_norm2, s_inv2, s_n2, s_slope, s_hidden, s_z,
    dshift, s_dpre, s_dattn, dheads, dpacked, s_dmid,
    load, store, in_send, in_recv, out_send, out_recv, core_send, core_recv, send, recv,
):
    row, col = lax.axis_index("row"), lax.axis_index("col")
    n_row, n_col = lax.axis_size("row"), lax.axis_size("col")
    up, down = lax.rem(row + n_row - 1, n_row), lax.rem(row + 1, n_row)
    left, right = lax.rem(col + n_col - 1, n_col), lax.rem(col + 1, n_col)
    last_row, last_col = row == n_row - 1, col == n_col - 1
    factor = HD**-0.5
    core, z, y = lax.rem(row, 2), lax.rem(row // 2, SIDE), lax.rem(col, SIDE)
    x = (row // 8) * 2 + col // SIDE
    here = (x, y, z)

    def device(xyz, c):
        return ((xyz[0] // 2) * 8 + xyz[2] * 2 + c, lax.rem(xyz[0], 2) * SIDE + xyz[1])

    def along(axis, k, other):
        there = list(here)
        there[axis] = lax.rem(there[axis] + k, SIDE)
        return device(there, 1 - core if other else core)

    sibling = device(here, 1 - core)
    seven = [(k, other) for k in range(SIDE) for other in (0, 1) if k + other > 0]
    barrier = pltpu.get_barrier_semaphore()
    greeted = [sibling, (up, col), (row, left), (up, left), (down, col), (row, right)]
    greeted += [(down, right)]
    greeted += [along(axis, k, o) for axis in range(3) for k, o in seven if k > 0]
    for peer in greeted:
        pl.semaphore_signal(barrier, inc=1, device_id=peer, device_id_type=MESH)

    hbm = (f_hbm, g_hbm, wqkv_hbm, wproj_hbm, w1_hbm, w2_hbm, wconv_hbm, g1_hbm, g2_hbm, pos_hbm)
    own = (f_ref, g_ref, wqkv_ref, wproj_ref, w1_ref, w2_ref, wconv_ref, g1_ref, g2_ref, pos_ref)
    loads = [pltpu.make_async_copy(s, t, load.at[i]) for i, (s, t) in enumerate(zip(hbm, own))]
    for c in loads:
        c.start()
    started = []

    def copy(src, dst, s, r, peer):
        c = pltpu.make_async_remote_copy(
            src_ref=src, dst_ref=dst, send_sem=s, recv_sem=r, device_id=peer, device_id_type=MESH
        )
        c.start()
        started.append(c)
        return c

    loads[0].wait()
    fs = f_ref[:, 0:16, :].astype(F32)[:, 0:8, :].reshape(ROWS // 2, 2, 8, C)
    pairs = jnp.where(iota((ROWS // 2, 8, C), 1) < 4, fs[:, 0], pltpu.roll(fs[:, 1], 4, 1))
    fstrip_in[...] = low(pairs.reshape(ROWS * 4, C))
    pl.semaphore_wait(barrier, len(greeted))
    f_arriving = [
        copy(fstrip_in.at[0:16], fcorner_ref, in_send.at[0], in_recv.at[0], (up, left)),
        copy(fstrip_in, fstrip_ref, in_send.at[1], in_recv.at[1], (row, left)),
        copy(f_ref.at[0:4], fr_ref, in_send.at[2], in_recv.at[2], (up, col)),
    ]
    loads[1].wait()
    cs = g_ref[:, 0:16, :].astype(F32)[:, 0:8, :]
    gstrip_in[...] = low(cs.reshape(ROWS * 8, C))
    g_arriving = [
        copy(gstrip_in.at[0:48], gcorner_ref, in_send.at[3], in_recv.at[3], (up, left)),
        copy(gstrip_in, gstrip_ref, in_send.at[4], in_recv.at[4], (row, left)),
        copy(g_ref.at[0:5], gr_ref, in_send.at[5], in_recv.at[5], (up, col)),
    ]

    sub = iota((8, C), 0)
    keep0 = jnp.where((sub == 3) & last_col, 0.0, 1.0)
    keep2 = jnp.where((sub == 4) & last_col, 0.0, 1.0)
    LASTB = NBLK - 1

    def put(target, i, rolled):
        whole = low(rolled[: LASTB * BLK])
        for b in range(LASTB):
            target[b, i * BLK : (i + 1) * BLK, :] = whole[b * BLK : (b + 1) * BLK]

    def put_last(target, i, body, last):
        target[LASTB, i * BLK : (i + 1) * BLK, :] = low(jnp.concatenate([body, last], axis=0))

    def put_x(i, v):
        put(xs, i, pltpu.roll(v, 60, 0))

    def put_x_last(i, v, extra):
        r = pltpu.roll(v, 12, 0)
        put_last(xs, i, r[:8], jnp.where(sub < 4, r[8:], extra))

    def put_g(i, v):
        for k, turn in enumerate((59, 60, 61)):
            put(gs.at[k], i, pltpu.roll(v, turn, 0))

    def put_g_last(i, v, extra):
        for k, n in enumerate((5, 4, 3)):
            r = pltpu.roll(v, 16 - n, 0)
            last = jnp.where(sub < 8 - n, r[8:], pltpu.roll(extra, 8 - n, 0))
            if k != 1:
                last = last * (keep0, keep2)[k // 2]
            put_last(gs.at[k], i, r[:8], last)

    for i in range(ROWS - 4):
        put_x(i, f_ref[i + 4].astype(F32))
    for i in range(ROWS - 3):
        put_g(i, g_ref[i + 3].astype(F32))

    for c in loads[2:]:
        c.wait()
    pad = eye(CP, C)
    sel, sel_one = spread(3 * CP, 3 * C, 0), spread(CP, C, 0)
    wq = low(nn(pad, wqkv_ref[...]))
    wqkvt[...] = low(nt(sel, wq))
    wqkvp[...] = low(nt(wq, sel))
    turned = low(nt(pad, wproj_ref[...]))
    wprojt[...] = low(nt(turned, sel_one))
    wprojp[...] = low(nt(sel_one, turned))
    w1p[...] = low(nn(pad, w1_ref[...]))
    w1t[...] = low(nt(eye(FF, FF), w1p[...]))
    w2t[...] = low(nn(pad, w2_ref[...]))
    w2p[...] = low(nt(eye(FF, FF), w2t[...]))
    gain1, gain2 = column(g1_ref), column(g2_ref)

    table = pos_ref[...]
    high = low(table)
    mid = low(table - high.astype(F32))
    rest_piece = low(table - high.astype(F32) - mid.astype(F32))
    entry, place = iota((225, 15 * BLK), 0), iota((225, 15 * BLK), 1)
    for kc in range(WIN):
        hit = entry == (place >> 4) * 15 + (place & 7) - kc + 7
        pick = low(jnp.where(hit, 1.0, 0.0))
        line = nn(high, pick) + nn(mid, pick) + nn(rest_piece, pick)
        for h in range(HEADS):
            offsets[h, kc : kc + 1, :] = line[h : h + 1]
    for h in range(HEADS):
        by_key = offsets[h]
        for kr in range(WIN):
            start = (WIN - 1 - kr) * BLK
            bias[h, kr * WIN : (kr + 1) * WIN, :] = by_key[:, start : start + PAIR]
    dshift[...] = jnp.zeros_like(dshift)

    def last_rows():
        f_arriving[2].wait_recv()
        for i in range(ROWS - 4, ROWS):
            put_x(i, fr_ref[i - 28].astype(F32))

    def last_block():
        f_arriving[1].wait_recv()
        f_arriving[0].wait_recv()
        quads = fstrip_ref[...].astype(F32).reshape(ROWS // 2, 8, C)
        corner = fcorner_ref[...].astype(F32).reshape(2, 8, C)

        def quad(source, i):
            return pltpu.roll(source[i // 2], 4, 0) if i % 2 == 0 else source[i // 2]

        for i in range(ROWS):
            if i < ROWS - 4:
                put_x_last(i, f_ref[i + 4, COLS - 16 :, :].astype(F32), quad(quads, i + 4))
            else:
                put_x_last(i, fr_ref[i - 28, COLS - 16 :, :].astype(F32), quad(corner, i - 28))

    lane = iota((1, PAIR), 1)
    second = ((lane >> 3) & 1) == 1
    k_sub, q_lane = iota((WIN * WIN, PAIR), 0), iota((WIN * WIN, PAIR), 1)
    rows_differ = ((k_sub >> 5) & 1) != ((q_lane >> 6) & 1)
    cols_differ = (((k_sub >> 2) & 1) != ((q_lane >> 2) & 1)) & (((q_lane >> 3) & 1) == 1)
    tok = iota((1, UT), 1) >> 4

    def place_of(u):
        t = u // 6
        return (1 - t) * (u % 3) + 3 * t, (1 - t) * (u // 3) + t * (u - 6)

    def lines(start, size):
        return pl.ds(start if isinstance(start, int) else pl.multiple_of(start, 16), size)

    def drops(half):
        return (tok == 27 - 16 * half) & last_row, (tok == 28 - 16 * half) & last_row

    def forward(*bs):
        at = [place_of(u) for u in bs]
        xv = [nt(pad, xs[b, lines(half * UT, UT), :]) for b, half in at]
        for b, x in zip(bs, xv):
            centred, inv1 = moments(x)
            normed1 = centred * inv1
            s_norm1[b] = normed1
            s_inv1[b] = inv1
            s_n1[b] = low(normed1 * gain1)
        for b in bs:
            packed[b] = low(nn(wqkvt[...], s_n1[b]))
        units = [(b, a, j) for b in bs for a in range(PAIRS) for j in range(HEADS // 2)]

        def part(b, third, a, j):
            top = third * CP + 64 * j
            return packed[b, top : top + 64, a * PAIR : (a + 1) * PAIR]

        scores = [tn(part(b, 1, a, j), two_heads(part(b, 0, a, j))) for b, a, j in units]
        soft = []
        for (b, a, j), score in zip(units, scores):
            block, half = place_of(b)
            differ = []
            if half * PAIRS + a == ROWS // WIN - 1:
                differ.append(rows_differ & last_row)
            if block == NBLK - 1:
                differ.append(cols_differ & last_col)
            if differ:
                mask = jnp.where(differ[0] | differ[-1], -100.0, 0.0)
            wide = []
            for s in range(2):
                sc = fold(score[:, s * PAIR : (s + 1) * PAIR], second)
                sc = sc * factor + bias[2 * j + s]
                if differ:
                    sc = sc + mask
                e = jnp.exp(sc - jnp.max(sc, axis=0, keepdims=True))
                p = e * (1.0 / jnp.sum(e, axis=0, keepdims=True))
                probs[b, a, 2 * j + s] = p
                wide.append(unfold(p, second))
            soft.append(jnp.concatenate(wide, axis=1))
        for (b, a, j), wide in zip(units, soft):
            o = nn(part(b, 2, a, j), wide)
            attended[b, 64 * j : 64 * j + 64, a * PAIR : (a + 1) * PAIR] = low(own_heads(o))

        middles = [x + nn(wprojt[...], attended[b]) for b, x in zip(bs, xv)]
        for b, middle in zip(bs, middles):
            centred2, inv2 = moments(middle)
            normed2 = centred2 * inv2
            s_norm2[b] = normed2
            s_inv2[b] = inv2
            s_n2[b] = low(normed2 * gain2)
        pres = [nn(w1t[...], s_n2[b]) for b in bs]
        for b, pre in zip(bs, pres):
            cdf, pdf = gelu_parts(pre)
            s_hidden[b] = low(pre * cdf)
            s_slope[b] = cdf + pre * pdf
        for b, (_, half), middle in zip(bs, at, middles):
            drop0, drop2 = drops(half)
            z = middle + nn(w2t[...], s_hidden[b])
            s_z[1, b] = low(z)
            if half == 1:
                s_z[0, b] = low(jnp.where(drop0, 0.0, z))
                s_z[2, b] = low(jnp.where(drop2, 0.0, z))

    forward(0, 1, 2)
    last_rows()
    last_block()
    forward(3, 4, 5, 6, 7)

    for c in g_arriving:
        c.wait_recv()
    for i in range(ROWS + 2):
        if i < ROWS - 3:
            extra = gstrip_ref[(i + 3) * 8 : (i + 4) * 8, :]
            put_g_last(i, g_ref[i + 3, COLS - 16 :, :].astype(F32), extra.astype(F32))
        else:
            k = i - ROWS + 3
            put_g(i, gr_ref[k].astype(F32))
            extra = gcorner_ref[k * 8 : (k + 1) * 8, :]
            put_g_last(i, gr_ref[k, COLS - 16 :, :].astype(F32), extra.astype(F32))

    def tap(b, dy, dx):
        return gs[dx, b, (2 - dy) * BLK : (2 - dy) * BLK + TOK, :]

    def halves(b):
        return (b, b + 3) if b < NBLK - 1 else (6, 7)

    def both(ref, b):
        return jnp.concatenate([ref[u] for u in halves(b)], axis=1)

    def edged(dy, b):
        return jnp.concatenate(
            [s_z[dy if place_of(u)[1] == 1 else 1, u] for u in halves(b)], axis=1
        )

    def over_blocks(term):
        total = term(0)
        for b in range(1, NBLK):
            total = total + term(b)
        return total

    def put_tile(place, tile):
        grads_ref[place * CP : (place + 1) * CP, :] = low(tile)

    def put_pair(place, left, right):
        put_tile(place, jnp.concatenate([left, right], axis=1))

    held_back = None
    for t in range(9):
        total = over_blocks(lambda b: nn(edged(t // 3, b), tap(b, t // 3, t % 3)))
        put_tile(t, total[:, :128])
        narrow = jnp.concatenate([total[:, 128:], jnp.zeros((CP, 256 - 12 - C), F32)], axis=1)
        narrow = narrow[:, :64]
        if t % 2 == 0:
            held_back = narrow
        else:
            put_pair(9 + t // 2, held_back, narrow)
    put_pair(13, held_back, jnp.zeros((CP, 64), F32))
    steps = ((first0, second0, third0), (first1, second1, third1), (first2, second2, third2))
    staged = ((core0, held0), (core1, held1))
    flying = [{}, {}, {}]

    def rows(start, size):
        return pl.ds(pl.multiple_of(start, 16), size)

    def share_rows(g, c, p, share):
        at = BASE[g] + c * HALVES[g] + p * PARTS[g] + share * SHARES[g]
        return rows(at, SHARES[g])

    def part_rows(g, c, p):
        return rows(BASE[g] + c * HALVES[g] + p * PARTS[g], PARTS[g])

    def go_core(g):
        flying[g]["core"] = [
            copy(
                grads_ref.at[part_rows(g, 1 - core, p)],
                staged[g][0].at[p],
                core_send.at[g, p],
                core_recv.at[g, p],
                sibling,
            )
            for p in range(3)
        ]

    def go_first(g):
        if g < 2:
            flying[g]["first"] = []
            for p in range(3):
                flying[g]["core"][p].wait_recv()
                total = grads_ref[part_rows(g, core, p), :].astype(F32)
                staged[g][1][p] = low(total + staged[g][0][p].astype(F32))
                group = []
                for k in range(1, SIDE):
                    share = lax.rem(here[p] + k, SIDE)
                    group.append(
                        copy(
                            staged[g][1].at[p, rows(share * SHARES[g], SHARES[g])],
                            steps[g][0].at[p, k - 1],
                            send.at[g, 0, p, k - 1],
                            recv.at[g, 0, p, k - 1],
                            along(p, k, 0),
                        )
                    )
                flying[g]["first"].append(group)
            return
        flying[g]["first"] = [
            [
                copy(
                    grads_ref.at[
                        share_rows(g, 1 - core if o else core, p, lax.rem(here[p] + k, SIDE))
                    ],
                    steps[g][0].at[p, i],
                    send.at[g, 0, p, i],
                    recv.at[g, 0, p, i],
                    along(p, k, o),
                )
                for i, (k, o) in enumerate(seven)
            ]
            for p in range(3)
        ]

    def spread_out(g, p, step, source, axis):
        target = steps[g][step]
        target[p, here[axis]] = source
        return [
            copy(
                target.at[p, here[axis]],
                target.at[p, here[axis]],
                send.at[g, step, p, k - 1],
                recv.at[g, step, p, k - 1],
                along(axis, k, 0),
            )
            for k in range(1, SIDE)
        ]

    def gathered(copies, target, p):
        for c in copies:
            c.wait_recv()
        total = target[p, 0].astype(F32)
        for k in range(1, SIDE):
            total = total + target[p, k].astype(F32)
        return low(total)

    def go_second(g):
        flying[g]["second"] = []
        for p in range(3):
            if g < 2:
                total = staged[g][1][p, rows(here[p] * SHARES[g], SHARES[g]), :].astype(F32)
            else:
                total = grads_ref[share_rows(g, core, p, here[p]), :].astype(F32)
            for i in range(len(flying[g]["first"][p])):
                flying[g]["first"][p][i].wait_recv()
                total = total + steps[g][0][p, i].astype(F32)
            flying[g]["second"].append(spread_out(g, p, 1, low(total), (p + 1) % 3))

    def go_third(g):
        flying[g]["third"] = []
        for p in range(3):
            total = gathered(flying[g]["second"][p], steps[g][1], p)
            flying[g]["third"].append(spread_out(g, p, 2, total, (p + 2) % 3))

    def go_back(g):
        flying[g]["back"] = []
        partners = [(k, 0) for k in range(1, SIDE)] if g < 2 else seven
        for p in range(3):
            at = share_rows(g, core, p, here[p])
            sum_ref[at, :] = gathered(flying[g]["third"][p], steps[g][2], p)
            flying[g]["back"].append(
                [
                    copy(
                        sum_ref.at[at],
                        sum_ref.at[at],
                        send.at[g, 3, p, i],
                        recv.at[g, 3, p, i],
                        along(p, k, o),
                    )
                    for i, (k, o) in enumerate(partners)
                ]
            )

    def go_end(g):
        flying[g]["end"] = []
        for p in range(3):
            for c in flying[g]["back"][p]:
                c.wait_recv()
            if g < 2:
                at = part_rows(g, core, p)
                flying[g]["end"].append(
                    copy(
                        sum_ref.at[at],
                        sum_ref.at[at],
                        core_send.at[g, 3 + p],
                        core_recv.at[g, 3 + p],
                        sibling,
                    )
                )

    go_core(0)

    line = iota((1, TOK), 1) >> 4

    def conv_back(b):
        total = None
        for dy in range(3):
            part = None
            for dx in range(3):
                product = nt(wconv_ref[3 * dy + dx], tap(b, dy, dx))
                part = product if part is None else part + product
            if dy != 1:
                part = jnp.where((line == (27, 28)[dy // 2]) & last_row, 0.0, part)
            total = part if total is None else total + part
        for i, u in enumerate(halves(b)):
            dshift[u, :C, :] = low(total[:, i * UT : (i + 1) * UT])

    def back_to_heads():
        bs = range(UNITS)
        d_pres = [low(nn(w2p[...], dshift[b]) * s_slope[b]) for b in bs]
        d_middles = []
        for b, d_pre in zip(bs, d_pres):
            s_dpre[b] = d_pre
            d_middle = dshift[b].astype(F32) + norm_back(
                nn(w1p[...], d_pre), s_norm2[b], s_inv2[b], gain2
            )
            s_dmid[b] = d_middle
            d_middles.append(low(d_middle))
        for b, d_attn in zip(bs, d_middles):
            s_dattn[b] = d_attn
            dheads[b] = low(nn(wprojp[...], d_attn))

    conv_back(0)
    conv_back(1)
    go_first(0)
    conv_back(2)
    conv_back(3)
    back_to_heads()

    fc2 = over_blocks(lambda b: nt(both(dshift, b), both(s_hidden, b)))
    fc1 = over_blocks(lambda b: nt(both(s_n2, b), both(s_dpre, b)))
    for place, total in ((14, fc2), (17, fc1)):
        put_tile(place, total[:, :128])
        put_tile(place + 1, total[:, 128:256])
        put_pair(place + 2, total[:, 256:], jnp.zeros((CP, 384 - FF), F32))
    proj = over_blocks(lambda b: nt(both(attended, b), both(s_dattn, b)))
    put_tile(20, proj[:, :128])
    put_pair(21, proj[:, 128:192], jnp.zeros((CP, 64), F32))
    go_core(1)
    go_second(0)

    def heads_back(step):
        units = [
            (u, a, j)
            for u in range(4 * step, 4 * step + 4)
            for a in range(PAIRS)
            for j in range(HEADS // 2)
        ]

        def part(ref, u, third, a, j):
            top = third * CP + 64 * j
            return ref[u, top : top + 64, a * PAIR : (a + 1) * PAIR]

        d_probs = [
            tn(part(packed, u, 2, a, j), two_heads(part(dheads, u, 0, a, j))) for u, a, j in units
        ]
        wide = []
        for (u, a, j), d_prob in zip(units, d_probs):
            p_wide, s_wide = [], []
            for s in range(2):
                p = probs[u, a, 2 * j + s]
                dp = fold(d_prob[:, s * PAIR : (s + 1) * PAIR], second)
                ds = p * (dp - jnp.sum(p * dp, axis=0, keepdims=True)) * factor
                p_wide.append(unfold(p, second))
                s_wide.append(unfold(ds, second))
            wide.append((p_wide, s_wide))
        for (u, a, j), (p_wide, s_wide) in zip(units, wide):
            lanes = slice(a * PAIR, (a + 1) * PAIR)
            dv = nt(part(dheads, u, 0, a, j), jnp.concatenate(p_wide, axis=0))
            dq = nn(part(packed, u, 1, a, j), jnp.concatenate(s_wide, axis=1))
            dk = nt(part(packed, u, 0, a, j), jnp.concatenate(s_wide, axis=0))
            dpacked[u, 64 * j : 64 * j + 64, lanes] = low(own_heads(dq))
            dpacked[u, CP + 64 * j : CP + 64 * j + 64, lanes] = low(own_heads(dk))
            dpacked[u, 2 * CP + 64 * j : 2 * CP + 64 * j + 64, lanes] = low(own_heads(dv))

    heads_back(0)
    go_first(1)
    heads_back(1)
    go_third(0)
    qkv = over_blocks(lambda b: nt(both(s_n1, b), both(dpacked, b)))
    for i in range(4):
        put_tile(22 + i, qkv[:, i * 128 : (i + 1) * 128])
    put_pair(26, qkv[:, 512:576], jnp.zeros((CP, 64), F32))
    put_tile(27, jnp.zeros((CP, 128), F32))
    go_first(2)

    ones_pair = eye(PAIR, PAIR)

    def inputs_back(*us):
        d_ins = [
            s_dmid[u] + norm_back(nn(wqkvp[...], dpacked[u]), s_norm1[u], s_inv1[u], gain1)
            for u in us
        ]
        for u, d_in in zip(us, d_ins):
            b, half = place_of(u)
            d_low = low(d_in)
            for a in range(PAIRS):
                natural = nt(ones_pair, d_low[:, a * PAIR : (a + 1) * PAIR])
                at = half * UT + a * PAIR
                d_ref[b, at : at + PAIR, :] = low(natural[:, :C])

    inputs_back(6, 7)
    edge = d_ref[NBLK - 1].astype(F32).reshape(ROWS // 2, 2, 2, 8, C)[:, :, 1]
    pairs = jnp.where(
        iota((ROWS // 2, 8, C), 1) < 4, pltpu.roll(edge[:, 0], 4, 1), edge[:, 1]
    )
    strip_out[...] = low(pairs.reshape(ROWS * 4, C))
    leaving = [
        copy(strip_out.at[112:128], hc_ref, out_send.at[2], out_recv.at[2], (down, right)),
        copy(strip_out, hs_ref, out_send.at[1], out_recv.at[1], (row, right)),
    ]
    go_second(1)
    inputs_back(0, 1, 2, 3, 4, 5)
    leaving.append(
        copy(d_ref.at[:, 448:512, :], hr_ref, out_send.at[0], out_recv.at[0], (down, col))
    )
    stores = [pltpu.make_async_copy(d_ref, d_hbm, store.at[0])]
    stores[0].start()

    def keep(g):
        for c in flying[g]["end"]:
            c.wait_recv()
        at = slice(BASE[g], BASE[g] + TILES[g] * CP)
        stores.append(pltpu.make_async_copy(sum_ref.at[at], sum_hbm.at[at], store.at[1 + g]))
        stores[-1].start()

    go_back(0)
    go_second(2)
    go_third(1)
    go_third(2)
    go_end(0)
    go_back(1)
    go_back(2)
    keep(0)
    go_end(1)
    go_end(2)
    keep(1)
    keep(2)
    for c in leaving:
        c.wait_recv()
    for c in started:
        c.wait_send()
    for c in stores:
        c.wait()


def call_layer(features, cotangent, w_qkv, w_proj, w_fc1, w_fc2_t, w_conv, g1, g2, table):
    reductions = [VMEM((3, n, 128), BF) for n in PARTS[:2] * 2]
    for slots in (2 * SIDE - 1, SIDE, SIDE):
        reductions += [VMEM((3, slots, n, 128), BF) for n in SHARES]
    inputs = (features, cotangent, w_qkv, w_proj, w_fc1, w_fc2_t, w_conv, g1, g2, table)
    scratch = [VMEM(v.shape, v.dtype) for v in inputs]
    scratch += [
        VMEM((NBLK, TOK, C), BF),
        VMEM((GROWS, 128), BF),
        VMEM((4, COLS, C), BF),
        VMEM((5, COLS, C), BF),
        VMEM((ROWS * 4, C), BF),
        VMEM((ROWS * 8, C), BF),
        VMEM((16, C), BF),
        VMEM((48, C), BF),
        VMEM((ROWS * 4, C), BF),
        VMEM((ROWS * 8, C), BF),
        VMEM((ROWS * 4, C), BF),
        VMEM((GROWS, 128), BF),
        *reductions,
        VMEM((NBLK, TOK, C), BF),
        VMEM((3, NBLK, (ROWS + 2) * BLK, C), BF),
        VMEM((3 * CP, CP), BF),
        VMEM((CP, 3 * CP), BF),
        VMEM((CP, CP), BF),
        VMEM((CP, CP), BF),
        VMEM((FF, CP), BF),
        VMEM((CP, FF), BF),
        VMEM((CP, FF), BF),
        VMEM((FF, CP), BF),
        VMEM((HEADS, WIN, 15 * BLK), F32),
        VMEM((HEADS, WIN * WIN, PAIR), F32),
        VMEM((UNITS, CP, UT), F32),
        VMEM((UNITS, 1, UT), F32),
        VMEM((UNITS, CP, UT), BF),
        VMEM((UNITS, 3 * CP, UT), BF),
        VMEM((UNITS, CP, UT), BF),
        VMEM((UNITS, PAIRS, HEADS, WIN * WIN, PAIR), F32),
        VMEM((UNITS, CP, UT), F32),
        VMEM((UNITS, 1, UT), F32),
        VMEM((UNITS, CP, UT), BF),
        VMEM((UNITS, FF, UT), F32),
        VMEM((UNITS, FF, UT), BF),
        VMEM((3, UNITS, CP, UT), BF),
        VMEM((UNITS, CP, UT), BF),
        VMEM((UNITS, FF, UT), BF),
        VMEM((UNITS, CP, UT), BF),
        VMEM((UNITS, CP, UT), BF),
        VMEM((UNITS, 3 * CP, UT), BF),
        VMEM((UNITS, CP, UT), F32),
        pltpu.SemaphoreType.DMA((10,)),
        pltpu.SemaphoreType.DMA((4,)),
        pltpu.SemaphoreType.DMA((6,)),
        pltpu.SemaphoreType.DMA((6,)),
        pltpu.SemaphoreType.DMA((3,)),
        pltpu.SemaphoreType.DMA((3,)),
        pltpu.SemaphoreType.DMA((2, 6)),
        pltpu.SemaphoreType.DMA((2, 6)),
        pltpu.SemaphoreType.DMA((3, 4, 3, 2 * SIDE - 1)),
        pltpu.SemaphoreType.DMA((3, 4, 3, 2 * SIDE - 1)),
    ]
    return pl.pallas_call(
        layer,
        out_shape=(
            jax.ShapeDtypeStruct((NBLK, TOK, C), BF),
            jax.ShapeDtypeStruct((GROWS, 128), BF),
            jax.ShapeDtypeStruct((NBLK, 64, C), BF),
            jax.ShapeDtypeStruct((ROWS * 4, C), BF),
            jax.ShapeDtypeStruct((16, C), BF),
        ),
        in_specs=[pl.BlockSpec(memory_space=pl.ANY)] * 10,
        out_specs=[pl.BlockSpec(memory_space=pl.ANY)] * 2 + [pl.BlockSpec(memory_space=VMEM)] * 3,
        scratch_shapes=scratch,
        compiler_params=pltpu.CompilerParams(
            collective_id=0, has_side_effects=True, vmem_limit_bytes=60 * 2**20
        ),
        name="layer",
    )(*inputs)


def results(
    d_hbm, hr_hbm, hs_hbm, hc_hbm, sum_hbm,
    out_hbm, qkv_hbm, proj_hbm, fc1_hbm, fc2_hbm, conv_hbm,
    d_ref, hr_ref, hs_ref, hc_ref, sum_ref,
    out_ref, qkv_ref, proj_ref, fc1_ref, fc2_ref, conv_ref, sel_ref, load, store,
):
    hbm = (hr_hbm, hs_hbm, hc_hbm, d_hbm, sum_hbm)
    own = (hr_ref, hs_ref, hc_ref, d_ref, sum_ref)
    loads = [pltpu.make_async_copy(s, t, load.at[i]) for i, (s, t) in enumerate(zip(hbm, own))]
    for c in (loads[4], *loads[:4]):
        c.start()
    stores = []

    def keep(source, target):
        stores.append(pltpu.make_async_copy(source, target, store.at[len(stores)]))
        stores[-1].start()

    sel_ref[...] = spread(3 * CP, 3 * C, 0)
    loads[4].wait()
    scale = 1.0 / math.sqrt(ROWS * COLS * lax.axis_size("row") * lax.axis_size("col"))

    def full(i):
        return sum_ref[i * CP : (i + 1) * CP, :]

    def rest(i):
        return full(9 + i // 2)[:, 64 * (i % 2) : 64 * (i % 2) + 64]

    def square(i, r):
        return jnp.concatenate([full(i), rest(r)], axis=1)

    for t in range(9):
        conv_ref[t] = square(t, t).astype(F32)[:C, :C] * scale
    keep(conv_ref, conv_hbm)
    for c in loads[:4]:
        c.wait()
    sub = iota((8, C), 0)
    extras = hs_ref[...].astype(F32).reshape(ROWS // 2, 8, C)
    corners = hc_ref[...].astype(F32).reshape(2, 8, C)
    for i in range(ROWS):
        if i < 4:
            pieces = [hr_ref[b, i * BLK : (i + 1) * BLK, :] for b in range(NBLK)]
            extra = corners[i // 2]
        else:
            pieces = [d_ref[b, (i - 4) * BLK : (i - 3) * BLK, :] for b in range(NBLK)]
            extra = extras[(i - 4) // 2]
        v = pltpu.roll(jnp.concatenate(pieces, axis=0).astype(F32), 4, 0)
        head = jnp.where(sub < 4, pltpu.roll(extra, 4, 0) if i % 2 else extra, v[:8])
        out_ref[i] = low(jnp.concatenate([head, v[8:]], axis=0))

    keep(out_ref, out_hbm)
    proj_ref[...] = nn(spread(CP, C, 1), jnp.concatenate([full(20), full(21)[:, :64]], axis=1))[:, :C] * scale
    keep(proj_ref, proj_hbm)
    fc2 = jnp.concatenate([full(14), full(15), full(16)], axis=1).astype(F32)
    fc2_ref[...] = fc2[:C, :FF] * scale
    keep(fc2_ref, fc2_hbm)
    fc1 = jnp.concatenate([full(17), full(18), full(19)], axis=1).astype(F32)
    fc1_ref[...] = fc1[:C, :FF] * scale
    keep(fc1_ref, fc1_hbm)
    qkv = jnp.concatenate([full(22), full(23), full(24), full(25), full(26)[:, :64]], axis=1)
    qkv_ref[...] = nn(qkv, sel_ref[...])[:C] * scale
    keep(qkv_ref, qkv_hbm)
    for c in stores:
        c.wait()


def call_results(d_shifted, halo, sums):
    operands = (d_shifted, *halo, sums)
    shapes = (
        jax.ShapeDtypeStruct((ROWS, COLS, C), BF),
        jax.ShapeDtypeStruct((C, 3 * C), F32),
        jax.ShapeDtypeStruct((C, C), F32),
        jax.ShapeDtypeStruct((C, FF), F32),
        jax.ShapeDtypeStruct((C, FF), F32),
        jax.ShapeDtypeStruct((9, C, C), F32),
    )
    return pl.pallas_call(
        results,
        out_shape=shapes,
        in_specs=[pl.BlockSpec(memory_space=pl.ANY)] * 5,
        out_specs=[pl.BlockSpec(memory_space=pl.ANY)] * 6,
        scratch_shapes=[
            *(VMEM(v.shape, v.dtype) for v in operands + shapes),
            VMEM((3 * CP, 3 * C), BF),
            pltpu.SemaphoreType.DMA((5,)),
            pltpu.SemaphoreType.DMA((6,)),
        ],
        compiler_params=pltpu.CompilerParams(vmem_limit_bytes=60 * 2**20),
        name="results",
    )(*operands)


def local(features, cotangent, w_qkv, w_proj, w_fc1, w_fc2, w_conv, gain_attn, gain_mlp, pos_table):
    d_shifted, sums, *halo = call_layer(
        features,
        cotangent,
        w_qkv,
        w_proj,
        w_fc1,
        w_fc2.T,
        w_conv,
        gain_attn.reshape(1, C),
        gain_mlp.reshape(1, C),
        pos_table.T,
    )
    d_features, qkv, proj, fc1, fc2, conv = call_results(d_shifted, halo, sums)
    return d_features, qkv, proj, fc1, fc2.T, conv


def solution(mesh):
    return jax.shard_map(
        local,
        mesh=mesh,
        in_specs=(P("row", "col", None), P("row", "col", None)) + (P(),) * 8,
        out_specs=(P("row", "col", None),) + (P(),) * 5,
        check_vma=False,
    )
```
